32 devices in a mesh: dp: 4 (over y, core), tp: 8 (over z, x).
Axes of the slice: x: 2, y: 2, z: 4, core: 2. Of those that a mesh axis runs over, the one named last changes fastest.
Arguments:
- tokens: bfloat16 [8192, 2048], P(('dp', 'tp')), may hold values from -6 to 6
- group_ids: int32 [8192], P(('dp', 'tp')), may hold values from 0 to 7
- mixture_counts: int32 [8], replicated, may hold values from 64 to 1024
- grad_out: bfloat16 [8192, 2048], P(('dp', 'tp')), may hold values from -6 to 6
- norm1_gain: bfloat16 [2048], replicated, may hold values from 0.5 to 1.5
- w_query: bfloat16 [2048, 2048], P(None, 'tp'), may hold values from -0.125 to 0.125
- w_key: bfloat16 [2048, 2048], P(None, 'tp'), may hold values from -0.125 to 0.125
- w_value: bfloat16 [2048, 2048], P(None, 'tp'), may hold values from -0.125 to 0.125
- w_gate_mix: bfloat16 [2048, 2048], P(None, 'tp'), may hold values from -0.125 to 0.125
- w_beta: bfloat16 [2048, 16], P(None, 'tp'), may hold values from -0.125 to 0.125
- conv_query: bfloat16 [4, 2048], P(None, 'tp'), may hold values from -3 to 3
- conv_key: bfloat16 [4, 2048], P(None, 'tp'), may hold values from -3 to 3
- conv_value: bfloat16 [4, 2048], P(None, 'tp'), may hold values from -3 to 3
- out_gain: bfloat16 [128], replicated, may hold values from 0.5 to 1.5
- w_out: bfloat16 [2048, 2048], P('tp'), may hold values from -0.125 to 0.125
- norm2_gain: bfloat16 [2048], replicated, may hold values from 0.5 to 1.5
- w_gate: bfloat16 [2048, 5632], P(None, 'tp'), may hold values from -0.125 to 0.125
- w_up: bfloat16 [2048, 5632], P(None, 'tp'), may hold values from -0.125 to 0.125
- w_down: bfloat16 [5632, 2048], P('tp'), may hold values from -0.078125 to 0.078125
Outputs:
- output: bfloat16 [8192, 2048], P(('dp', 'tp'))
- grad_tokens: bfloat16 [8192, 2048], P(('dp', 'tp'))
- grad_norm1_gain: float32 [2048], replicated
- grad_w_query: float32 [2048, 2048], P(None, 'tp')
- grad_w_key: float32 [2048, 2048], P(None, 'tp')
- grad_w_value: float32 [2048, 2048], P(None, 'tp')
- grad_w_gate_mix: float32 [2048, 2048], P(None, 'tp')
- grad_w_beta: float32 [2048, 16], P(None, 'tp')
- grad_conv_query: float32 [4, 2048], P(None, 'tp')
- grad_conv_key: float32 [4, 2048], P(None, 'tp')
- grad_conv_value: float32 [4, 2048], P(None, 'tp')
- grad_out_gain: float32 [128], replicated
- grad_w_out: float32 [2048, 2048], P('tp')
- grad_norm2_gain: float32 [2048], replicated
- grad_w_gate: float32 [2048, 5632], P(None, 'tp')
- grad_w_up: float32 [2048, 5632], P(None, 'tp')
- grad_w_down: float32 [5632, 2048], P('tp')
The draws below stay inside these ranges and needn't reach their ends.
All inputs are finite; a program needn't handle non-finite values.
Results may differ from the reference program's by a relative error of at most 0.02.
Values may be sent and summed in bfloat16 or wider, within the bound.
A program may use at most 384 MiB of HBM per device.

```python
import jax
import jax.numpy as jnp
from jax import lax

D = 2048
H = 16
HEAD_DIM = 128
FF = 5632
SPAN = 64
SEQ_LEN = 2048
GROUPS = 8
GROUP_TOK = 2048
TOKENS = 8192
N_DP = 4


def set_ends(drawn, own_key, least, high):
    longest = drawn.shape.index(max(drawn.shape))
    spots = []
    for shift in (0, 1):
        where = [jax.random.randint(jax.random.fold_in(own_key, axis), (), 0, length) for axis, length in enumerate(drawn.shape)]
        where[longest] = (where[longest] + shift) % drawn.shape[longest]
        spots.append(tuple(where))
    return drawn.at[spots[0]].set(least).at[spots[1]].set(high)


def level_of(rng, dims, shards, least, largest):
    factor_of = 1.0
    for dim, shards_of in shards:
        draws = jax.random.uniform(jax.random.fold_in(jax.random.fold_in(rng, 6), dim), (shards_of,), jnp.float32, least / len(shards), largest / len(shards))
        factor_of = factor_of * jnp.repeat(jnp.exp(draws), dims[dim] // shards_of).reshape((-1,) + (1,) * (len(dims) - 1 - dim))
    return factor_of


def scatter_about(key, dims, width, limit, shards=(), held_as=jnp.bfloat16):
    factor_of = level_of(key, dims, shards, -0.22, 0.18) if shards else 1.0
    drawn = jax.random.normal(key, dims, jnp.float32) * width * factor_of
    return jnp.minimum(jnp.maximum(drawn, -limit), limit).astype(held_as)


def setup_inputs(seed: int = 0) -> dict:
    seeds = jax.random.split(jax.random.key(seed), 20)
    return {
        "tokens": scatter_about(seeds[0], (TOKENS, D), 1.0, 6.0, ((0, 32),)),
        "group_ids": set_ends(jax.random.randint(seeds[1], (TOKENS,), 0, GROUPS), jax.random.fold_in(seeds[1], 1), 0, GROUPS - 1).astype(jnp.int32),
        "mixture_counts": set_ends(jax.random.randint(seeds[2], (GROUPS,), 64, 1025), jax.random.fold_in(seeds[2], 1), 64, 1024).astype(jnp.int32),
        "grad_out": scatter_about(seeds[3], (TOKENS, D), 1.0, 6.0, ((0, 32),)),
        "norm1_gain": jnp.clip(1.0 + 0.1 * jax.random.normal(seeds[4], (D,), jnp.float32), 0.5, 1.5).astype(jnp.bfloat16),
        "w_query": scatter_about(seeds[5], (D, D), D ** -0.5, 0.125, ((1, 8),)),
        "w_key": scatter_about(seeds[6], (D, D), D ** -0.5, 0.125, ((1, 8),)),
        "w_value": scatter_about(seeds[7], (D, D), D ** -0.5, 0.125, ((1, 8),)),
        "w_gate_mix": scatter_about(seeds[8], (D, D), D ** -0.5, 0.125, ((1, 8),)),
        "w_beta": scatter_about(seeds[9], (D, H), D ** -0.5, 0.125, ((1, 8),)),
        "conv_query": scatter_about(seeds[10], (4, D), 4 ** -0.5, 3.0, ((1, 8),)),
        "conv_key": scatter_about(seeds[11], (4, D), 4 ** -0.5, 3.0, ((1, 8),)),
        "conv_value": scatter_about(seeds[12], (4, D), 4 ** -0.5, 3.0, ((1, 8),)),
        "out_gain": jnp.clip(1.0 + 0.1 * jax.random.normal(seeds[13], (HEAD_DIM,), jnp.float32), 0.5, 1.5).astype(jnp.bfloat16),
        "w_out": scatter_about(seeds[14], (D, D), D ** -0.5, 0.125, ((0, 8),)),
        "norm2_gain": jnp.clip(1.0 + 0.1 * jax.random.normal(seeds[15], (D,), jnp.float32), 0.5, 1.5).astype(jnp.bfloat16),
        "w_gate": scatter_about(seeds[16], (D, FF), D ** -0.5, 0.125, ((1, 8),)),
        "w_up": scatter_about(seeds[17], (D, FF), D ** -0.5, 0.125, ((1, 8),)),
        "w_down": scatter_about(seeds[18], (FF, D), FF ** -0.5, 0.078125, ((0, 8),)),
    }


@jax.custom_vjp
def low(v):
    return lax.optimization_barrier(v.astype(jnp.bfloat16)).astype(jnp.float32)

@jax.custom_vjp
def low_back(v):
    return v

def low_keep(v):
    return (low(v), None)

def low_pass(kept, grad):
    return (grad,)

def back_keep(v):
    return (v, None)

def back_low(kept, grad):
    return (low(grad),)
low.defvjp(low_keep, low_pass)
low_back.defvjp(back_keep, back_low)
HIGH = lax.Precision.HIGHEST

def matmul(left, right):
    return jnp.dot(left, right, precision=HIGH)

def rms_scale(values, gain):
    return values * lax.rsqrt(lax.optimization_barrier(jnp.mean(values * values, -1, keepdims=True)) + 1e-05) * gain

def short_conv(projected, kernel):
    row_count, channels = projected.shape
    seq_count = row_count // SEQ_LEN
    shaped = projected.reshape(seq_count, SEQ_LEN, channels)
    padded = jnp.pad(shaped, ((0, 0), (3, 0), (0, 0)))
    summed = kernel[0] * padded[:, 0:SEQ_LEN]
    for offset in range(1, 4):
        summed = summed + kernel[offset] * padded[:, offset:offset + SEQ_LEN]
    return jax.nn.silu(summed).reshape(row_count, channels)

def unit_rows(values):
    return values * lax.rsqrt(lax.optimization_barrier(jnp.sum(values * values, -1, keepdims=True)) + 1e-06)

def block_step(memory, block):
    query_rows, key_rows, value_rows, beta_rows = block
    key_beta = key_rows * beta_rows[..., None]
    value_beta = value_rows * beta_rows[..., None]
    row_ids = lax.broadcasted_iota(jnp.int32, (SPAN, SPAN), 0)
    col_ids = lax.broadcasted_iota(jnp.int32, (SPAN, SPAN), 1)
    inner_prod = jnp.einsum('bid,bjd->bij', key_beta, key_rows, precision=HIGH)
    system = jnp.eye(SPAN, dtype=jnp.float32) + jnp.where(row_ids > col_ids, inner_prod, 0.0)
    solved = jax.scipy.linalg.solve_triangular(system, jnp.concatenate([key_beta, value_beta], -1), lower=True, unit_diagonal=True)
    head_width = key_rows.shape[-1]
    w_factors = solved[..., :head_width]
    u_factors = solved[..., head_width:]
    fresh_values = u_factors - jnp.einsum('bid,bde->bie', w_factors, memory, precision=HIGH)
    scores = jnp.einsum('bid,bjd->bij', query_rows, key_rows, precision=HIGH)
    scores = jnp.where(row_ids >= col_ids, scores, 0.0)
    result = jnp.einsum('bid,bde->bie', query_rows, memory, precision=HIGH) + jnp.einsum('bij,bje->bie', scores, fresh_values, precision=HIGH)
    memory = memory + jnp.einsum('bid,bie->bde', key_rows, fresh_values, precision=HIGH)
    return (memory, result)

def delta_rule(queries, keys_all, values_all, betas):
    batch, length, head_width = queries.shape
    blocks = length // SPAN

    def to_blocks(values):
        return values.reshape(batch, blocks, SPAN, head_width).transpose(1, 0, 2, 3)
    beta_blocks = betas.reshape(batch, blocks, SPAN).transpose(1, 0, 2)
    start_memory = jnp.zeros((batch, head_width, head_width), jnp.float32)
    final_memory, results = lax.scan(jax.checkpoint(block_step), start_memory, (to_blocks(queries), to_blocks(keys_all), to_blocks(values_all), beta_blocks))
    return results.transpose(1, 0, 2, 3).reshape(batch, length, head_width)

def core_mixer(query_raw, key_raw, value_raw, gate_raw, beta_raw, conv_query, conv_key, conv_value, out_gain):
    row_count, channels = query_raw.shape
    heads = channels // HEAD_DIM
    seq_count = row_count // SEQ_LEN

    def split_heads(values):
        shaped = values.reshape(seq_count, SEQ_LEN, heads, HEAD_DIM).transpose(0, 2, 1, 3)
        return shaped.reshape(seq_count * heads, SEQ_LEN, HEAD_DIM)
    queries = unit_rows(split_heads(short_conv(query_raw, conv_query))) * HEAD_DIM ** (-0.5)
    keys_all = unit_rows(split_heads(short_conv(key_raw, conv_key)))
    values_all = split_heads(short_conv(value_raw, conv_value))
    betas = jax.nn.sigmoid(beta_raw).reshape(seq_count, SEQ_LEN, heads).transpose(0, 2, 1).reshape(seq_count * heads, SEQ_LEN)
    delta = delta_rule(queries, keys_all, values_all, betas)
    delta = delta.reshape(seq_count, heads, SEQ_LEN, HEAD_DIM).transpose(0, 2, 1, 3).reshape(row_count, heads, HEAD_DIM)
    normed = delta * lax.rsqrt(lax.optimization_barrier(jnp.mean(delta * delta, -1, keepdims=True)) + 1e-05) * out_gain
    gated = normed * jax.nn.silu(gate_raw.reshape(row_count, heads, HEAD_DIM))
    return gated.reshape(row_count, channels)

def block_forward(tokens, norm1_gain, w_query, w_key, w_value, w_gate_mix, w_beta, conv_query, conv_key, conv_value, out_gain, w_out, norm2_gain, w_gate, w_up, w_down):
    normed = low(rms_scale(tokens, norm1_gain))
    query_raw = low_back(matmul(normed, w_query))
    key_raw = low_back(matmul(normed, w_key))
    value_raw = low_back(matmul(normed, w_value))
    gate_raw = low_back(matmul(normed, w_gate_mix))
    beta_raw = low_back(matmul(normed, w_beta))
    mixed = low(core_mixer(query_raw, key_raw, value_raw, gate_raw, beta_raw, conv_query, conv_key, conv_value, out_gain))
    attn = low_back(matmul(mixed, w_out))
    resid = tokens + attn
    normed_mlp = low(rms_scale(resid, norm2_gain))
    gate = low_back(matmul(normed_mlp, w_gate))
    up_vals = low_back(matmul(normed_mlp, w_up))
    hidden = low(jax.nn.silu(gate) * up_vals)
    return resid + low_back(matmul(hidden, w_down))

def reference(tokens, group_ids, mixture_counts, grad_out, norm1_gain, w_query, w_key, w_value, w_gate_mix, w_beta, conv_query, conv_key, conv_value, out_gain, w_out, norm2_gain, w_gate, w_up, w_down):
    counts = mixture_counts.astype(jnp.float32)
    group_scale = jnp.sqrt(jnp.mean(counts) / counts)
    group_cols = lax.broadcasted_iota(jnp.int32, (1, GROUPS), 1)
    token_scale = lax.optimization_barrier(jnp.sum(jnp.where(group_ids[:, None] == group_cols, group_scale[None, :], 0.0), 1))
    cotangent = grad_out.astype(jnp.float32) * token_scale[:, None]
    params = (norm1_gain, w_query, w_key, w_value, w_gate_mix, w_beta, conv_query, conv_key, conv_value, out_gain, w_out, norm2_gain, w_gate, w_up, w_down)
    params = tuple((p.astype(jnp.float32) for p in params))
    inputs = tokens.astype(jnp.float32).reshape(N_DP, GROUP_TOK, D)
    cotangent = cotangent.reshape(N_DP, GROUP_TOK, D)

    def per_group(totals, pair):
        group_in, group_ct = pair
        result, backward = jax.vjp(block_forward, group_in, *params)
        grads = backward(group_ct)
        totals = tuple((a + b for a, b in zip(totals, grads[1:])))
        return (totals, (result, grads[0]))
    start = tuple((jnp.zeros_like(p) for p in params))
    totals, (results, input_grads) = lax.scan(per_group, start, (inputs, cotangent))
    output = results.reshape(TOKENS, D).astype(jnp.bfloat16)
    grad_tokens = input_grads.reshape(TOKENS, D).astype(jnp.bfloat16)
    return (output, grad_tokens, totals[0], totals[1], totals[2], totals[3], totals[4], totals[5], totals[6], totals[7], totals[8], totals[9], totals[10], totals[11], totals[12], totals[13], totals[14])
```

```python
import jax
import jax.numpy as jnp
from jax import lax
from jax.experimental import pallas as pl
from jax.experimental.pallas import tpu as pltpu
from jax.sharding import PartitionSpec as P

GROUPS = 8
HEAD_DIM = 128
SPAN = 64
SEQ_LEN = 2048
TILE = 256
F32 = jnp.float32
BF16 = jnp.bfloat16
NN = ((1,), (0,))
NT = ((1,), (1,))
TN = ((0,), (0,))


def split(values):
    high = values.astype(BF16)
    return high, (values - high.astype(F32)).astype(BF16)


def dot(left, right, dims):
    return lax.dot_general(left, right, (dims, ((), ())), preferred_element_type=F32)


def product(left, right, dims):
    return (
        dot(left[0], right[0], dims)
        + (dot(left[0], right[1], dims) + dot(left[1], right[0], dims))
    )


def quick(left, right, dims):
    return dot(left[0], right[0], dims)


def rows_of(pair, start, size):
    return pair[0][start : start + size], pair[1][start : start + size]


def sigmoid(values):
    return 1.0 / (1.0 + jnp.exp(-values))


def tile_masks():
    row = lax.broadcasted_iota(jnp.int32, (TILE, TILE), 0)
    col = lax.broadcasted_iota(jnp.int32, (TILE, TILE), 1)
    return row, col


def invert(lower, row, col):
    def level(size):
        return (row // (2 * size) == col // (2 * size)) & (row // size > col // size)

    inverse = jnp.where(row == col, 1.0, 0.0) - jnp.where(level(1), lower, 0.0)
    size = 2
    while size < SPAN:
        part = split(jnp.where(level(size), lower, 0.0))
        held = split(inverse)
        inverse = inverse - product(held, split(product(part, held, NN)), NN)
        size *= 2
    return inverse


def conv_rows(buffer, taps):
    total = taps[0:1] * buffer[pl.ds(5, TILE), :]
    for offset in range(1, 4):
        total = total + taps[offset : offset + 1] * buffer[pl.ds(5 + offset, TILE), :]
    return total


def mixer_forward_body(
    heads, proj_ref, conv_ref, gain_ref, mixed_ref, wu_ref, fresh_ref, out_ref, state_ref,
    inverse_ref, rows_buf, state,
):
    tile = pl.program_id(1)
    wide = heads * HEAD_DIM

    @pl.when(tile == 0)
    def _():
        rows_buf[0:8, :] = jnp.zeros((8, 3 * wide), F32)
        state[...] = jnp.zeros_like(state)

    @pl.when(tile > 0)
    def _():
        rows_buf[0:8, :] = rows_buf[TILE : TILE + 8, :]

    rows_buf[8 : 8 + TILE, :] = proj_ref[:, : 3 * wide]
    summed = conv_rows(rows_buf, conv_ref[...])
    active = summed * sigmoid(summed)
    row, col = tile_masks()
    same = row // SPAN == col // SPAN
    for head in range(heads):
        lo = head * HEAD_DIM
        query = active[:, lo : lo + HEAD_DIM]
        key = active[:, wide + lo : wide + lo + HEAD_DIM]
        value = active[:, 2 * wide + lo : 2 * wide + lo + HEAD_DIM]
        gate = proj_ref[:, 3 * wide + lo : 3 * wide + lo + HEAD_DIM]
        beta = sigmoid(proj_ref[:, 4 * wide + head : 4 * wide + head + 1])
        query = query * (
            lax.rsqrt(jnp.sum(query * query, -1, keepdims=True) + 1e-06) * HEAD_DIM ** (-0.5)
        )
        key = key * lax.rsqrt(jnp.sum(key * key, -1, keepdims=True) + 1e-06)
        key_beta = key * beta
        key_s = split(key)
        query_s = split(query)
        key_beta_s = split(key_beta)
        lower = jnp.where(same & (row > col), product(key_beta_s, key_s, NT), 0.0)
        inverse = invert(lower, row, col)
        inverse_ref[head] = inverse
        both = product(split(inverse), split(jnp.concatenate([key_beta, value * beta], 1)), NN)
        wu_ref[:, 2 * lo : 2 * lo + 2 * HEAD_DIM] = both
        scores = jnp.where(same & (row >= col), product(query_s, key_s, NT), 0.0)
        weights_s = split(both[:, :HEAD_DIM])
        fresh_all = []
        carried_all = []
        memory = state[head]
        for block in range(TILE // SPAN):
            start = block * SPAN
            state_ref[block, head] = memory
            stacked = tuple(
                jnp.concatenate([a[start : start + SPAN], b[start : start + SPAN]], 0)
                for a, b in zip(weights_s, query_s)
            )
            read = product(stacked, split(memory), NN)
            fresh = both[start : start + SPAN, HEAD_DIM:] - read[:SPAN]
            fresh_all.append(fresh)
            carried_all.append(read[SPAN:])
            memory = memory + product(rows_of(key_s, start, SPAN), split(fresh), TN)
        state[head] = memory
        fresh = jnp.concatenate(fresh_all, 0)
        fresh_ref[:, lo : lo + HEAD_DIM] = fresh
        out = jnp.concatenate(carried_all, 0) + product(split(scores), split(fresh), NN)
        out_ref[:, lo : lo + HEAD_DIM] = out
        scale = lax.rsqrt(jnp.mean(out * out, -1, keepdims=True) + 1e-05)
        mixed = out * scale * gain_ref[...] * (gate * sigmoid(gate))
        mixed_ref[:, lo : lo + HEAD_DIM] = mixed.astype(BF16)


def mixer_forward(proj, conv, gain, heads):
    rows = proj.shape[0]
    wide = heads * HEAD_DIM
    tiles = SEQ_LEN // TILE
    seqs = rows // SEQ_LEN
    blocks = TILE // SPAN

    def at(seq, tile):
        return (seq * tiles + tile, 0)

    return pl.pallas_call(
        lambda *refs: mixer_forward_body(heads, *refs),
        grid=(seqs, tiles),
        in_specs=[
            pl.BlockSpec((TILE, proj.shape[1]), at),
            pl.BlockSpec(conv.shape, lambda seq, tile: (0, 0)),
            pl.BlockSpec(gain.shape, lambda seq, tile: (0, 0)),
        ],
        out_specs=[
            pl.BlockSpec((TILE, wide), at),
            pl.BlockSpec((TILE, 2 * wide), at),
            pl.BlockSpec((TILE, wide), at),
            pl.BlockSpec((TILE, wide), at),
            pl.BlockSpec((blocks, heads, HEAD_DIM, HEAD_DIM), lambda s, t: (s * tiles + t, 0, 0, 0)),
            pl.BlockSpec((None, heads, TILE, TILE), lambda s, t: (s * tiles + t, 0, 0, 0)),
        ],
        out_shape=[
            jax.ShapeDtypeStruct((rows, wide), BF16),
            jax.ShapeDtypeStruct((rows, 2 * wide), F32),
            jax.ShapeDtypeStruct((rows, wide), F32),
            jax.ShapeDtypeStruct((rows, wide), F32),
            jax.ShapeDtypeStruct((rows // SPAN, heads, HEAD_DIM, HEAD_DIM), F32),
            jax.ShapeDtypeStruct((rows // TILE, heads, TILE, TILE), F32),
        ],
        scratch_shapes=[
            pltpu.VMEM((TILE + 8, 3 * wide), F32),
            pltpu.VMEM((heads, HEAD_DIM, HEAD_DIM), F32),
        ],
        compiler_params=pltpu.CompilerParams(vmem_limit_bytes=48 * 2**20),
        name="mixer_forward",
    )(proj, conv, gain)


def unit_back(raw, scale, grad):
    along = jnp.sum(raw * grad, -1, keepdims=True)
    return scale * grad - raw * (scale * scale * scale * along)


def mixer_backward_body(
    heads, proj_ref, before_ref, conv_ref, gain_ref, grad_ref, wu_ref, fresh_ref, out_ref,
    state_ref, inverse_ref, raw_grad_ref, conv_grad_ref, gain_grad_ref,
    rows_buf, grad_buf, state_grad,
):
    step = pl.program_id(1)
    steps = pl.num_programs(1)
    wide = heads * HEAD_DIM

    @pl.when((step == 0) & (pl.program_id(0) == 0))
    def _():
        conv_grad_ref[...] = jnp.zeros_like(conv_grad_ref)
        gain_grad_ref[...] = jnp.zeros_like(gain_grad_ref)

    @pl.when(step == 0)
    def _():
        grad_buf[TILE : TILE + 8, :] = jnp.zeros((8, 3 * wide), F32)
        state_grad[...] = jnp.zeros_like(state_grad)

    @pl.when(step > 0)
    def _():
        grad_buf[TILE : TILE + 8, :] = grad_buf[0:8, :]

    first = step == steps - 1
    rows_buf[0:8, :] = jnp.where(first, 0.0, before_ref[:, : 3 * wide])
    rows_buf[8 : 8 + TILE, :] = proj_ref[:, : 3 * wide]
    summed = conv_rows(rows_buf, conv_ref[...])
    smooth = sigmoid(summed)
    active = summed * smooth
    slope = smooth * (1.0 + summed * (1.0 - smooth))
    row, col = tile_masks()
    same = row // SPAN == col // SPAN
    lane = lax.broadcasted_iota(jnp.int32, (TILE, HEAD_DIM), 1)
    beta_grads = jnp.zeros((TILE, HEAD_DIM), F32)
    gain_total = jnp.zeros((1, HEAD_DIM), F32)
    for head in range(heads):
        lo = head * HEAD_DIM
        query_raw = active[:, lo : lo + HEAD_DIM]
        key_raw = active[:, wide + lo : wide + lo + HEAD_DIM]
        value = active[:, 2 * wide + lo : 2 * wide + lo + HEAD_DIM]
        gate = proj_ref[:, 3 * wide + lo : 3 * wide + lo + HEAD_DIM]
        beta = sigmoid(proj_ref[:, 4 * wide + head : 4 * wide + head + 1])
        query_scale = lax.rsqrt(jnp.sum(query_raw * query_raw, -1, keepdims=True) + 1e-06)
        key_scale = lax.rsqrt(jnp.sum(key_raw * key_raw, -1, keepdims=True) + 1e-06)
        query = query_raw * (query_scale * HEAD_DIM ** (-0.5))
        key = key_raw * key_scale
        key_beta = key * beta
        grad = grad_ref[:, lo : lo + HEAD_DIM]
        out = out_ref[:, lo : lo + HEAD_DIM]
        scale = lax.rsqrt(jnp.mean(out * out, -1, keepdims=True) + 1e-05)
        gate_s = sigmoid(gate)
        normed = out * scale
        gain_total = gain_total + jnp.sum(grad * normed * (gate * gate_s), 0, keepdims=True)
        gate_grad = grad * normed * gain_ref[...] * (gate_s * (1.0 + gate * (1.0 - gate_s)))
        normed_grad = grad * gain_ref[...] * (gate * gate_s)
        out_grad = scale * normed_grad - out * (
            scale * scale * scale * jnp.mean(out * normed_grad, -1, keepdims=True)
        )
        key_s = split(key)
        query_s = split(query)
        out_grad_s = split(out_grad)
        fresh = fresh_ref[:, lo : lo + HEAD_DIM]
        fresh_s = split(fresh)
        both = wu_ref[:, 2 * lo : 2 * lo + 2 * HEAD_DIM]
        both_s = split(both)
        weights_s = both_s[0][:, :HEAD_DIM], both_s[1][:, :HEAD_DIM]
        within = same & (row >= col)
        scores_s = split(jnp.where(within, product(query_s, key_s, NT), 0.0))
        scores_grad_s = split(jnp.where(within, product(out_grad_s, fresh_s, NT), 0.0))
        fresh_grad_in = product(scores_s, out_grad_s, TN)
        query_grad = product(scores_grad_s, key_s, NN)
        key_grad = product(scores_grad_s, query_s, TN)
        carry = state_grad[head]
        blocks = TILE // SPAN
        parts = [None] * blocks
        for block in range(blocks - 1, -1, -1):
            start = block * SPAN
            memory_s = split(state_ref[block, head])
            carry_s = split(carry)
            fresh_grad = fresh_grad_in[start : start + SPAN] + product(
                rows_of(key_s, start, SPAN), carry_s, NN
            )
            fresh_grad_s = split(fresh_grad)
            out_rows = rows_of(out_grad_s, start, SPAN)
            stacked = tuple(
                jnp.concatenate([a, b], 0) for a, b in zip(out_rows, fresh_grad_s)
            )
            back = product(stacked, memory_s, NT)
            through = product(rows_of(fresh_s, start, SPAN), carry_s, NT)
            parts[block] = (fresh_grad, back[:SPAN], -back[SPAN:], through)
            carry = carry + (
                product(rows_of(query_s, start, SPAN), out_rows, TN)
                - product(rows_of(weights_s, start, SPAN), fresh_grad_s, TN)
            )
        state_grad[head] = carry
        fresh_grad, query_more, weights_grad, key_more = (
            jnp.concatenate([part[i] for part in parts], 0) for i in range(4)
        )
        query_grad = query_grad + query_more
        key_grad = key_grad + key_more
        both_grad = jnp.concatenate([weights_grad, fresh_grad], 1)
        right_grad = product(split(inverse_ref[head]), split(both_grad), TN)
        lower_grad = jnp.where(
            same & (row > col), -product(split(right_grad), both_s, NT), 0.0
        )
        lower_grad_s = split(lower_grad)
        key_beta_grad = right_grad[:, :HEAD_DIM] + product(lower_grad_s, key_s, NN)
        value_beta_grad = right_grad[:, HEAD_DIM:]
        key_grad = key_grad + product(lower_grad_s, split(key_beta), TN) + key_beta_grad * beta
        beta_grad = jnp.sum(key_beta_grad * key + value_beta_grad * value, -1, keepdims=True)
        beta_grad = beta_grad * (beta * (1.0 - beta))
        beta_grads = jnp.where(lane == head, beta_grad, beta_grads)
        query_back = unit_back(query_raw, query_scale, query_grad * HEAD_DIM ** (-0.5))
        key_back = unit_back(key_raw, key_scale, key_grad)
        grad_buf[0:TILE, lo : lo + HEAD_DIM] = query_back * slope[:, lo : lo + HEAD_DIM]
        grad_buf[0:TILE, wide + lo : wide + lo + HEAD_DIM] = (
            key_back * slope[:, wide + lo : wide + lo + HEAD_DIM]
        )
        grad_buf[0:TILE, 2 * wide + lo : 2 * wide + lo + HEAD_DIM] = (
            value_beta_grad * beta * slope[:, 2 * wide + lo : 2 * wide + lo + HEAD_DIM]
        )
        raw_grad_ref[:, 3 * wide + lo : 3 * wide + lo + HEAD_DIM] = gate_grad.astype(BF16)
    raw_grad_ref[:, 4 * wide :] = beta_grads.astype(BF16)
    gain_grad_ref[0:1, :] += gain_total
    taps = conv_ref[...]
    here = grad_buf[0:TILE, :]
    total = taps[3:4] * here
    conv_grad_ref[3:4, :] += jnp.sum(here * rows_buf[8 : 8 + TILE, :], 0, keepdims=True)
    for offset in range(3):
        total = total + taps[offset : offset + 1] * grad_buf[pl.ds(3 - offset, TILE), :]
        conv_grad_ref[offset : offset + 1, :] += jnp.sum(
            here * rows_buf[pl.ds(5 + offset, TILE), :], 0, keepdims=True
        )
    raw_grad_ref[:, : 3 * wide] = total.astype(BF16)


def mixer_backward(proj, conv, gain, grad, wu, fresh, out, states, inverses, heads):
    rows = proj.shape[0]
    wide = heads * HEAD_DIM
    tiles = SEQ_LEN // TILE
    seqs = rows // SEQ_LEN
    blocks = TILE // SPAN

    def index(seq, step):
        return seq * tiles + tiles - 1 - step

    def at(seq, step):
        return (index(seq, step), 0)

    def ahead(seq, step):
        return (jnp.maximum(index(seq, step) * (TILE // 8) - 1, 0), 0)

    def fixed(seq, step):
        return (0, 0)

    return pl.pallas_call(
        lambda *refs: mixer_backward_body(heads, *refs),
        grid=(seqs, tiles),
        in_specs=[
            pl.BlockSpec((TILE, proj.shape[1]), at),
            pl.BlockSpec((8, proj.shape[1]), ahead),
            pl.BlockSpec(conv.shape, fixed),
            pl.BlockSpec(gain.shape, fixed),
            pl.BlockSpec((TILE, wide), at),
            pl.BlockSpec((TILE, 2 * wide), at),
            pl.BlockSpec((TILE, wide), at),
            pl.BlockSpec((TILE, wide), at),
            pl.BlockSpec(
                (blocks, heads, HEAD_DIM, HEAD_DIM), lambda s, t: (index(s, t), 0, 0, 0)
            ),
            pl.BlockSpec((None, heads, TILE, TILE), lambda s, t: (index(s, t), 0, 0, 0)),
        ],
        out_specs=[
            pl.BlockSpec((TILE, 4 * wide + 128), at),
            pl.BlockSpec((8, 3 * wide), fixed),
            pl.BlockSpec((8, HEAD_DIM), fixed),
        ],
        out_shape=[
            jax.ShapeDtypeStruct((rows, 4 * wide + 128), BF16),
            jax.ShapeDtypeStruct((8, 3 * wide), F32),
            jax.ShapeDtypeStruct((8, HEAD_DIM), F32),
        ],
        scratch_shapes=[
            pltpu.VMEM((TILE + 8, 3 * wide), F32),
            pltpu.VMEM((TILE + 8, 3 * wide), F32),
            pltpu.VMEM((heads, HEAD_DIM, HEAD_DIM), F32),
        ],
        compiler_params=pltpu.CompilerParams(vmem_limit_bytes=48 * 2**20),
        name="mixer_backward",
    )(proj, proj, conv, gain, grad, wu, fresh, out, states, inverses)


def rms_scale(values, gain):
    return values * lax.rsqrt(jnp.mean(values * values, -1, keepdims=True) + 1e-05) * gain


def swiglu(gate, up_vals):
    return jax.nn.silu(gate) * up_vals


def left_product(left, right):
    return lax.dot_general(left, right, (((0,), (0,)), ((), ())), preferred_element_type=F32)


def right_product(left, right):
    return lax.dot_general(left, right, (((1,), (1,)), ((), ())), preferred_element_type=F32)


def make_fold(kept_rows, weight, piece):
    weight_grad = left_product(kept_rows, piece)
    rows_grad = right_product(piece, weight)
    return (weight_grad, rows_grad)


def make_rows(source, weight, transposed):
    if transposed:
        return right_product(source, weight)
    return jnp.dot(source, weight, preferred_element_type=F32)


def shards(
    tokens,
    group_ids,
    mixture_counts,
    grad_out,
    norm1_gain,
    w_query,
    w_key,
    w_value,
    w_gate_mix,
    w_beta,
    conv_query,
    conv_key,
    conv_value,
    out_gain,
    w_out,
    norm2_gain,
    w_gate,
    w_up,
    w_down,
):
    inputs = tokens.astype(F32)
    normed, norm1_back = jax.vjp(rms_scale, inputs, norm1_gain.astype(F32))
    gathered = lax.all_gather(normed.astype(BF16), "tp", axis=0, tiled=True)
    heads = w_beta.shape[1]
    w_beta = jnp.pad(w_beta, ((0, 0), (0, 128 - heads)))
    mix_weights = jnp.concatenate([w_query, w_key, w_value, w_gate_mix, w_beta], 1)
    projected = jnp.dot(gathered, mix_weights, preferred_element_type=F32)
    head_cols = w_query.shape[1]
    conv = jnp.concatenate([conv_query, conv_key, conv_value], 1).astype(F32)
    gain = out_gain.astype(F32)[None]
    mixed, *kept = mixer_forward(projected, conv, gain, heads)
    attn = lax.psum_scatter(
        make_rows(mixed, w_out, False).astype(jnp.bfloat16), "tp", scatter_dimension=0, tiled=True
    ).astype(jnp.float32)
    resid = inputs + attn
    normed_mlp, norm2_back = jax.vjp(rms_scale, resid, norm2_gain.astype(F32))
    gathered_mlp = lax.all_gather(normed_mlp.astype(BF16), "tp", axis=0, tiled=True)
    pair_weights = jnp.concatenate([w_gate, w_up], 1)
    ff_cols = w_gate.shape[1]
    paired = jnp.dot(gathered_mlp, pair_weights, preferred_element_type=F32)
    hidden_full, swiglu_back = jax.vjp(swiglu, paired[:, :ff_cols], paired[:, ff_cols:])
    hidden = hidden_full.astype(BF16)
    mlp_out = lax.psum_scatter(
        make_rows(hidden, w_down, False).astype(jnp.bfloat16), "tp", scatter_dimension=0, tiled=True
    ).astype(jnp.float32)
    output = (resid + mlp_out).astype(BF16)
    group_cols = lax.broadcasted_iota(jnp.int32, (1, GROUPS), 1)
    counts = mixture_counts.astype(F32)
    group_scale = jnp.sqrt(jnp.mean(counts) / counts)
    token_scale = jnp.sum(jnp.where(group_ids[:, None] == group_cols, group_scale[None, :], 0.0), 1)
    grad_rows = grad_out.astype(F32) * token_scale[:, None]
    grad_mlp = grad_rows.astype(BF16)
    grad_w_down, hidden_grad = make_fold(
        hidden, w_down, lax.all_gather(grad_mlp, "tp", axis=0, tiled=True)
    )
    gate_grad, up_grad = swiglu_back(hidden_grad)
    pair_grad = jnp.concatenate([gate_grad, up_grad], 1).astype(BF16)
    pair_weight_grad = left_product(gathered_mlp, pair_grad)
    normed_mlp_grad = lax.psum_scatter(
        make_rows(pair_grad, pair_weights, True).astype(jnp.bfloat16),
        "tp",
        scatter_dimension=0,
        tiled=True,
    ).astype(jnp.float32)
    resid_norm_grad, norm2_grad = norm2_back(normed_mlp_grad)
    resid_grad = grad_rows + resid_norm_grad
    attn_grad = resid_grad.astype(BF16)
    grad_w_out, mixed_grad = make_fold(
        mixed, w_out, lax.all_gather(attn_grad, "tp", axis=0, tiled=True)
    )
    raw_grad, conv_grad, gain_grad = mixer_backward(
        projected, conv, gain, mixed_grad, *kept, heads
    )
    mix_weight_grad = left_product(gathered, raw_grad)
    normed_grad = lax.psum_scatter(
        make_rows(raw_grad, mix_weights, True).astype(jnp.bfloat16),
        "tp",
        scatter_dimension=0,
        tiled=True,
    ).astype(jnp.float32)
    input_norm_grad, norm1_grad = norm1_back(normed_grad)
    grad_tokens = (resid_grad + input_norm_grad).astype(BF16)
    summed = (
        lax.psum(mix_weight_grad.astype(jnp.bfloat16), "dp").astype(jnp.float32),
        lax.psum(grad_w_out.astype(jnp.bfloat16), "dp").astype(jnp.float32),
        lax.psum(pair_weight_grad.astype(jnp.bfloat16), "dp").astype(jnp.float32),
        lax.psum(grad_w_down.astype(jnp.bfloat16), "dp").astype(jnp.float32),
    )
    conv_total = lax.psum(conv_grad[:4], "dp")
    gains = lax.psum((norm1_grad, gain_grad[0], norm2_grad), ("dp", "tp"))
    mix_total = summed[0]
    pair_total = summed[2]
    return (
        output,
        grad_tokens,
        gains[0],
        mix_total[:, 0:head_cols],
        mix_total[:, head_cols : 2 * head_cols],
        mix_total[:, 2 * head_cols : 3 * head_cols],
        mix_total[:, 3 * head_cols : 4 * head_cols],
        mix_total[:, 4 * head_cols : 4 * head_cols + heads],
        conv_total[:, 0:head_cols],
        conv_total[:, head_cols : 2 * head_cols],
        conv_total[:, 2 * head_cols :],
        gains[1],
        summed[1],
        gains[2],
        pair_total[:, :ff_cols],
        pair_total[:, ff_cols:],
        summed[3],
    )


def solution(mesh):
    return jax.shard_map(
        shards,
        mesh=mesh,
        in_specs=(
            P(("dp", "tp"), None),
            P(("dp", "tp")),
            P(),
            P(("dp", "tp"), None),
            P(),
            P(None, "tp"),
            P(None, "tp"),
            P(None, "tp"),
            P(None, "tp"),
            P(None, "tp"),
            P(None, "tp"),
            P(None, "tp"),
            P(None, "tp"),
            P(),
            P("tp", None),
            P(),
            P(None, "tp"),
            P(None, "tp"),
            P("tp", None),
        ),
        out_specs=(
            P(("dp", "tp"), None),
            P(("dp", "tp"), None),
            P(),
            P(None, "tp"),
            P(None, "tp"),
            P(None, "tp"),
            P(None, "tp"),
            P(None, "tp"),
            P(None, "tp"),
            P(None, "tp"),
            P(None, "tp"),
            P(),
            P("tp", None),
            P(),
            P(None, "tp"),
            P(None, "tp"),
            P("tp", None),
        ),
        check_vma=False,
    )
```

```python
import functools

import jax
import jax.numpy as jnp
from jax import lax
from jax.experimental import pallas as pl
from jax.experimental.pallas import tpu as pltpu
from jax.sharding import Mesh
from jax.sharding import PartitionSpec as P

GROUPS = 8
HEAD_DIM = 128
SPAN = 64
SEQ_LEN = 2048
TILE = 256
F32 = jnp.float32
BF16 = jnp.bfloat16
NN = ((1,), (0,))
NT = ((1,), (1,))
TN = ((0,), (0,))


def split(values):
    high = values.astype(BF16)
    return high, (values - high.astype(F32)).astype(BF16)


def dot(left, right, dims):
    return lax.dot_general(left, right, (dims, ((), ())), preferred_element_type=F32)


def product(left, right, dims):
    return (
        dot(left[0], right[0], dims)
        + (dot(left[0], right[1], dims) + dot(left[1], right[0], dims))
    )


def quick(left, right, dims):
    return dot(left[0], right[0], dims)


def rows_of(pair, start, size):
    return pair[0][start : start + size], pair[1][start : start + size]


def sigmoid(values):
    return 1.0 / (1.0 + jnp.exp(-values))


def tile_masks():
    row = lax.broadcasted_iota(jnp.int32, (TILE, TILE), 0)
    col = lax.broadcasted_iota(jnp.int32, (TILE, TILE), 1)
    return row, col


def invert(lower, row, col):
    def level(size):
        return (row // (2 * size) == col // (2 * size)) & (row // size > col // size)

    inverse = jnp.where(row == col, 1.0, 0.0) - jnp.where(level(1), lower, 0.0)
    size = 2
    while size < SPAN:
        part = split(jnp.where(level(size), lower, 0.0))
        held = split(inverse)
        inverse = inverse - product(held, split(product(part, held, NN)), NN)
        size *= 2
    return inverse


def conv_rows(buffer, taps):
    total = taps[0:1] * buffer[pl.ds(5, TILE), :]
    for offset in range(1, 4):
        total = total + taps[offset : offset + 1] * buffer[pl.ds(5 + offset, TILE), :]
    return total


def run_errands(errands, plan, step, late):
    if not errands:
        return
    if not late:
        pl.when(step == 0)(lambda: greet(True))
    for at in sorted({entry[0] for entry in plan}):

        @pl.when(step == at)
        def _(at=at):
            for when, index, phase in plan:
                if when == at and (phase == "finish") == late:
                    getattr(errands[index], phase)()


def errand_operands(errands):
    kinds, sources = [e[0] for e in errands], [e[1] for e in errands]
    specs = [pl.BlockSpec(memory_space=pl.ANY)] * len(errands)
    shapes = [errand_target(*errand) for errand in errands]
    return kinds, sources, specs, shapes, errand_scratch(kinds, sources) if errands else []


def mixer_params(errands, collective_id):
    extra = {"collective_id": collective_id, "has_side_effects": True} if errands else {}
    return pltpu.CompilerParams(vmem_limit_bytes=48 * 2**20, **extra)


def mixer_forward_body(heads, kinds, plan, *refs):
    first_ref, refs, errands = take_errands(kinds, refs, 3, 6) if kinds else (refs[0], refs[1:], ())
    proj_ref = first_ref
    conv_ref, gain_ref, mixed_ref, wu_ref, fresh_ref, out_ref, state_ref, inverse_ref, *refs = refs
    rows_buf, state = refs
    tile = pl.program_id(1)
    run_errands(errands, plan, tile, False)
    wide = heads * HEAD_DIM

    @pl.when(tile == 0)
    def _():
        rows_buf[0:8, :] = jnp.zeros((8, 3 * wide), F32)
        state[...] = jnp.zeros_like(state)

    @pl.when(tile > 0)
    def _():
        rows_buf[0:8, :] = rows_buf[TILE : TILE + 8, :]

    rows_buf[8 : 8 + TILE, :] = proj_ref[:, : 3 * wide]
    summed = conv_rows(rows_buf, conv_ref[...])
    active = summed * sigmoid(summed)
    row, col = tile_masks()
    same = row // SPAN == col // SPAN
    for head in range(heads):
        lo = head * HEAD_DIM
        query = active[:, lo : lo + HEAD_DIM]
        key = active[:, wide + lo : wide + lo + HEAD_DIM]
        value = active[:, 2 * wide + lo : 2 * wide + lo + HEAD_DIM]
        gate = proj_ref[:, 3 * wide + lo : 3 * wide + lo + HEAD_DIM]
        beta = sigmoid(proj_ref[:, 4 * wide + head : 4 * wide + head + 1])
        query = query * (
            lax.rsqrt(jnp.sum(query * query, -1, keepdims=True) + 1e-06) * HEAD_DIM ** (-0.5)
        )
        key = key * lax.rsqrt(jnp.sum(key * key, -1, keepdims=True) + 1e-06)
        key_beta = key * beta
        key_s = split(key)
        query_s = split(query)
        key_beta_s = split(key_beta)
        lower = jnp.where(same & (row > col), product(key_beta_s, key_s, NT), 0.0)
        inverse = invert(lower, row, col)
        inverse_ref[head] = inverse
        both = product(split(inverse), split(jnp.concatenate([key_beta, value * beta], 1)), NN)
        wu_ref[:, 2 * lo : 2 * lo + 2 * HEAD_DIM] = both
        scores = jnp.where(same & (row >= col), product(query_s, key_s, NT), 0.0)
        weights_s = split(both[:, :HEAD_DIM])
        fresh_all = []
        carried_all = []
        memory = state[head]
        for block in range(TILE // SPAN):
            start = block * SPAN
            state_ref[block, head] = memory
            stacked = tuple(
                jnp.concatenate([a[start : start + SPAN], b[start : start + SPAN]], 0)
                for a, b in zip(weights_s, query_s)
            )
            read = product(stacked, split(memory), NN)
            fresh = both[start : start + SPAN, HEAD_DIM:] - read[:SPAN]
            fresh_all.append(fresh)
            carried_all.append(read[SPAN:])
            memory = memory + product(rows_of(key_s, start, SPAN), split(fresh), TN)
        state[head] = memory
        fresh = jnp.concatenate(fresh_all, 0)
        fresh_ref[:, lo : lo + HEAD_DIM] = fresh
        out = jnp.concatenate(carried_all, 0) + product(split(scores), split(fresh), NN)
        out_ref[:, lo : lo + HEAD_DIM] = out
        scale = lax.rsqrt(jnp.mean(out * out, -1, keepdims=True) + 1e-05)
        mixed = out * scale * gain_ref[...] * (gate * sigmoid(gate))
        mixed_ref[:, lo : lo + HEAD_DIM] = mixed.astype(BF16)
    run_errands(errands, plan, tile, True)


def mixer_forward(proj, conv, gain, heads, errands=(), plan=(), collective_id=None):
    rows = proj.shape[0]
    wide = heads * HEAD_DIM
    tiles = SEQ_LEN // TILE
    seqs = rows // SEQ_LEN
    blocks = TILE // SPAN

    def at(seq, tile):
        return (seq * tiles + tile, 0)

    kinds, sources, specs, shapes, scratch = errand_operands(errands)
    return pl.pallas_call(
        functools.partial(mixer_forward_body, heads, kinds, plan),
        grid=(seqs, tiles),
        in_specs=[
            pl.BlockSpec((TILE, proj.shape[1]), at),
            pl.BlockSpec(conv.shape, lambda seq, tile: (0, 0)),
            pl.BlockSpec(gain.shape, lambda seq, tile: (0, 0)),
            *specs,
        ],
        out_specs=[
            pl.BlockSpec((TILE, wide), at),
            pl.BlockSpec((TILE, 2 * wide), at),
            pl.BlockSpec((TILE, wide), at),
            pl.BlockSpec((TILE, wide), at),
            pl.BlockSpec((blocks, heads, HEAD_DIM, HEAD_DIM), lambda s, t: (s * tiles + t, 0, 0, 0)),
            pl.BlockSpec((None, heads, TILE, TILE), lambda s, t: (s * tiles + t, 0, 0, 0)),
            *specs,
        ],
        out_shape=[
            jax.ShapeDtypeStruct((rows, wide), BF16),
            jax.ShapeDtypeStruct((rows, 2 * wide), F32),
            jax.ShapeDtypeStruct((rows, wide), F32),
            jax.ShapeDtypeStruct((rows, wide), F32),
            jax.ShapeDtypeStruct((rows // SPAN, heads, HEAD_DIM, HEAD_DIM), F32),
            jax.ShapeDtypeStruct((rows // TILE, heads, TILE, TILE), F32),
            *shapes,
        ],
        scratch_shapes=[
            pltpu.VMEM((TILE + 8, 3 * wide), F32),
            pltpu.VMEM((heads, HEAD_DIM, HEAD_DIM), F32),
            *scratch,
        ],
        compiler_params=mixer_params(errands, collective_id),
        name="mixer_forward",
    )(proj, conv, gain, *sources)


def unit_back(raw, scale, grad):
    along = jnp.sum(raw * grad, -1, keepdims=True)
    return scale * grad - raw * (scale * scale * scale * along)


def mixer_backward_body(heads, kinds, plan, *refs):
    first_ref, refs, errands = take_errands(kinds, refs, 10, 3) if kinds else (refs[0], refs[1:], ())
    proj_ref = first_ref
    before_ref, conv_ref, gain_ref, grad_ref, wu_ref, fresh_ref, out_ref, *refs = refs
    state_ref, inverse_ref, raw_grad_ref, conv_grad_ref, gain_grad_ref, *refs = refs
    rows_buf, grad_buf, state_grad = refs
    step = pl.program_id(1)
    run_errands(errands, plan, step, False)
    steps = pl.num_programs(1)
    wide = heads * HEAD_DIM

    @pl.when((step == 0) & (pl.program_id(0) == 0))
    def _():
        conv_grad_ref[...] = jnp.zeros_like(conv_grad_ref)
        gain_grad_ref[...] = jnp.zeros_like(gain_grad_ref)

    @pl.when(step == 0)
    def _():
        grad_buf[TILE : TILE + 8, :] = jnp.zeros((8, 3 * wide), F32)
        state_grad[...] = jnp.zeros_like(state_grad)

    @pl.when(step > 0)
    def _():
        grad_buf[TILE : TILE + 8, :] = grad_buf[0:8, :]

    first = step == steps - 1
    rows_buf[0:8, :] = jnp.where(first, 0.0, before_ref[:, : 3 * wide])
    rows_buf[8 : 8 + TILE, :] = proj_ref[:, : 3 * wide]
    summed = conv_rows(rows_buf, conv_ref[...])
    smooth = sigmoid(summed)
    active = summed * smooth
    slope = smooth * (1.0 + summed * (1.0 - smooth))
    row, col = tile_masks()
    same = row // SPAN == col // SPAN
    lane = lax.broadcasted_iota(jnp.int32, (TILE, HEAD_DIM), 1)
    beta_grads = jnp.zeros((TILE, HEAD_DIM), F32)
    gain_total = jnp.zeros((1, HEAD_DIM), F32)
    for head in range(heads):
        lo = head * HEAD_DIM
        query_raw = active[:, lo : lo + HEAD_DIM]
        key_raw = active[:, wide + lo : wide + lo + HEAD_DIM]
        value = active[:, 2 * wide + lo : 2 * wide + lo + HEAD_DIM]
        gate = proj_ref[:, 3 * wide + lo : 3 * wide + lo + HEAD_DIM]
        beta = sigmoid(proj_ref[:, 4 * wide + head : 4 * wide + head + 1])
        query_scale = lax.rsqrt(jnp.sum(query_raw * query_raw, -1, keepdims=True) + 1e-06)
        key_scale = lax.rsqrt(jnp.sum(key_raw * key_raw, -1, keepdims=True) + 1e-06)
        query = query_raw * (query_scale * HEAD_DIM ** (-0.5))
        key = key_raw * key_scale
        key_beta = key * beta
        grad = grad_ref[:, lo : lo + HEAD_DIM]
        out = out_ref[:, lo : lo + HEAD_DIM]
        scale = lax.rsqrt(jnp.mean(out * out, -1, keepdims=True) + 1e-05)
        gate_s = sigmoid(gate)
        normed = out * scale
        gain_total = gain_total + jnp.sum(grad * normed * (gate * gate_s), 0, keepdims=True)
        gate_grad = grad * normed * gain_ref[...] * (gate_s * (1.0 + gate * (1.0 - gate_s)))
        normed_grad = grad * gain_ref[...] * (gate * gate_s)
        out_grad = scale * normed_grad - out * (
            scale * scale * scale * jnp.mean(out * normed_grad, -1, keepdims=True)
        )
        key_s = split(key)
        query_s = split(query)
        out_grad_s = split(out_grad)
        fresh = fresh_ref[:, lo : lo + HEAD_DIM]
        fresh_s = split(fresh)
        both = wu_ref[:, 2 * lo : 2 * lo + 2 * HEAD_DIM]
        both_s = split(both)
        weights_s = both_s[0][:, :HEAD_DIM], both_s[1][:, :HEAD_DIM]
        within = same & (row >= col)
        scores_s = split(jnp.where(within, product(query_s, key_s, NT), 0.0))
        scores_grad_s = split(jnp.where(within, product(out_grad_s, fresh_s, NT), 0.0))
        fresh_grad_in = product(scores_s, out_grad_s, TN)
        query_grad = product(scores_grad_s, key_s, NN)
        key_grad = product(scores_grad_s, query_s, TN)
        carry = state_grad[head]
        blocks = TILE // SPAN
        parts = [None] * blocks
        for block in range(blocks - 1, -1, -1):
            start = block * SPAN
            memory_s = split(state_ref[block, head])
            carry_s = split(carry)
            fresh_grad = fresh_grad_in[start : start + SPAN] + product(
                rows_of(key_s, start, SPAN), carry_s, NN
            )
            fresh_grad_s = split(fresh_grad)
            out_rows = rows_of(out_grad_s, start, SPAN)
            stacked = tuple(
                jnp.concatenate([a, b], 0) for a, b in zip(out_rows, fresh_grad_s)
            )
            back = product(stacked, memory_s, NT)
            through = product(rows_of(fresh_s, start, SPAN), carry_s, NT)
            parts[block] = (fresh_grad, back[:SPAN], -back[SPAN:], through)
            carry = carry + (
                product(rows_of(query_s, start, SPAN), out_rows, TN)
                - product(rows_of(weights_s, start, SPAN), fresh_grad_s, TN)
            )
        state_grad[head] = carry
        fresh_grad, query_more, weights_grad, key_more = (
            jnp.concatenate([part[i] for part in parts], 0) for i in range(4)
        )
        query_grad = query_grad + query_more
        key_grad = key_grad + key_more
        both_grad = jnp.concatenate([weights_grad, fresh_grad], 1)
        right_grad = product(split(inverse_ref[head]), split(both_grad), TN)
        lower_grad = jnp.where(
            same & (row > col), -product(split(right_grad), both_s, NT), 0.0
        )
        lower_grad_s = split(lower_grad)
        key_beta_grad = right_grad[:, :HEAD_DIM] + product(lower_grad_s, key_s, NN)
        value_beta_grad = right_grad[:, HEAD_DIM:]
        key_grad = key_grad + product(lower_grad_s, split(key_beta), TN) + key_beta_grad * beta
        beta_grad = jnp.sum(key_beta_grad * key + value_beta_grad * value, -1, keepdims=True)
        beta_grad = beta_grad * (beta * (1.0 - beta))
        beta_grads = jnp.where(lane == head, beta_grad, beta_grads)
        query_back = unit_back(query_raw, query_scale, query_grad * HEAD_DIM ** (-0.5))
        key_back = unit_back(key_raw, key_scale, key_grad)
        grad_buf[0:TILE, lo : lo + HEAD_DIM] = query_back * slope[:, lo : lo + HEAD_DIM]
        grad_buf[0:TILE, wide + lo : wide + lo + HEAD_DIM] = (
            key_back * slope[:, wide + lo : wide + lo + HEAD_DIM]
        )
        grad_buf[0:TILE, 2 * wide + lo : 2 * wide + lo + HEAD_DIM] = (
            value_beta_grad * beta * slope[:, 2 * wide + lo : 2 * wide + lo + HEAD_DIM]
        )
        raw_grad_ref[:, 3 * wide + lo : 3 * wide + lo + HEAD_DIM] = gate_grad.astype(BF16)
    raw_grad_ref[:, 4 * wide :] = beta_grads.astype(BF16)
    gain_grad_ref[0:1, :] += gain_total
    taps = conv_ref[...]
    here = grad_buf[0:TILE, :]
    total = taps[3:4] * here
    conv_grad_ref[3:4, :] += jnp.sum(here * rows_buf[8 : 8 + TILE, :], 0, keepdims=True)
    for offset in range(3):
        total = total + taps[offset : offset + 1] * grad_buf[pl.ds(3 - offset, TILE), :]
        conv_grad_ref[offset : offset + 1, :] += jnp.sum(
            here * rows_buf[pl.ds(5 + offset, TILE), :], 0, keepdims=True
        )
    raw_grad_ref[:, : 3 * wide] = total.astype(BF16)
    run_errands(errands, plan, step, True)


def mixer_backward(
    proj, conv, gain, grad, wu, fresh, out, states, inverses, heads,
    errands=(), plan=(), collective_id=None,
):
    rows = proj.shape[0]
    wide = heads * HEAD_DIM
    tiles = SEQ_LEN // TILE
    seqs = rows // SEQ_LEN
    blocks = TILE // SPAN

    def index(seq, step):
        return seq * tiles + tiles - 1 - step

    def at(seq, step):
        return (index(seq, step), 0)

    def ahead(seq, step):
        return (jnp.maximum(index(seq, step) * (TILE // 8) - 1, 0), 0)

    def fixed(seq, step):
        return (0, 0)

    kinds, sources, specs, shapes, scratch = errand_operands(errands)
    return pl.pallas_call(
        functools.partial(mixer_backward_body, heads, kinds, plan),
        grid=(seqs, tiles),
        in_specs=[
            pl.BlockSpec((TILE, proj.shape[1]), at),
            pl.BlockSpec((8, proj.shape[1]), ahead),
            pl.BlockSpec(conv.shape, fixed),
            pl.BlockSpec(gain.shape, fixed),
            pl.BlockSpec((TILE, wide), at),
            pl.BlockSpec((TILE, 2 * wide), at),
            pl.BlockSpec((TILE, wide), at),
            pl.BlockSpec((TILE, wide), at),
            pl.BlockSpec(
                (blocks, heads, HEAD_DIM, HEAD_DIM), lambda s, t: (index(s, t), 0, 0, 0)
            ),
            pl.BlockSpec((None, heads, TILE, TILE), lambda s, t: (index(s, t), 0, 0, 0)),
            *specs,
        ],
        out_specs=[
            pl.BlockSpec((TILE, 4 * wide + 128), at),
            pl.BlockSpec((8, 3 * wide), fixed),
            pl.BlockSpec((8, HEAD_DIM), fixed),
            *specs,
        ],
        out_shape=[
            jax.ShapeDtypeStruct((rows, 4 * wide + 128), BF16),
            jax.ShapeDtypeStruct((8, 3 * wide), F32),
            jax.ShapeDtypeStruct((8, HEAD_DIM), F32),
            *shapes,
        ],
        scratch_shapes=[
            pltpu.VMEM((TILE + 8, 3 * wide), F32),
            pltpu.VMEM((TILE + 8, 3 * wide), F32),
            pltpu.VMEM((heads, HEAD_DIM, HEAD_DIM), F32),
            *scratch,
        ],
        compiler_params=mixer_params(errands, collective_id),
        name="mixer_backward",
    )(proj, proj, conv, gain, grad, wu, fresh, out, states, inverses, *sources)


MESH = pl.DeviceIdType.MESH


def place():
    return lax.axis_index("core"), lax.axis_index("zl"), lax.axis_index("x")


def slot_of(core, deep, wide):
    own_core, own_deep, own_wide = place()
    return (
        jnp.where(core, 1 - own_core, own_core) * 4
        + jnp.where(deep, 1 - own_deep, own_deep) * 2
        + jnp.where(wide, 1 - own_wide, own_wide)
    )


def is_moved():
    return lax.axis_index("core") != lax.axis_index("zh")


def greet(everyone=False):
    barrier = pltpu.get_barrier_semaphore()
    axes = ("core", "zl", "x", "y", "zh") if everyone else ("core", "zl", "x")
    for axis in axes:
        pl.semaphore_signal(barrier, inc=1, device_id=neighbour(axis), device_id_type=MESH)
    peers = len(axes)
    if everyone:
        pl.when(is_moved())(
            lambda: pl.semaphore_signal(
                barrier, inc=1, device_id=partner(), device_id_type=MESH
            )
        )
        peers = peers + is_moved().astype(jnp.int32)
    pl.semaphore_wait(barrier, peers)


def partner():
    return {"core": lax.axis_index("zh"), "zh": lax.axis_index("core")}


def row_half(ref, index):
    rows = ref.shape[0] // 2
    return ref.at[pl.ds(pl.multiple_of(index * rows, 16), rows)]


class Errand:
    sems = 1
    staged = True

    def __init__(self, source, target, send, recv, local, stage=None):
        self.source, self.target, self.stage = source, target, stage
        self.send, self.recv, self.local = send, recv, local
        self.y = lax.axis_index("y")

    def remote(self, index, source, target, device):
        return pltpu.make_async_remote_copy(
            src_ref=source, dst_ref=target, send_sem=self.send.at[index],
            recv_sem=self.recv.at[index], device_id=device, device_id_type=MESH,
        )

    def stays(self, action):
        pl.when(jnp.logical_not(is_moved()))(action)

    def own_target(self):
        return self.target

    def here(self):
        source = self.source if self.stage is None else self.stage
        return pltpu.make_async_copy(source, self.own_target(), self.local)

    def stage_in(self):
        return pltpu.make_async_copy(self.source, self.stage, self.local)

    def start_here(self):
        self.stays(lambda: (self.here() if self.stage is None else self.stage_in()).start())

    def pass_here(self):
        def action():
            self.stage_in().wait()
            self.here().start()

        if self.stage is not None:
            self.stays(action)

    def finish_here(self):
        self.stays(lambda: self.here().wait())


class Exchange(Errand):
    def far(self):
        return self.remote(0, self.source, self.target, partner())

    def start(self):
        pl.when(is_moved())(lambda: self.far().start())
        self.start_here()

    def middle(self):
        self.pass_here()

    def finish(self):
        pl.when(is_moved())(lambda: self.far().wait())
        self.finish_here()


class Swap(Errand):
    sems = 2

    def first(self):
        mine = row_half(self.target, self.y)
        return self.remote(0, row_half(self.source, self.y), mine, partner())

    def second(self, landing=False):
        half = row_half(self.target, 1 - self.y if landing else self.y)
        return self.remote(1, half, half, neighbour("y"))

    def start(self):
        pl.when(is_moved())(lambda: self.first().start())
        self.start_here()

    def middle(self):
        @pl.when(is_moved())
        def _():
            self.first().wait_recv()
            self.second().start()

        self.pass_here()

    def finish(self):
        @pl.when(is_moved())
        def _():
            self.first().wait_send()
            self.second().wait_send()
            self.second(True).wait_recv()

        self.finish_here()


class HalfOverY(Errand):
    staged = False

    def copy(self):
        return self.remote(0, row_half(self.source, 1 - self.y), self.target, neighbour("y"))

    def start(self):
        self.copy().start()

    def middle(self):
        pass

    def finish(self):
        self.copy().wait()


class Across(Errand):
    staged = False

    def copy(self):
        return self.remote(0, self.source, self.target, neighbour("zh"))

    def start(self):
        pl.when(is_moved())(lambda: self.copy().start())

    def middle(self):
        pass

    def finish(self):
        pl.when(is_moved())(lambda: self.copy().wait_send())
        self.stays(lambda: self.copy().wait_recv())


class ExchangeGather(Errand):
    sems = 12

    def moves(self):
        own = slot_of(0, 0, 0)
        wide, deep, far = slot_of(0, 0, 1), slot_of(0, 1, 0), slot_of(0, 1, 1)
        rows = self.source.shape[0]
        half = rows // 2
        return {
            0: ("x", own, wide, 0, half), 1: ("zl", own, deep, half, half),
            2: ("x", own, wide, half, half), 3: ("zl", own, deep, 0, half),
            4: ("core", own, slot_of(1, 0, 0), 0, rows),
            5: ("zl", wide, far, 0, half), 6: ("x", deep, far, half, half),
            7: ("core", wide, slot_of(1, 0, 1), 0, rows),
            8: ("core", deep, slot_of(1, 1, 0), 0, rows),
            9: ("core", far, slot_of(1, 1, 1), 0, half),
            10: ("core", far, slot_of(1, 1, 1), half, half),
        }

    def move(self, index, landing=False):
        axis, source, target, start, size = self.moves()[index]
        view = self.target.at[target if landing else source, pl.ds(start, size)]
        return self.remote(index, view, view, neighbour(axis))

    def launch(self, *indices):
        for index in indices:
            self.move(index).start()

    def arrived(self, *indices):
        for index in indices:
            self.move(index, True).wait_recv()

    def own_target(self):
        return self.target.at[slot_of(0, 0, 0)]

    def far(self, landing=False):
        there = slot_of(0, 0, 0)
        if not landing:
            there = there + (lax.axis_index("zh") - lax.axis_index("core")) * 4
        return self.remote(11, self.source, self.target.at[there], partner())

    def start(self):
        pl.when(is_moved())(lambda: self.far().start())
        self.start_here()

    def settle(self):
        self.pass_here()

    def spread(self):
        pl.when(is_moved())(lambda: self.far(True).wait_recv())
        self.finish_here()
        self.launch(0, 1, 2, 3, 4)

    def middle(self):
        self.arrived(0)
        self.launch(5)
        self.arrived(1)
        self.launch(6)
        self.arrived(2)
        self.launch(7)
        self.arrived(3)
        self.launch(8)

    def late(self):
        self.arrived(5)
        self.launch(9)
        self.arrived(6)
        self.launch(10)

    def finish(self):
        self.arrived(4, 7, 8, 9, 10)
        pl.when(is_moved())(lambda: self.far().wait_send())
        for index in range(11):
            self.move(index).wait_send()


class Spread(Errand):
    sems = 3

    def own_target(self):
        return row_half(self.target, self.y)

    def over(self):
        return self.remote(0, self.source, self.own_target(), neighbour("y"))

    def other(self, index, axis):
        view = row_half(self.target, 1 - self.y)
        return self.remote(index, view, view, neighbour(axis))

    def cross(self):
        return self.remote(1, self.source, self.own_target(), neighbour("core"))

    def start(self):
        @pl.when(jnp.logical_not(is_moved()))
        def _():
            self.over().start()
            self.cross().start()

        self.start_here()

    def middle(self):
        @pl.when(jnp.logical_not(is_moved()))
        def _():
            self.other(0, "y").wait_recv()
            self.other(2, "core").start()

        self.pass_here()

    def finish(self):
        @pl.when(jnp.logical_not(is_moved()))
        def _():
            self.over().wait_send()
            self.cross().wait_send()
            self.other(2, "core").wait_send()

        @pl.when(is_moved())
        def _():
            self.cross().wait_recv()
            self.other(2, "core").wait_recv()

        self.finish_here()


def errand_target(kind, source):
    if kind is ExchangeGather:
        return jax.ShapeDtypeStruct((8, *source.shape), source.dtype)
    rows = source.shape[0]
    rows = {HalfOverY: rows // 2, Spread: 2 * rows}.get(kind, rows)
    return jax.ShapeDtypeStruct((rows, *source.shape[1:]), source.dtype)


def errand_scratch(kinds, sources=()):
    total = max(1, sum(kind.sems for kind in kinds))
    stages = [
        pltpu.VMEM(source.shape if kind.staged else (16, 128), BF16)
        for kind, source in zip(kinds, sources)
    ]
    return [
        *stages,
        pltpu.SemaphoreType.DMA((total,)),
        pltpu.SemaphoreType.DMA((total,)),
        pltpu.SemaphoreType.DMA((max(1, len(kinds)),)),
    ]


def make_errands(kinds, sources, targets, send, recv, local, stages=None):
    made, at = [], 0
    for index, (kind, source, target) in enumerate(zip(kinds, sources, targets)):
        view = pl.ds(at, kind.sems)
        stage = stages[index] if stages and kind.staged else None
        made.append(kind(source, target, send.at[view], recv.at[view], local.at[index], stage))
        at += kind.sems
    return made


def neighbour(axis):
    return {axis: 1 - lax.axis_index(axis)}


def column_tile(columns):
    for size in (512, 384, 256, 128):
        if columns % size == 0:
            return size
    return columns


def column_parts(columns):
    tile = column_tile(columns)
    if tile != columns or columns <= 512:
        return [(0, tile, columns // tile)]
    whole = columns // 256 * 256
    return [(0, 256, whole // 256), (whole, columns - whole, 1)]


def by_columns(columns, body):
    for start, size, steps in column_parts(columns):
        if steps == 1:
            body(pl.ds(start, size))
        else:

            def column(step, _, start=start, size=size):
                body(pl.ds(pl.multiple_of(start + step * size, 128), size))
                return 0

            lax.fori_loop(0, steps, column, 0)


def take_errands(kinds, refs, inputs, outputs):
    extra = len(kinds)
    sources = refs[inputs : inputs + extra]
    targets = refs[inputs + extra + outputs : inputs + 2 * extra + outputs]
    errands = make_errands(kinds, sources, targets, *refs[-3:], refs[-3 - extra : -3])
    rest = (
        *refs[:inputs], *refs[inputs + extra : inputs + extra + outputs],
        *refs[inputs + 2 * extra + outputs : -3 - extra],
    )
    return rest[0], rest[1:], errands


def gather_body(dims, count, kinds, block_ref, *refs):
    block_ref, refs, errands = take_errands(kinds, (block_ref, *refs), 1 + count, 1 + count)
    weight_refs, gathered_ref, product_refs = refs[:count], refs[count], refs[count + 1 : 2 * count + 1]
    held = refs[2 * count + 1]
    weights, results = refs[2 * count + 2 : 3 * count + 2], refs[3 * count + 2 : 4 * count + 2]
    send, recv, local = refs[4 * count + 2 :]
    rows = block_ref.shape[0]
    half = rows // 2
    own = slot_of(0, 0, 0)
    load_own = pltpu.make_async_copy(block_ref, held.at[own], local.at[0])
    load_own.start()
    loads = [
        pltpu.make_async_copy(ref, weight, local.at[1 + i])
        for i, (ref, weight) in enumerate(zip(weight_refs, weights))
    ]
    for load in loads:
        load.start()
    greet(bool(kinds))
    load_own.wait()

    def move(index, axis, slot, start, size):
        view = held.at[slot, pl.ds(start, size)]
        return pltpu.make_async_remote_copy(
            src_ref=view, dst_ref=view, send_sem=send.at[index], recv_sem=recv.at[index],
            device_id=neighbour(axis), device_id_type=MESH,
        )

    def arrived(index, axis, slot, start, size):
        move(index, axis, slot, start, size).wait_recv()

    wide_slot, deep_slot, far_slot = slot_of(0, 0, 1), slot_of(0, 1, 0), slot_of(0, 1, 1)
    sends = []

    def launch(*args):
        copy = move(*args)
        copy.start()
        sends.append(copy)

    launch(0, "x", own, 0, half)
    launch(1, "zl", own, half, half)
    launch(2, "x", own, half, half)
    launch(3, "zl", own, 0, half)
    launch(4, "core", own, 0, rows)
    for errand in errands:
        errand.start()

    stores = []

    def store(ref, out, slot):
        copy = pltpu.make_async_copy(ref.at[slot], out.at[slot], local.at[1 + count + len(stores)])
        copy.start()
        stores.append(copy)

    def multiply(slot):
        store(held, gathered_ref, slot)
        for weight, result, product_ref in zip(weights, results, product_refs):

            def column(at):
                right = weight[:, at] if dims == NN else weight[at, :]
                result[slot, :, at] = dot(held[slot], right, dims).astype(result.dtype)

            by_columns(result.shape[2], column)
            store(result, product_ref, slot)

    for load in loads:
        load.wait()
    multiply(own)
    arrived(0, "x", wide_slot, 0, half)
    launch(5, "zl", wide_slot, 0, half)
    arrived(1, "zl", deep_slot, half, half)
    launch(6, "x", deep_slot, half, half)
    other = slot_of(1, 0, 0)
    arrived(4, "core", other, 0, rows)
    multiply(other)
    arrived(2, "x", wide_slot, half, half)
    launch(7, "core", wide_slot, 0, rows)
    arrived(3, "zl", deep_slot, 0, half)
    launch(8, "core", deep_slot, 0, rows)
    multiply(wide_slot)
    multiply(deep_slot)
    other_wide, other_deep, other_far = slot_of(1, 0, 1), slot_of(1, 1, 0), slot_of(1, 1, 1)
    arrived(7, "core", other_wide, 0, rows)
    multiply(other_wide)
    arrived(8, "core", other_deep, 0, rows)
    multiply(other_deep)
    for errand in errands:
        errand.middle()
    arrived(5, "zl", far_slot, 0, half)
    launch(9, "core", far_slot, 0, half)
    arrived(6, "x", far_slot, half, half)
    launch(10, "core", far_slot, half, half)
    multiply(far_slot)
    arrived(9, "core", other_far, 0, half)
    arrived(10, "core", other_far, half, half)
    multiply(other_far)
    for copy in sends:
        copy.wait_send()
    for copy in stores:
        copy.wait()
    for errand in errands:
        errand.finish()


def gather_multiply(block, weights, dims, collective_id, name, errands=(), out_type=F32):
    rows, depth = block.shape
    widths = [w.shape[1] if dims == NN else w.shape[0] for w in weights]
    count = len(weights)
    kinds, sources = [e[0] for e in errands], [e[1] for e in errands]
    gathered, *products = pl.pallas_call(
        functools.partial(gather_body, dims, count, kinds),
        in_specs=[pl.BlockSpec(memory_space=pl.ANY)] * (1 + count + len(kinds)),
        out_specs=[pl.BlockSpec(memory_space=pl.ANY)] * (1 + count + len(kinds)),
        out_shape=[jax.ShapeDtypeStruct((8, rows, depth), BF16)]
        + [jax.ShapeDtypeStruct((8, rows, width), out_type) for width in widths]
        + [errand_target(*errand) for errand in errands],
        scratch_shapes=[pltpu.VMEM((8, rows, depth), BF16)]
        + [pltpu.VMEM(w.shape, BF16) for w in weights]
        + [pltpu.VMEM((8, rows, width), out_type) for width in widths]
        + [
            pltpu.SemaphoreType.DMA((11,)),
            pltpu.SemaphoreType.DMA((11,)),
            pltpu.SemaphoreType.DMA((1 + count + 8 * (1 + count),)),
            *errand_scratch(kinds, sources),
        ],
        compiler_params=pltpu.CompilerParams(
            collective_id=collective_id, has_side_effects=True, vmem_limit_bytes=56 * 2**20
        ),
        name=name,
    )(block, *weights, *sources)
    flat = [v.reshape(8 * rows, v.shape[2]) for v in (gathered, *products[:count])]
    return (*flat, *products[count:])


def scatter_core(dims, lefts, weights, buffers, beside):
    sending, crossing, partial, far_recv, side_recv, total, send, recv = buffers
    rows, width = total.shape
    half = rows // 2

    def move(index, axis, src, dst):
        return pltpu.make_async_remote_copy(
            src_ref=src, dst_ref=dst, send_sem=send.at[index], recv_sem=recv.at[index],
            device_id=neighbour(axis), device_id_type=MESH,
        )

    sends = []

    def launch(*args):
        copy = move(*args)
        copy.start()
        sends.append(copy)

    def multiply(slot, write):
        def column(at):
            value = None
            for left, weight in zip(lefts, weights):
                right = weight[:, at] if dims == NN else weight[at, :]
                term = dot(left[slot], right, dims)
                value = term if value is None else value + term
            write(at, value)

        by_columns(width, column)

    places = ((1, 1), (0, 1), (1, 0), (0, 0))

    def cross(index):
        def write(at, value):
            sending[index, :, at] = value.astype(BF16)

        multiply(slot_of(1, *places[index]), write)
        launch(index, "core", sending.at[index], crossing.at[index])

    def crossed(index):
        move(index, "core", sending.at[index], crossing.at[index]).wait_recv()

    def local_sum(index):
        crossed(index)

        def write(at, value):
            partial[index, :, at] = (value + crossing[index, :, at].astype(F32)).astype(BF16)

        multiply(slot_of(0, *places[index]), write)

    first, second = pl.ds(0, half), pl.ds(half, half)
    cross(0)
    beside(0)
    cross(1)
    local_sum(0)
    launch(4, "x", partial.at[0, first], far_recv.at[0])
    launch(5, "zl", partial.at[0, second], far_recv.at[1])
    cross(2)
    local_sum(1)
    launch(6, "x", partial.at[1, first], side_recv.at[0, first])
    local_sum(2)
    launch(7, "zl", partial.at[2, second], side_recv.at[1, second])
    cross(3)
    beside(1)
    move(4, "x", partial.at[0, first], far_recv.at[0]).wait_recv()
    partial[2, first] = (partial[2, first].astype(F32) + far_recv[0].astype(F32)).astype(BF16)
    launch(8, "zl", partial.at[2, first], side_recv.at[1, first])
    move(5, "zl", partial.at[0, second], far_recv.at[1]).wait_recv()
    partial[1, second] = (partial[1, second].astype(F32) + far_recv[1].astype(F32)).astype(BF16)
    launch(9, "x", partial.at[1, second], side_recv.at[0, second])
    beside(2)
    crossed(3)

    def write(at, value):
        total[:, at] = value + crossing[3, :, at].astype(F32)

    multiply(slot_of(0, 0, 0), write)
    move(6, "x", partial.at[1, first], side_recv.at[0, first]).wait_recv()
    total[first] += side_recv[0, first].astype(F32)
    move(7, "zl", partial.at[2, second], side_recv.at[1, second]).wait_recv()
    total[second] += side_recv[1, second].astype(F32)
    beside(3)
    move(8, "zl", partial.at[2, first], side_recv.at[1, first]).wait_recv()
    total[first] += side_recv[1, first].astype(F32)
    move(9, "x", partial.at[1, second], side_recv.at[0, second]).wait_recv()
    total[second] += side_recv[0, second].astype(F32)
    return sends


def scatter_scratch(rows, width):
    return [
        pltpu.VMEM((4, rows, width), BF16),
        pltpu.VMEM((4, rows, width), BF16),
        pltpu.VMEM((3, rows, width), BF16),
        pltpu.VMEM((2, rows // 2, width), BF16),
        pltpu.VMEM((2, rows, width), BF16),
        pltpu.VMEM((rows, width), F32),
        pltpu.SemaphoreType.DMA((10,)),
        pltpu.SemaphoreType.DMA((10,)),
    ]


def scatter_body(dims, count, kinds, *refs):
    first_ref, refs, errands = take_errands(kinds, refs, 2 * count, 1)
    refs = (first_ref, *refs)
    total_ref = refs[2 * count]
    operands = refs[2 * count + 1 : 4 * count + 1]
    buffers, local = refs[4 * count + 1 : -1], refs[-1]
    loads = [
        pltpu.make_async_copy(ref, operand, local.at[i])
        for i, (ref, operand) in enumerate(zip(refs[: 2 * count], operands))
    ]
    for load in loads:
        load.start()
    greet(bool(kinds))
    for load in loads:
        load.wait()

    def beside(point):
        for errand in errands:
            if point == 0:
                errand.start()
            elif point == 3:
                errand.middle()

    sends = scatter_core(dims, operands[:count], operands[count:], buffers, beside)
    store = pltpu.make_async_copy(buffers[5], total_ref, local.at[2 * count])
    store.start()
    for copy in sends:
        copy.wait_send()
    store.wait()
    for errand in errands:
        errand.finish()


def multiply_scatter(lefts, weights, dims, collective_id, name, errands=()):
    rows = lefts[0].shape[0] // 8
    width = weights[0].shape[1] if dims == NN else weights[0].shape[0]
    count = len(lefts)
    lefts = [left.reshape(8, rows, left.shape[1]) for left in lefts]
    kinds, sources = [e[0] for e in errands], [e[1] for e in errands]
    return pl.pallas_call(
        functools.partial(scatter_body, dims, count, kinds),
        in_specs=[pl.BlockSpec(memory_space=pl.ANY)] * (2 * count + len(kinds)),
        out_specs=[pl.BlockSpec(memory_space=pl.ANY)] * (1 + len(kinds)),
        out_shape=[jax.ShapeDtypeStruct((rows, width), F32)]
        + [errand_target(*errand) for errand in errands],
        scratch_shapes=[pltpu.VMEM(v.shape, BF16) for v in (*lefts, *weights)]
        + [
            *scatter_scratch(rows, width),
            pltpu.SemaphoreType.DMA((2 * count + 1,)),
            *errand_scratch(kinds, sources),
        ],
        compiler_params=pltpu.CompilerParams(
            collective_id=collective_id, has_side_effects=True, vmem_limit_bytes=56 * 2**20
        ),
        name=name,
    )(*lefts, *weights, *sources)


def begin_body(
    tokens_ref, gain_ref, conv_ref, *refs,
):
    weight_refs, refs = refs[:5], refs[5:]
    moved_ref, gathered_ref, product_ref, weights_ref, new_conv_ref, *refs = refs
    tokens, held, weights, result, send, recv, errand_send, errand_recv, local = refs
    rows = tokens_ref.shape[0]
    half = rows // 2
    starts = [0]
    for ref in weight_refs:
        starts.append(starts[-1] + ref.shape[1])
    parts = [pl.ds(start, ref.shape[1]) for start, ref in zip(starts, weight_refs)]
    greet(True)
    kinds = [Exchange, Exchange] + [Swap] * 5
    targets = [tokens, new_conv_ref] + [weights.at[:, part] for part in parts]
    block, taps, *swaps = make_errands(
        kinds, [tokens_ref, conv_ref, *weight_refs], targets, errand_send, errand_recv, local
    )
    block.start()
    taps.start()
    swaps[0].start()
    block.finish()
    for swap in swaps[1:]:
        swap.start()
    own = slot_of(0, 0, 0)
    values = tokens[...].astype(F32)
    scale = lax.rsqrt(jnp.mean(values * values, -1, keepdims=True) + 1e-05)
    held[own] = (values * scale * gain_ref[...]).astype(BF16)
    keep = pltpu.make_async_copy(tokens, moved_ref, local.at[7])
    keep.start()

    def move(index, axis, slot, start, size):
        view = held.at[slot, pl.ds(start, size)]
        return pltpu.make_async_remote_copy(
            src_ref=view, dst_ref=view, send_sem=send.at[index], recv_sem=recv.at[index],
            device_id=neighbour(axis), device_id_type=MESH,
        )

    def arrived(*args):
        move(*args).wait_recv()

    wide_slot, deep_slot, far_slot = slot_of(0, 0, 1), slot_of(0, 1, 0), slot_of(0, 1, 1)
    sends = []

    def launch(*args):
        copy = move(*args)
        copy.start()
        sends.append(copy)

    launch(0, "x", own, 0, half)
    launch(1, "zl", own, half, half)
    launch(2, "x", own, half, half)
    launch(3, "zl", own, 0, half)
    launch(4, "core", own, 0, rows)
    arrived(0, "x", wide_slot, 0, half)
    launch(5, "zl", wide_slot, 0, half)
    arrived(1, "zl", deep_slot, half, half)
    launch(6, "x", deep_slot, half, half)
    swaps[0].middle()
    arrived(2, "x", wide_slot, half, half)
    launch(7, "core", wide_slot, 0, rows)
    arrived(3, "zl", deep_slot, 0, half)
    launch(8, "core", deep_slot, 0, rows)
    swaps[1].middle()
    arrived(5, "zl", far_slot, 0, half)
    launch(9, "core", far_slot, 0, half)
    arrived(6, "x", far_slot, half, half)
    launch(10, "core", far_slot, half, half)
    arrived(4, "core", slot_of(1, 0, 0), 0, rows)
    arrived(7, "core", slot_of(1, 0, 1), 0, rows)
    arrived(8, "core", slot_of(1, 1, 0), 0, rows)
    arrived(9, "core", slot_of(1, 1, 1), 0, half)
    arrived(10, "core", slot_of(1, 1, 1), half, half)
    store = pltpu.make_async_copy(held, gathered_ref, local.at[8])
    store.start()
    stores = []
    for index, (swap, part) in enumerate(zip(swaps, parts)):
        if index + 2 < len(swaps):
            swaps[index + 2].middle()
        swap.finish()

        def multiply(slot, _, part=part):
            result[slot, :, part] = dot(held[slot], weights[:, part], NN)
            return 0

        lax.fori_loop(0, 8, multiply, 0)
        for view, out, sem in (
            (result.at[:, :, part], product_ref.at[:, :, part], 9 + 2 * index),
            (weights.at[:, part], weights_ref.at[:, part], 10 + 2 * index),
        ):
            copy = pltpu.make_async_copy(view, out, local.at[sem])
            copy.start()
            stores.append(copy)
    taps.finish()
    for copy in sends:
        copy.wait_send()
    keep.wait()
    store.wait()
    for copy in stores:
        copy.wait()


def begin(tokens, gain, conv, weights, collective_id):
    rows, depth = tokens.shape
    width = sum(w.shape[1] for w in weights)
    hbm = pl.BlockSpec(memory_space=pl.ANY)
    moved, gathered, product, weights, conv = pl.pallas_call(
        begin_body,
        in_specs=[hbm, pl.BlockSpec(memory_space=pltpu.VMEM)] + [hbm] * (1 + len(weights)),
        out_specs=[hbm] * 5,
        out_shape=[
            jax.ShapeDtypeStruct(tokens.shape, BF16),
            jax.ShapeDtypeStruct((8, rows, depth), BF16),
            jax.ShapeDtypeStruct((8, rows, width), F32),
            jax.ShapeDtypeStruct((depth, width), BF16),
            jax.ShapeDtypeStruct(conv.shape, conv.dtype),
        ],
        scratch_shapes=[
            pltpu.VMEM((rows, depth), BF16),
            pltpu.VMEM((8, rows, depth), BF16),
            pltpu.VMEM((depth, width), BF16),
            pltpu.VMEM((8, rows, width), F32),
            pltpu.SemaphoreType.DMA((11,)),
            pltpu.SemaphoreType.DMA((11,)),
            pltpu.SemaphoreType.DMA((12,)),
            pltpu.SemaphoreType.DMA((12,)),
            pltpu.SemaphoreType.DMA((19,)),
        ],
        compiler_params=pltpu.CompilerParams(
            collective_id=collective_id, has_side_effects=True, vmem_limit_bytes=56 * 2**20
        ),
        name="begin",
    )(tokens, gain, conv, *weights)
    return moved, gathered.reshape(8 * rows, depth), product.reshape(8 * rows, width), weights, conv


CHUNKS = 4


def finish_body(kinds, *refs):
    first_ref, refs, errands = take_errands(kinds, refs, 7, 3)
    left_ref, weight_ref, grad_ref, tokens_ref, resid_ref, gain_ref, small_ref = first_ref, *refs[:6]
    tokens_grad_ref, total_grad_ref, small_out_ref, *refs = refs[6:]
    left, weight, mine, came, far, tokens, resid, moving, small, small_recv = refs[:10]
    buffers, refs = refs[10:18], refs[18:]
    chain_send, chain_recv, small_send, small_recv_sem, move_send, move_recv, local = refs
    loads = [
        pltpu.make_async_copy(source, target, local.at[i])
        for i, (source, target) in enumerate(
            (
                (left_ref, left), (weight_ref, weight), (tokens_ref, tokens), (resid_ref, resid),
                (small_ref, small), (row_half(grad_ref, lax.axis_index("y")), mine),
            )
        )
    ]
    for load in loads:
        load.start()
    greet(True)
    y = lax.axis_index("y")
    moved = is_moved()
    stays = jnp.logical_not(moved)
    size = mine.shape[0] // CHUNKS

    def chain(stage, index, source, target, axis):
        return pltpu.make_async_remote_copy(
            src_ref=source, dst_ref=target, send_sem=chain_send.at[stage, index],
            recv_sem=chain_recv.at[stage, index], device_id=neighbour(axis), device_id_type=MESH,
        )

    def rows_in(ref, index, other=False):
        owner = 1 - y if other else y
        start = owner * (size * CHUNKS) + index * size
        return ref.at[pl.ds(pl.multiple_of(start, 16), size)]

    def chunk(ref, index):
        return ref.at[pl.ds(index * size, size)]

    def over(index):
        return chain(0, index, rows_in(grad_ref, index, True), chunk(came, index), "y")

    def across(index):
        return chain(1, index, chunk(mine, index), chunk(far, index), "zh")

    def back(index):
        return chain(2, index, chunk(mine, index), rows_in(total_grad_ref, index), "y")

    def landing(index):
        view = rows_in(total_grad_ref, index, True)
        return chain(2, index, view, view, "y")

    def cross(index):
        return chain(3, index, chunk(mine, index), rows_in(total_grad_ref, index), "core")

    def pass_on(index):
        view = rows_in(total_grad_ref, index, True)
        return chain(4, index, view, view, "core")

    def near(index):
        return pltpu.make_async_copy(
            chunk(mine, index), rows_in(total_grad_ref, index), local.at[6 + index]
        )

    def add(index, other):
        at = pl.ds(index * size, size)
        mine[at] = (mine[at].astype(F32) + other[at].astype(F32)).astype(BF16)

    def sum_y(index):
        over(index).wait_recv()
        add(index, came)
        pl.when(moved)(across(index).start)

    def sum_z(index):
        @pl.when(stays)
        def _():
            across(index).wait_recv()
            add(index, far)
            back(index).start()
            cross(index).start()
            near(index).start()

    def forward(index):
        @pl.when(stays)
        def _():
            landing(index).wait_recv()
            pass_on(index).start()

    for index in range(CHUNKS):
        over(index).start()
    for load in loads:
        load.wait()

    def beside(point):
        if point == 0:
            for errand in errands:
                errand.start()
            sum_y(0)
        elif point == 1:
            sum_y(1)
        elif point == 2:
            sum_z(0)
            sum_y(2)
        elif point == 3:
            for errand in errands:
                errand.middle()
            sum_z(1)

    sends = scatter_core(NT, [left], [weight], buffers, beside)
    total = buffers[5]
    gain = gain_ref[...]

    def backward(step, along):
        at = pl.ds(pl.multiple_of(step * 32, 32), 32)
        values = tokens[at].astype(F32)
        scale = lax.rsqrt(jnp.mean(values * values, -1, keepdims=True) + 1e-05)
        grad = total[at]
        scaled = grad * gain
        mean = jnp.mean(values * scaled, -1, keepdims=True)
        change = scale * scaled - values * (scale * scale * scale * mean)
        moving[at] = (resid[at] + change).astype(BF16)
        return along + jnp.sum(grad * values * scale, 0, keepdims=True)

    along = lax.fori_loop(
        0, total.shape[0] // 32, backward, jnp.zeros((1, total.shape[1]), F32)
    )
    small[0:1, :] = along
    move = make_errands([Exchange], [moving], [tokens_grad_ref], move_send, move_recv, local.at[pl.ds(6 + CHUNKS, 1)])[0]
    move.start()
    sum_y(3)
    axes = ("core", "x", "zl", "y", "zh")

    def small_round(index):
        copy = pltpu.make_async_remote_copy(
            src_ref=small, dst_ref=small_recv.at[index], send_sem=small_send.at[index],
            recv_sem=small_recv_sem.at[index], device_id=neighbour(axes[index]),
            device_id_type=MESH,
        )
        copy.start()
        copy.wait()
        small[...] += small_recv[index]

    small_round(0)
    small_round(1)
    small_round(2)
    sum_z(2)
    forward(0)
    small_round(3)
    small_round(4)
    small_store = pltpu.make_async_copy(small, small_out_ref, local.at[7 + CHUNKS])
    small_store.start()
    forward(1)
    sum_z(3)
    forward(2)
    forward(3)
    for copy in sends:
        copy.wait_send()
    for index in range(CHUNKS):
        over(index).wait_send()

        @pl.when(moved)
        def _(index=index):
            across(index).wait_send()
            cross(index).wait_recv()
            pass_on(index).wait_recv()

        @pl.when(stays)
        def _(index=index):
            back(index).wait_send()
            cross(index).wait_send()
            pass_on(index).wait_send()
            near(index).wait()

    for errand in errands:
        errand.finish()
    move.finish()
    small_store.wait()


def finish(left, weight, weight_grad, tokens, resid_grad, gain, small, collective_id, errands=()):
    rows, width = tokens.shape
    left = left.reshape(8, rows, left.shape[1])
    kinds, sources = [e[0] for e in errands], [e[1] for e in errands]
    hbm = pl.BlockSpec(memory_space=pl.ANY)
    depth, columns = weight_grad.shape
    half = pltpu.VMEM((depth // 2, columns), BF16)
    return pl.pallas_call(
        functools.partial(finish_body, kinds),
        in_specs=[hbm] * 5 + [pl.BlockSpec(memory_space=pltpu.VMEM), hbm] + [hbm] * len(kinds),
        out_specs=[hbm] * (3 + len(kinds)),
        out_shape=[
            jax.ShapeDtypeStruct(tokens.shape, BF16),
            jax.ShapeDtypeStruct(weight_grad.shape, BF16),
            jax.ShapeDtypeStruct(small.shape, F32),
            *[errand_target(*errand) for errand in errands],
        ],
        scratch_shapes=[
            pltpu.VMEM(left.shape, BF16),
            pltpu.VMEM(weight.shape, BF16),
            half,
            half,
            half,
            pltpu.VMEM((rows, width), BF16),
            pltpu.VMEM((rows, width), F32),
            pltpu.VMEM((rows, width), BF16),
            pltpu.VMEM(small.shape, F32),
            pltpu.VMEM((5, *small.shape), F32),
            *scatter_scratch(rows, width),
            pltpu.SemaphoreType.DMA((5, CHUNKS)),
            pltpu.SemaphoreType.DMA((5, CHUNKS)),
            pltpu.SemaphoreType.DMA((5,)),
            pltpu.SemaphoreType.DMA((5,)),
            pltpu.SemaphoreType.DMA((1,)),
            pltpu.SemaphoreType.DMA((1,)),
            pltpu.SemaphoreType.DMA((8 + CHUNKS,)),
            *errand_scratch(kinds, sources),
        ],
        compiler_params=pltpu.CompilerParams(
            collective_id=collective_id, has_side_effects=True, vmem_limit_bytes=58 * 2**20
        ),
        name="finish",
    )(left, weight, weight_grad, tokens, resid_grad, gain, small, *sources)


def rms_scale(values, gain):
    return values * lax.rsqrt(jnp.mean(values * values, -1, keepdims=True) + 1e-05) * gain


def swiglu(gate, up_vals):
    return jax.nn.silu(gate) * up_vals


def left_product(left, right):
    return dot(left, right, TN)


def token_scales(group_ids, mixture_counts):
    group_cols = lax.broadcasted_iota(jnp.int32, (1, GROUPS), 1)
    counts = mixture_counts.astype(F32)
    group_scale = jnp.sqrt(jnp.mean(counts) / counts)
    return jnp.sum(jnp.where(group_ids[:, None] == group_cols, group_scale[None, :], 0.0), 1)


def mixer_weights(w_query, w_key, w_value, w_gate_mix, w_beta):
    padded = jnp.pad(w_beta, ((0, 0), (0, 128 - w_beta.shape[1])))
    return jnp.concatenate([w_query, w_key, w_value, w_gate_mix, padded], 1)


ALL = ("y", "core", "zh", "zl", "x")
SIZES = (2, 2, 2, 2, 2)


FORWARD_PLAN = (
    (0, 0, "start"), (0, 1, "start"), (1, 0, "settle"), (3, 0, "spread"), (3, 2, "start"),
    (4, 1, "middle"), (6, 0, "middle"), (7, 0, "late"), (7, 2, "middle"),
    (7, 0, "finish"), (7, 1, "finish"), (7, 2, "finish"),
)
BACKWARD_PLAN = (
    (0, 0, "start"), (0, 1, "start"), (0, 2, "start"), (0, 3, "start"), (4, 2, "middle"),
    (7, 0, "finish"), (7, 1, "finish"), (7, 2, "finish"), (7, 3, "finish"),
)


def halves_sum(values, came):
    rows = came.shape[0]
    mine = lax.dynamic_slice_in_dim(values, lax.axis_index("y") * rows, rows, 0)
    return (mine.astype(F32) + came.astype(F32)).astype(BF16)


def total_of(part, far):
    return (part.astype(F32) + far.astype(F32)).astype(BF16)


def shards_ring(
    tokens, group_ids, mixture_counts, grad_out, norm1_gain, w_query, w_key, w_value, w_gate_mix,
    w_beta, conv_query, conv_key, conv_value, out_gain, w_out, norm2_gain, w_gate, w_up, w_down,
):
    heads = w_beta.shape[1]
    head_cols = w_query.shape[1]
    gain = out_gain.astype(F32)[None]
    gain1 = norm1_gain.astype(F32)[None]
    conv = jnp.concatenate([conv_query, conv_key, conv_value], 1).astype(F32)
    conv = jnp.pad(conv, ((0, 4), (0, 0)))
    grad_mlp = grad_out.astype(F32) * token_scales(group_ids, mixture_counts)[:, None]
    padded_beta = jnp.pad(w_beta, ((0, 0), (0, 128 - heads)))
    tokens, gathered, projected, mix_weights, conv = begin(
        tokens, gain1, conv, [w_query, w_key, w_value, w_gate_mix, padded_beta], 1
    )
    inputs = tokens.astype(F32)
    mixed, *kept, gathered_grad, w_out, w_gate = mixer_forward(
        projected, conv, gain, heads,
        [(ExchangeGather, grad_mlp.astype(BF16)), (Swap, w_out), (Swap, w_gate)],
        FORWARD_PLAN, 2,
    )
    gathered_grad = gathered_grad.reshape(-1, gathered_grad.shape[2])
    own = (lax.axis_index("core") * 2 + lax.axis_index("zl")) * 2 + lax.axis_index("x")
    rows = tokens.shape[0]
    grad_rows = lax.dynamic_slice_in_dim(gathered_grad, own * rows, rows, 0).astype(F32)
    attn, w_up = multiply_scatter([mixed], [w_out], NN, 3, "scatter_attn", [(Swap, w_up)])
    resid = inputs + attn
    normed_mlp, norm2_back = jax.vjp(rms_scale, resid, norm2_gain.astype(F32))
    gathered_mlp, gate, up_vals, w_down = gather_multiply(
        normed_mlp.astype(BF16), [w_gate, w_up], NN, 4, "gather_normed_mlp", [(Swap, w_down)]
    )
    hidden_full, swiglu_back = jax.vjp(swiglu, gate, up_vals)
    hidden = hidden_full.astype(BF16)
    hidden_grad = dot(gathered_grad, w_down, NT)
    gate_grad, up_grad = (v.astype(BF16) for v in swiglu_back(hidden_grad))
    down_grad = left_product(hidden, gathered_grad).astype(BF16)
    gate_wgrad = left_product(gathered_mlp, gate_grad).astype(BF16)
    up_wgrad = left_product(gathered_mlp, up_grad).astype(BF16)
    normed_mlp_grad, down_came, gate_came = multiply_scatter(
        [gate_grad, up_grad], [w_gate, w_up], NT, 5, "scatter_normed_mlp_grad",
        [(HalfOverY, down_grad), (HalfOverY, gate_wgrad)],
    )
    resid_norm_grad, norm2_grad = norm2_back(normed_mlp_grad)
    resid_grad = grad_rows + resid_norm_grad
    down_part = halves_sum(down_grad, down_came)
    gate_part = halves_sum(gate_wgrad, gate_came)
    gathered_attn, mixed_grad, up_came, down_far = gather_multiply(
        resid_grad.astype(BF16), [w_out], NT, 6, "gather_attn_grad",
        [(HalfOverY, up_wgrad), (Across, down_part)],
    )
    up_part = halves_sum(up_wgrad, up_came)
    out_grad = left_product(mixed, gathered_attn).astype(BF16)
    raw_grad, conv_grad, gain_grad, gate_far, up_far, down_total, out_came = mixer_backward(
        projected, conv, gain, mixed_grad, *kept, heads,
        [
            (Across, gate_part), (Across, up_part), (Spread, total_of(down_part, down_far)),
            (HalfOverY, out_grad),
        ],
        BACKWARD_PLAN, 7,
    )
    out_part = halves_sum(out_grad, out_came)
    mlp_out, gate_total, up_total, out_far = multiply_scatter(
        [hidden], [w_down], NN, 8, "scatter_mlp",
        [
            (Spread, total_of(gate_part, gate_far)), (Spread, total_of(up_part, up_far)),
            (Across, out_part),
        ],
    )
    output = (resid + mlp_out).astype(BF16)
    mix_weight_grad = left_product(gathered, raw_grad).astype(BF16)
    width = tokens.shape[1]
    placed = jnp.where(
        lax.broadcasted_iota(jnp.int32, (8, 1, 1), 0) == own, conv_grad[None, :4], 0.0
    ).reshape(-1, width)
    small = jnp.concatenate(
        [
            jnp.zeros((1, width), F32), norm2_grad[None],
            jnp.pad(gain_grad[:1], ((0, 0), (0, width - gain_grad.shape[1]))), placed,
        ],
        0,
    )
    small = jnp.pad(small, ((0, -small.shape[0] % 8), (0, 0)))
    grad_tokens, mix_total, small, output, out_total = finish(
        raw_grad, mix_weights, mix_weight_grad, tokens, resid_grad, gain1, small, 9,
        [(Exchange, output), (Spread, total_of(out_part, out_far))],
    )
    shard = (lax.axis_index("zh") * 2 + lax.axis_index("zl")) * 2 + lax.axis_index("x")
    placed = small[3 : 3 + 4 * 24 * head_cols // width].reshape(8, 4, 3 * head_cols)
    conv_total = lax.dynamic_index_in_dim(placed, shard, 0, keepdims=False)
    mix_total = mix_total.astype(F32)
    return (
        output,
        grad_tokens,
        small[0],
        mix_total[:, 0:head_cols],
        mix_total[:, head_cols : 2 * head_cols],
        mix_total[:, 2 * head_cols : 3 * head_cols],
        mix_total[:, 3 * head_cols : 4 * head_cols],
        mix_total[:, 4 * head_cols : 4 * head_cols + heads],
        conv_total[:, 0:head_cols],
        conv_total[:, head_cols : 2 * head_cols],
        conv_total[:, 2 * head_cols :],
        small[2, :HEAD_DIM],
        out_total.astype(F32),
        small[1],
        gate_total.astype(F32),
        up_total.astype(F32),
        down_total.astype(F32),
    )


def right_product(left, right):
    return dot(left, right, NT)


def make_fold(kept_rows, weight, piece):
    weight_grad = left_product(kept_rows, piece)
    rows_grad = right_product(piece, weight)
    return (weight_grad, rows_grad)


def make_rows(source, weight, transposed):
    if transposed:
        return right_product(source, weight)
    return jnp.dot(source, weight, preferred_element_type=F32)


def shards(
    tokens,
    group_ids,
    mixture_counts,
    grad_out,
    norm1_gain,
    w_query,
    w_key,
    w_value,
    w_gate_mix,
    w_beta,
    conv_query,
    conv_key,
    conv_value,
    out_gain,
    w_out,
    norm2_gain,
    w_gate,
    w_up,
    w_down,
):
    inputs = tokens.astype(F32)
    normed, norm1_back = jax.vjp(rms_scale, inputs, norm1_gain.astype(F32))
    gathered = lax.all_gather(normed.astype(BF16), "tp", axis=0, tiled=True)
    heads = w_beta.shape[1]
    mix_weights = mixer_weights(w_query, w_key, w_value, w_gate_mix, w_beta)
    projected = jnp.dot(gathered, mix_weights, preferred_element_type=F32)
    head_cols = w_query.shape[1]
    conv = jnp.concatenate([conv_query, conv_key, conv_value], 1).astype(F32)
    gain = out_gain.astype(F32)[None]
    mixed, *kept = mixer_forward(projected, conv, gain, heads)
    attn = lax.psum_scatter(
        make_rows(mixed, w_out, False).astype(jnp.bfloat16), "tp", scatter_dimension=0, tiled=True
    ).astype(jnp.float32)
    resid = inputs + attn
    normed_mlp, norm2_back = jax.vjp(rms_scale, resid, norm2_gain.astype(F32))
    gathered_mlp = lax.all_gather(normed_mlp.astype(BF16), "tp", axis=0, tiled=True)
    pair_weights = jnp.concatenate([w_gate, w_up], 1)
    ff_cols = w_gate.shape[1]
    paired = jnp.dot(gathered_mlp, pair_weights, preferred_element_type=F32)
    hidden_full, swiglu_back = jax.vjp(swiglu, paired[:, :ff_cols], paired[:, ff_cols:])
    hidden = hidden_full.astype(BF16)
    mlp_out = lax.psum_scatter(
        make_rows(hidden, w_down, False).astype(jnp.bfloat16), "tp", scatter_dimension=0, tiled=True
    ).astype(jnp.float32)
    output = (resid + mlp_out).astype(BF16)
    token_scale = token_scales(group_ids, mixture_counts)
    grad_rows = grad_out.astype(F32) * token_scale[:, None]
    grad_mlp = grad_rows.astype(BF16)
    grad_w_down, hidden_grad = make_fold(
        hidden, w_down, lax.all_gather(grad_mlp, "tp", axis=0, tiled=True)
    )
    gate_grad, up_grad = swiglu_back(hidden_grad)
    pair_grad = jnp.concatenate([gate_grad, up_grad], 1).astype(BF16)
    pair_weight_grad = left_product(gathered_mlp, pair_grad)
    normed_mlp_grad = lax.psum_scatter(
        make_rows(pair_grad, pair_weights, True).astype(jnp.bfloat16),
        "tp",
        scatter_dimension=0,
        tiled=True,
    ).astype(jnp.float32)
    resid_norm_grad, norm2_grad = norm2_back(normed_mlp_grad)
    resid_grad = grad_rows + resid_norm_grad
    attn_grad = resid_grad.astype(BF16)
    grad_w_out, mixed_grad = make_fold(
        mixed, w_out, lax.all_gather(attn_grad, "tp", axis=0, tiled=True)
    )
    raw_grad, conv_grad, gain_grad = mixer_backward(
        projected, conv, gain, mixed_grad, *kept, heads
    )
    mix_weight_grad = left_product(gathered, raw_grad)
    normed_grad = lax.psum_scatter(
        make_rows(raw_grad, mix_weights, True).astype(jnp.bfloat16),
        "tp",
        scatter_dimension=0,
        tiled=True,
    ).astype(jnp.float32)
    input_norm_grad, norm1_grad = norm1_back(normed_grad)
    grad_tokens = (resid_grad + input_norm_grad).astype(BF16)
    summed = (
        lax.psum(mix_weight_grad.astype(jnp.bfloat16), "dp").astype(jnp.float32),
        lax.psum(grad_w_out.astype(jnp.bfloat16), "dp").astype(jnp.float32),
        lax.psum(pair_weight_grad.astype(jnp.bfloat16), "dp").astype(jnp.float32),
        lax.psum(grad_w_down.astype(jnp.bfloat16), "dp").astype(jnp.float32),
    )
    conv_total = lax.psum(conv_grad[:4], "dp")
    gains = lax.psum((norm1_grad, gain_grad[0], norm2_grad), ("dp", "tp"))
    mix_total = summed[0]
    pair_total = summed[2]
    return (
        output,
        grad_tokens,
        gains[0],
        mix_total[:, 0:head_cols],
        mix_total[:, head_cols : 2 * head_cols],
        mix_total[:, 2 * head_cols : 3 * head_cols],
        mix_total[:, 3 * head_cols : 4 * head_cols],
        mix_total[:, 4 * head_cols : 4 * head_cols + heads],
        conv_total[:, 0:head_cols],
        conv_total[:, head_cols : 2 * head_cols],
        conv_total[:, 2 * head_cols :],
        gains[1],
        summed[1],
        gains[2],
        pair_total[:, :ff_cols],
        pair_total[:, ff_cols:],
        summed[3],
    )


def solution(mesh):
    rows, cols, all_rows = "tp", "tp", ("dp", "tp")
    body = shards
    if dict(mesh.shape) == {"dp": 4, "tp": 8}:
        mesh = Mesh(mesh.devices.reshape(SIZES), ALL)
        rows = cols = ("zh", "zl", "x")
        all_rows = ALL
        body = shards_ring
    by_row, by_col, by_token = P(rows, None), P(None, cols), P(all_rows, None)
    return jax.shard_map(
        body,
        mesh=mesh,
        in_specs=(
            by_token, P(all_rows), P(), by_token, P(), by_col, by_col, by_col, by_col, by_col,
            by_col, by_col, by_col, P(), by_row, P(), by_col, by_col, by_row,
        ),
        out_specs=(
            by_token, by_token, P(), by_col, by_col, by_col, by_col, by_col, by_col, by_col,
            by_col, P(), by_row, P(), by_col, by_col, by_row,
        ),
        check_vma=False,
    )
```

```python
import functools

import jax
import jax.numpy as jnp
from jax import lax
from jax.experimental import pallas as pl
from jax.experimental.pallas import tpu as pltpu
from jax.sharding import Mesh
from jax.sharding import PartitionSpec as P

GROUPS = 8
HEAD_DIM = 128
SPAN = 64
SEQ_LEN = 2048
TILE = 256
F32 = jnp.float32
BF16 = jnp.bfloat16
NN = ((1,), (0,))
NT = ((1,), (1,))
TN = ((0,), (0,))


def split(values):
    high = values.astype(BF16)
    return high, (values - high.astype(F32)).astype(BF16)


def dot(left, right, dims):
    return lax.dot_general(left, right, (dims, ((), ())), preferred_element_type=F32)


def product(left, right, dims):
    return (
        dot(left[0], right[0], dims)
        + (dot(left[0], right[1], dims) + dot(left[1], right[0], dims))
    )


def quick(left, right, dims):
    return dot(left[0], right[0], dims)


def rows_of(pair, start, size):
    return pair[0][start : start + size], pair[1][start : start + size]


def sigmoid(values):
    return 1.0 / (1.0 + jnp.exp(-values))


def tile_masks():
    row = lax.broadcasted_iota(jnp.int32, (TILE, TILE), 0)
    col = lax.broadcasted_iota(jnp.int32, (TILE, TILE), 1)
    return row, col


def invert_all(lowers, row, col, refine=False):
    def level(size):
        return (row // (2 * size) == col // (2 * size)) & (row // size > col // size)

    first = level(1)
    eye = jnp.where(row == col, 1.0, 0.0)
    inverses = [eye - jnp.where(first, lower, 0.0) for lower in lowers]
    size = 2
    while size < SPAN:
        mask = level(size)
        parts = [split(jnp.where(mask, lower, 0.0)) for lower in lowers]
        held = [split(inverse) for inverse in inverses]
        firsts = [quick(part, h, NN) for part, h in zip(parts, held)]
        seconds = [quick(h, split(f), NN) for h, f in zip(held, firsts)]
        inverses = [inverse - second for inverse, second in zip(inverses, seconds)]
        size *= 2
    if True:
        held = [split(inverse) for inverse in inverses]
        rest = [
            eye - inverse - product(split(lower), h, NN)
            for lower, inverse, h in zip(lowers, inverses, held)
        ]
        inverses = [
            inverse + quick(h, split(r), NN) for inverse, h, r in zip(inverses, held, rest)
        ]
    return inverses


def conv_rows(buffer, taps):
    total = taps[0:1] * buffer[pl.ds(5, TILE), :]
    for offset in range(1, 4):
        total = total + taps[offset : offset + 1] * buffer[pl.ds(5 + offset, TILE), :]
    return total


LATE_PHASES = ("settle_late", "forward", "finish")


def run_errands(errands, plan, step, late):
    if not errands:
        return
    if not late:
        pl.when(step == 0)(lambda: greet(True))
    for at in sorted({entry[0] for entry in plan}):

        @pl.when(step == at)
        def _(at=at):
            for when, index, phase in plan:
                if when == at and (phase in LATE_PHASES) == late:
                    getattr(errands[index], phase)()


def errand_operands(errands):
    kinds, sources = [e[0] for e in errands], [e[1] for e in errands]
    specs = [pl.BlockSpec(memory_space=pl.ANY)] * len(errands)
    shapes = [errand_target(*errand) for errand in errands]
    return kinds, sources, specs, shapes, errand_scratch(kinds, sources) if errands else []


def mixer_params(errands, collective_id):
    extra = {"collective_id": collective_id, "has_side_effects": True} if errands else {}
    return pltpu.CompilerParams(vmem_limit_bytes=48 * 2**20, **extra)


def mixer_forward_body(heads, kinds, plan, *refs):
    first_ref, refs, errands = take_errands(kinds, refs, 3, 6) if kinds else (refs[0], refs[1:], ())
    proj_ref = first_ref
    conv_ref, gain_ref, mixed_ref, wu_ref, fresh_ref, out_ref, state_ref, inverse_ref, *refs = refs
    rows_buf, state = refs
    tile = pl.program_id(1)
    run_errands(errands, plan, tile, False)
    wide = heads * HEAD_DIM

    @pl.when(tile == 0)
    def _():
        rows_buf[0:8, :] = jnp.zeros((8, 3 * wide), F32)
        state[...] = jnp.zeros_like(state)

    @pl.when(tile > 0)
    def _():
        rows_buf[0:8, :] = rows_buf[TILE : TILE + 8, :]

    rows_buf[8 : 8 + TILE, :] = proj_ref[:, : 3 * wide]
    summed = conv_rows(rows_buf, conv_ref[...])
    active = summed * sigmoid(summed)
    row, col = tile_masks()
    same = row // SPAN == col // SPAN
    held = []
    for head in range(heads):
        lo = head * HEAD_DIM
        query = active[:, lo : lo + HEAD_DIM]
        key = active[:, wide + lo : wide + lo + HEAD_DIM]
        value = active[:, 2 * wide + lo : 2 * wide + lo + HEAD_DIM]
        beta = sigmoid(proj_ref[:, 4 * wide + head : 4 * wide + head + 1])
        query = query * (
            lax.rsqrt(jnp.sum(query * query, -1, keepdims=True) + 1e-06) * HEAD_DIM ** (-0.5)
        )
        key = key * lax.rsqrt(jnp.sum(key * key, -1, keepdims=True) + 1e-06)
        key_beta = key * beta
        held.append((split(query), split(key), key_beta, value * beta))
    lowers = [
        jnp.where(same & (row > col), product(split(key_beta), key_s, NT), 0.0)
        for _, key_s, key_beta, _ in held
    ]
    inverses = invert_all(lowers, row, col)
    boths = [
        product(split(inverse), split(jnp.concatenate([key_beta, value_beta], 1)), NN)
        for inverse, (_, _, key_beta, value_beta) in zip(inverses, held)
    ]
    scores = [
        jnp.where(same & (row >= col), product(query_s, key_s, NT), 0.0)
        for query_s, key_s, _, _ in held
    ]
    weights = [split(both[:, :HEAD_DIM]) for both in boths]
    memories = [state[head] for head in range(heads)]
    fresh_all = [[] for _ in range(heads)]
    carried_all = [[] for _ in range(heads)]
    for block in range(TILE // SPAN):
        start = block * SPAN
        for head in range(heads):
            state_ref[block, head] = memories[head]
        reads = [
            product(
                tuple(
                    jnp.concatenate([a[start : start + SPAN], b[start : start + SPAN]], 0)
                    for a, b in zip(weights[head], held[head][0])
                ),
                split(memories[head]),
                NN,
            )
            for head in range(heads)
        ]
        for head in range(heads):
            fresh_all[head].append(boths[head][start : start + SPAN, HEAD_DIM:] - reads[head][:SPAN])
            carried_all[head].append(reads[head][SPAN:])
        memories = [
            memories[head]
            + product(rows_of(held[head][1], start, SPAN), split(fresh_all[head][-1]), TN)
            for head in range(heads)
        ]
    for head in range(heads):
        lo = head * HEAD_DIM
        state[head] = memories[head]
        inverse_ref[head] = inverses[head]
        wu_ref[:, 2 * lo : 2 * lo + 2 * HEAD_DIM] = boths[head]
        fresh = jnp.concatenate(fresh_all[head], 0)
        fresh_ref[:, lo : lo + HEAD_DIM] = fresh
        out = jnp.concatenate(carried_all[head], 0)
        out = out + product(split(scores[head]), split(fresh), NN)
        out_ref[:, lo : lo + HEAD_DIM] = out
        gate = proj_ref[:, 3 * wide + lo : 3 * wide + lo + HEAD_DIM]
        scale = lax.rsqrt(jnp.mean(out * out, -1, keepdims=True) + 1e-05)
        mixed = out * scale * gain_ref[...] * (gate * sigmoid(gate))
        mixed_ref[:, lo : lo + HEAD_DIM] = mixed.astype(BF16)
    run_errands(errands, plan, tile, True)


def mixer_forward(proj, conv, gain, heads, errands=(), plan=(), collective_id=None):
    rows = proj.shape[0]
    wide = heads * HEAD_DIM
    tiles = SEQ_LEN // TILE
    seqs = rows // SEQ_LEN
    blocks = TILE // SPAN

    def at(seq, tile):
        return (seq * tiles + tile, 0)

    kinds, sources, specs, shapes, scratch = errand_operands(errands)
    return pl.pallas_call(
        functools.partial(mixer_forward_body, heads, kinds, plan),
        grid=(seqs, tiles),
        in_specs=[
            pl.BlockSpec((TILE, proj.shape[1]), at),
            pl.BlockSpec(conv.shape, lambda seq, tile: (0, 0)),
            pl.BlockSpec(gain.shape, lambda seq, tile: (0, 0)),
            *specs,
        ],
        out_specs=[
            pl.BlockSpec((TILE, wide), at),
            pl.BlockSpec((TILE, 2 * wide), at),
            pl.BlockSpec((TILE, wide), at),
            pl.BlockSpec((TILE, wide), at),
            pl.BlockSpec((blocks, heads, HEAD_DIM, HEAD_DIM), lambda s, t: (s * tiles + t, 0, 0, 0)),
            pl.BlockSpec((None, heads, TILE, TILE), lambda s, t: (s * tiles + t, 0, 0, 0)),
            *specs,
        ],
        out_shape=[
            jax.ShapeDtypeStruct((rows, wide), BF16),
            jax.ShapeDtypeStruct((rows, 2 * wide), F32),
            jax.ShapeDtypeStruct((rows, wide), F32),
            jax.ShapeDtypeStruct((rows, wide), F32),
            jax.ShapeDtypeStruct((rows // SPAN, heads, HEAD_DIM, HEAD_DIM), F32),
            jax.ShapeDtypeStruct((rows // TILE, heads, TILE, TILE), F32),
            *shapes,
        ],
        scratch_shapes=[
            pltpu.VMEM((TILE + 8, 3 * wide), F32),
            pltpu.VMEM((heads, HEAD_DIM, HEAD_DIM), F32),
            *scratch,
        ],
        compiler_params=mixer_params(errands, collective_id),
        name="mixer_forward",
    )(proj, conv, gain, *sources)


def unit_back(raw, scale, grad):
    along = jnp.sum(raw * grad, -1, keepdims=True)
    return scale * grad - raw * (scale * scale * scale * along)


def mixer_backward_body(heads, kinds, plan, *refs):
    first_ref, refs, errands = take_errands(kinds, refs, 10, 3) if kinds else (refs[0], refs[1:], ())
    proj_ref = first_ref
    before_ref, conv_ref, gain_ref, grad_ref, wu_ref, fresh_ref, out_ref, *refs = refs
    state_ref, inverse_ref, raw_grad_ref, conv_grad_ref, gain_grad_ref, *refs = refs
    rows_buf, grad_buf, state_grad = refs
    step = pl.program_id(1)
    run_errands(errands, plan, step, False)
    steps = pl.num_programs(1)
    wide = heads * HEAD_DIM

    @pl.when((step == 0) & (pl.program_id(0) == 0))
    def _():
        conv_grad_ref[...] = jnp.zeros_like(conv_grad_ref)
        gain_grad_ref[...] = jnp.zeros_like(gain_grad_ref)

    @pl.when(step == 0)
    def _():
        grad_buf[TILE : TILE + 8, :] = jnp.zeros((8, 3 * wide), F32)
        state_grad[...] = jnp.zeros_like(state_grad)

    @pl.when(step > 0)
    def _():
        grad_buf[TILE : TILE + 8, :] = grad_buf[0:8, :]

    first = step == steps - 1
    rows_buf[0:8, :] = jnp.where(first, 0.0, before_ref[:, : 3 * wide])
    rows_buf[8 : 8 + TILE, :] = proj_ref[:, : 3 * wide]
    summed = conv_rows(rows_buf, conv_ref[...])
    smooth = sigmoid(summed)
    active = summed * smooth
    slope = smooth * (1.0 + summed * (1.0 - smooth))
    row, col = tile_masks()
    same = row // SPAN == col // SPAN
    lane = lax.broadcasted_iota(jnp.int32, (TILE, HEAD_DIM), 1)
    beta_grads = jnp.zeros((TILE, HEAD_DIM), F32)
    gain_total = jnp.zeros((1, HEAD_DIM), F32)
    within = same & (row >= col)
    below = same & (row > col)
    every = range(heads)
    at = [slice(head * HEAD_DIM, (head + 1) * HEAD_DIM) for head in every]
    query_raw = [active[:, lo] for lo in at]
    key_raw = [active[:, wide : 2 * wide][:, lo] for lo in at]
    value = [active[:, 2 * wide :][:, lo] for lo in at]
    beta = [sigmoid(proj_ref[:, 4 * wide + head : 4 * wide + head + 1]) for head in every]
    query_scale = [lax.rsqrt(jnp.sum(q * q, -1, keepdims=True) + 1e-06) for q in query_raw]
    key_scale = [lax.rsqrt(jnp.sum(k * k, -1, keepdims=True) + 1e-06) for k in key_raw]
    key = [k * scale for k, scale in zip(key_raw, key_scale)]
    key_s = [split(k) for k in key]
    query_s = [
        split(q * (scale * HEAD_DIM ** (-0.5))) for q, scale in zip(query_raw, query_scale)
    ]
    out_grad_s = []
    for head, lo in enumerate(at):
        gate = proj_ref[:, 3 * wide + head * HEAD_DIM : 3 * wide + (head + 1) * HEAD_DIM]
        grad = grad_ref[:, lo]
        out = out_ref[:, lo]
        scale = lax.rsqrt(jnp.mean(out * out, -1, keepdims=True) + 1e-05)
        gate_s = sigmoid(gate)
        normed = out * scale
        gain_total = gain_total + jnp.sum(grad * normed * (gate * gate_s), 0, keepdims=True)
        gate_grad = grad * normed * gain_ref[...] * (gate_s * (1.0 + gate * (1.0 - gate_s)))
        normed_grad = grad * gain_ref[...] * (gate * gate_s)
        out_grad = scale * normed_grad - out * (
            scale * scale * scale * jnp.mean(out * normed_grad, -1, keepdims=True)
        )
        out_grad_s.append(split(out_grad))
        raw_grad_ref[:, 3 * wide + head * HEAD_DIM : 3 * wide + (head + 1) * HEAD_DIM] = (
            gate_grad.astype(BF16)
        )
    fresh_s = [split(fresh_ref[:, lo]) for lo in at]
    both_s = [split(wu_ref[:, 2 * head * HEAD_DIM : 2 * (head + 1) * HEAD_DIM]) for head in every]
    weights_s = [(high[:, :HEAD_DIM], low[:, :HEAD_DIM]) for high, low in both_s]
    scores_s = [
        split(jnp.where(within, product(query_s[h], key_s[h], NT), 0.0)) for h in every
    ]
    fresh_grad_in = [product(scores_s[h], out_grad_s[h], TN) for h in every]
    carry = [state_grad[head] for head in every]
    blocks = TILE // SPAN
    parts = [[None] * blocks for _ in every]
    for block in range(blocks - 1, -1, -1):
        start = block * SPAN
        carry_s = [split(c) for c in carry]
        fresh_grad = [
            fresh_grad_in[h][start : start + SPAN]
            + product(rows_of(key_s[h], start, SPAN), carry_s[h], NN)
            for h in every
        ]
        fresh_grad_s = [split(f) for f in fresh_grad]
        out_rows = [rows_of(out_grad_s[h], start, SPAN) for h in every]
        carry = [
            carry[h]
            + (
                product(rows_of(query_s[h], start, SPAN), out_rows[h], TN)
                - product(rows_of(weights_s[h], start, SPAN), fresh_grad_s[h], TN)
            )
            for h in every
        ]
        for h in every:
            stacked = tuple(
                jnp.concatenate([a, b], 0) for a, b in zip(out_rows[h], fresh_grad_s[h])
            )
            back = product(stacked, split(state_ref[block, h]), NT)
            through = product(rows_of(fresh_s[h], start, SPAN), carry_s[h], NT)
            parts[h][block] = (fresh_grad[h], back[:SPAN], -back[SPAN:], through)
    for h in every:
        state_grad[h] = carry[h]
    scores_grad_s = [
        split(jnp.where(within, product(out_grad_s[h], fresh_s[h], NT), 0.0)) for h in every
    ]
    joined = [
        [jnp.concatenate([part[i] for part in parts[h]], 0) for i in range(4)] for h in every
    ]
    query_grad = [joined[h][1] + product(scores_grad_s[h], key_s[h], NN) for h in every]
    key_grad = [joined[h][3] + product(scores_grad_s[h], query_s[h], TN) for h in every]
    right_grad = [
        product(
            split(inverse_ref[h]),
            split(jnp.concatenate([joined[h][2], joined[h][0]], 1)),
            TN,
        )
        for h in every
    ]
    lower_grad_s = [
        split(jnp.where(below, -product(split(right_grad[h]), both_s[h], NT), 0.0)) for h in every
    ]
    key_beta_grad = [
        right_grad[h][:, :HEAD_DIM] + product(lower_grad_s[h], key_s[h], NN) for h in every
    ]
    key_grad = [
        key_grad[h]
        + product(lower_grad_s[h], split(key[h] * beta[h]), TN)
        + key_beta_grad[h] * beta[h]
        for h in every
    ]
    for h, lo in enumerate(at):
        value_beta_grad = right_grad[h][:, HEAD_DIM:]
        beta_grad = jnp.sum(
            key_beta_grad[h] * key[h] + value_beta_grad * value[h], -1, keepdims=True
        )
        beta_grad = beta_grad * (beta[h] * (1.0 - beta[h]))
        beta_grads = jnp.where(lane == h, beta_grad, beta_grads)
        query_back = unit_back(query_raw[h], query_scale[h], query_grad[h] * HEAD_DIM ** (-0.5))
        key_back = unit_back(key_raw[h], key_scale[h], key_grad[h])
        for index, grad in enumerate((query_back, key_back, value_beta_grad * beta[h])):
            first = index * wide + h * HEAD_DIM
            grad_buf[0:TILE, first : first + HEAD_DIM] = grad * slope[:, first : first + HEAD_DIM]
    raw_grad_ref[:, 4 * wide :] = beta_grads.astype(BF16)
    gain_grad_ref[0:1, :] += gain_total
    taps = conv_ref[...]
    here = grad_buf[0:TILE, :]
    total = taps[3:4] * here
    conv_grad_ref[3:4, :] += jnp.sum(here * rows_buf[8 : 8 + TILE, :], 0, keepdims=True)
    for offset in range(3):
        total = total + taps[offset : offset + 1] * grad_buf[pl.ds(3 - offset, TILE), :]
        conv_grad_ref[offset : offset + 1, :] += jnp.sum(
            here * rows_buf[pl.ds(5 + offset, TILE), :], 0, keepdims=True
        )
    raw_grad_ref[:, : 3 * wide] = total.astype(BF16)
    run_errands(errands, plan, step, True)


def mixer_backward(
    proj, conv, gain, grad, wu, fresh, out, states, inverses, heads,
    errands=(), plan=(), collective_id=None,
):
    rows = proj.shape[0]
    wide = heads * HEAD_DIM
    tiles = SEQ_LEN // TILE
    seqs = rows // SEQ_LEN
    blocks = TILE // SPAN

    def index(seq, step):
        return seq * tiles + tiles - 1 - step

    def at(seq, step):
        return (index(seq, step), 0)

    def ahead(seq, step):
        return (jnp.maximum(index(seq, step) * (TILE // 8) - 1, 0), 0)

    def fixed(seq, step):
        return (0, 0)

    kinds, sources, specs, shapes, scratch = errand_operands(errands)
    return pl.pallas_call(
        functools.partial(mixer_backward_body, heads, kinds, plan),
        grid=(seqs, tiles),
        in_specs=[
            pl.BlockSpec((TILE, proj.shape[1]), at),
            pl.BlockSpec((8, proj.shape[1]), ahead),
            pl.BlockSpec(conv.shape, fixed),
            pl.BlockSpec(gain.shape, fixed),
            pl.BlockSpec((TILE, wide), at),
            pl.BlockSpec((TILE, 2 * wide), at),
            pl.BlockSpec((TILE, wide), at),
            pl.BlockSpec((TILE, wide), at),
            pl.BlockSpec(
                (blocks, heads, HEAD_DIM, HEAD_DIM), lambda s, t: (index(s, t), 0, 0, 0)
            ),
            pl.BlockSpec((None, heads, TILE, TILE), lambda s, t: (index(s, t), 0, 0, 0)),
            *specs,
        ],
        out_specs=[
            pl.BlockSpec((TILE, 4 * wide + 128), at),
            pl.BlockSpec((8, 3 * wide), fixed),
            pl.BlockSpec((8, HEAD_DIM), fixed),
            *specs,
        ],
        out_shape=[
            jax.ShapeDtypeStruct((rows, 4 * wide + 128), BF16),
            jax.ShapeDtypeStruct((8, 3 * wide), F32),
            jax.ShapeDtypeStruct((8, HEAD_DIM), F32),
            *shapes,
        ],
        scratch_shapes=[
            pltpu.VMEM((TILE + 8, 3 * wide), F32),
            pltpu.VMEM((TILE + 8, 3 * wide), F32),
            pltpu.VMEM((heads, HEAD_DIM, HEAD_DIM), F32),
            *scratch,
        ],
        compiler_params=mixer_params(errands, collective_id),
        name="mixer_backward",
    )(proj, proj, conv, gain, grad, wu, fresh, out, states, inverses, *sources)


MESH = pl.DeviceIdType.MESH


def place():
    return lax.axis_index("core"), lax.axis_index("zl"), lax.axis_index("x")


def slot_of(core, deep, wide):
    own_core, own_deep, own_wide = place()
    return (
        jnp.where(core, 1 - own_core, own_core) * 4
        + jnp.where(deep, 1 - own_deep, own_deep) * 2
        + jnp.where(wide, 1 - own_wide, own_wide)
    )


def is_moved():
    return lax.axis_index("core") != lax.axis_index("zh")


def greet(everyone=False):
    barrier = pltpu.get_barrier_semaphore()
    axes = ("core", "zl", "x", "y", "zh") if everyone else ("core", "zl", "x")
    for axis in axes:
        pl.semaphore_signal(barrier, inc=1, device_id=neighbour(axis), device_id_type=MESH)
    peers = len(axes)
    if everyone:
        pl.when(is_moved())(
            lambda: pl.semaphore_signal(
                barrier, inc=1, device_id=partner(), device_id_type=MESH
            )
        )
        peers = peers + is_moved().astype(jnp.int32)
    pl.semaphore_wait(barrier, peers)


def partner():
    return {"core": lax.axis_index("zh"), "zh": lax.axis_index("core")}


def row_half(ref, index):
    rows = ref.shape[0] // 2
    return ref.at[pl.ds(pl.multiple_of(index * rows, 16), rows)]


class Errand:
    sems = 1
    buffers = 1

    def __init__(self, source, target, send, recv, local, buffers=()):
        self.source, self.target, self.held = source, target, buffers
        self.stage = buffers[0] if buffers else None
        self.send, self.recv, self.local = send, recv, local
        self.y = lax.axis_index("y")

    def remote(self, index, source, target, device):
        return pltpu.make_async_remote_copy(
            src_ref=source, dst_ref=target, send_sem=self.send.at[index],
            recv_sem=self.recv.at[index], device_id=device, device_id_type=MESH,
        )

    @staticmethod
    def buffer_shape(shape):
        return shape

    def stays(self, action):
        pl.when(jnp.logical_not(is_moved()))(action)

    def own_target(self):
        return self.target

    def here(self):
        source = self.source if self.stage is None else self.stage
        return pltpu.make_async_copy(source, self.own_target(), self.local)

    def stage_in(self):
        return pltpu.make_async_copy(self.source, self.stage, self.local)

    def start_here(self):
        self.stays(lambda: (self.here() if self.stage is None else self.stage_in()).start())

    def pass_here(self):
        def action():
            self.stage_in().wait()
            self.here().start()

        if self.stage is not None:
            self.stays(action)

    def finish_here(self):
        self.stays(lambda: self.here().wait())


class Exchange(Errand):
    def far(self):
        return self.remote(0, self.source, self.target, partner())

    def start(self):
        pl.when(is_moved())(lambda: self.far().start())
        self.start_here()

    def middle(self):
        self.pass_here()

    def finish(self):
        pl.when(is_moved())(lambda: self.far().wait())
        self.finish_here()


class Swap(Errand):
    sems = 4

    def piece(self, ref, owner, index):
        rows = ref.shape[0] // 4
        return ref.at[pl.ds(pl.multiple_of((owner * 2 + index) * rows, 16), rows)]

    def first(self, index):
        return self.remote(
            index, self.piece(self.source, self.y, index), self.piece(self.target, self.y, index),
            partner(),
        )

    def second(self, index, landing=False):
        half = self.piece(self.target, 1 - self.y if landing else self.y, index)
        return self.remote(2 + index, half, half, neighbour("y"))

    def start(self):
        @pl.when(is_moved())
        def _():
            self.first(0).start()
            self.first(1).start()

        self.start_here()

    def pass_piece(self, index):
        @pl.when(is_moved())
        def _():
            self.first(index).wait_recv()
            self.second(index).start()

    def early(self):
        self.pass_piece(0)
        self.pass_here()

    def late(self):
        self.pass_piece(1)

    def middle(self):
        self.early()
        self.late()

    def finish(self):
        @pl.when(is_moved())
        def _():
            for index in range(2):
                self.first(index).wait_send()
                self.second(index).wait_send()
                self.second(index, True).wait_recv()

        self.finish_here()


class HalfOverY(Errand):
    buffers = 0

    def copy(self):
        return self.remote(0, row_half(self.source, 1 - self.y), self.target, neighbour("y"))

    def start(self):
        self.copy().start()

    def middle(self):
        pass

    def finish(self):
        self.copy().wait()


class Across(Errand):
    buffers = 0

    def copy(self):
        return self.remote(0, self.source, self.target, neighbour("zh"))

    def start(self):
        pl.when(is_moved())(lambda: self.copy().start())

    def middle(self):
        pass

    def finish(self):
        pl.when(is_moved())(lambda: self.copy().wait_send())
        self.stays(lambda: self.copy().wait_recv())


SCATTER_CUT = 192


class Gather(Errand):
    sems = 11

    def ring(self):
        return Ring(self.target, self.send, self.recv, 32, self.stage)

    def own(self):
        return pltpu.make_async_copy(self.stage, self.target.at[slot_of(0, 0, 0)], self.local)

    def start(self):
        self.stage_in().start()
        self.stage_in().wait()
        self.own().start()
        self.ring().launch(0, 1, 2, 3, 4)

    def early(self):
        ring = self.ring()
        ring.arrived(0)
        ring.launch(5)
        ring.arrived(1)
        ring.launch(6)

    def middle(self):
        ring = self.ring()
        ring.arrived(2)
        ring.launch(7)
        ring.arrived(3)
        ring.launch(8)

    def late(self):
        ring = self.ring()
        ring.arrived(5)
        ring.launch(9)
        ring.arrived(6)
        ring.launch(10)

    def finish(self):
        ring = self.ring()
        ring.arrived(4, 7, 8, 9, 10)
        ring.finish()
        self.own().wait()


class Spread(Errand):
    sems = 3

    def own_target(self):
        return row_half(self.target, self.y)

    def over(self):
        return self.remote(0, self.source, self.own_target(), neighbour("y"))

    def other(self, index, axis):
        view = row_half(self.target, 1 - self.y)
        return self.remote(index, view, view, neighbour(axis))

    def cross(self):
        return self.remote(1, self.source, self.own_target(), neighbour("core"))

    def start(self):
        @pl.when(jnp.logical_not(is_moved()))
        def _():
            self.over().start()
            self.cross().start()

        self.start_here()

    def middle(self):
        @pl.when(jnp.logical_not(is_moved()))
        def _():
            self.other(0, "y").wait_recv()
            self.other(2, "core").start()

        self.pass_here()

    def finish(self):
        @pl.when(jnp.logical_not(is_moved()))
        def _():
            self.over().wait_send()
            self.cross().wait_send()
            self.other(2, "core").wait_send()

        @pl.when(is_moved())
        def _():
            self.cross().wait_recv()
            self.other(2, "core").wait_recv()

        self.finish_here()


class Chain(Errand):
    sems = 5
    buffers = 2

    def mine(self):
        return self.held[0]

    def load(self):
        return pltpu.make_async_copy(self.source, self.mine(), self.local)

    def across(self):
        return self.remote(0, self.mine(), self.held[1], neighbour("zh"))

    def own_rows(self):
        return row_half(self.target, self.y)

    def near(self):
        return pltpu.make_async_copy(self.mine(), self.own_rows(), self.local)

    def over(self):
        return self.remote(1, self.mine(), self.own_rows(), neighbour("y"))

    def cross(self):
        return self.remote(2, self.mine(), self.own_rows(), neighbour("core"))

    def other(self, index, axis):
        view = row_half(self.target, 1 - self.y)
        return self.remote(index, view, view, neighbour(axis))

    def add(self, more):
        mine = self.mine()
        mine[...] = (mine[...].astype(F32) + more[...].astype(F32)).astype(BF16)

    def start(self):
        self.load().start()

    def launch(self):
        self.load().wait()
        pl.when(is_moved())(lambda: self.across().start())

    def settle(self):
        @pl.when(jnp.logical_not(is_moved()))
        def _():
            self.across().wait_recv()
            self.add(self.held[1])
            self.over().start()
            self.cross().start()
            self.near().start()

    def settle_late(self):
        self.settle()

    def forward(self):
        @pl.when(jnp.logical_not(is_moved()))
        def _():
            self.other(1, "y").wait_recv()
            self.other(3, "core").start()

    def finish(self):
        @pl.when(jnp.logical_not(is_moved()))
        def _():
            self.near().wait()
            self.over().wait_send()
            self.cross().wait_send()
            self.other(3, "core").wait_send()

        @pl.when(is_moved())
        def _():
            self.across().wait_send()
            self.cross().wait_recv()
            self.other(3, "core").wait_recv()


class FullChain(Chain):
    buffers = 3

    @staticmethod
    def buffer_shape(shape):
        return (shape[0] // 2, *shape[1:])

    def load(self):
        return pltpu.make_async_copy(row_half(self.source, self.y), self.mine(), self.local)

    def halves(self):
        return self.remote(4, row_half(self.source, 1 - self.y), self.held[2], neighbour("y"))

    def start(self):
        self.halves().start()
        self.load().start()

    def launch(self):
        self.load().wait()
        self.halves().wait()
        self.add(self.held[2])
        pl.when(is_moved())(lambda: self.across().start())


def errand_target(kind, source):
    if kind is Gather:
        return jax.ShapeDtypeStruct((8, *source.shape), source.dtype)
    rows = source.shape[0]
    rows = {HalfOverY: rows // 2, Spread: 2 * rows, Chain: 2 * rows}.get(kind, rows)
    return jax.ShapeDtypeStruct((rows, *source.shape[1:]), source.dtype)


def errand_scratch(kinds, sources=()):
    total = max(1, sum(kind.sems for kind in kinds))
    places = [
        pltpu.VMEM(kind.buffer_shape(source.shape), BF16)
        for kind, source in zip(kinds, sources)
        for _ in range(kind.buffers)
    ]
    return [
        *places,
        pltpu.SemaphoreType.DMA((total,)),
        pltpu.SemaphoreType.DMA((total,)),
        pltpu.SemaphoreType.DMA((max(1, len(kinds)),)),
    ]


def make_errands(kinds, sources, targets, send, recv, local, places=()):
    made, at, used = [], 0, 0
    for index, (kind, source, target) in enumerate(zip(kinds, sources, targets)):
        view = pl.ds(at, kind.sems)
        held = places[used : used + kind.buffers] if places else ()
        made.append(kind(source, target, send.at[view], recv.at[view], local.at[index], held))
        at += kind.sems
        used += kind.buffers
    return made


def neighbour(axis):
    return {axis: 1 - lax.axis_index(axis)}


def column_tile(columns):
    for size in (512, 384, 256, 128):
        if columns % size == 0:
            return size
    return columns


def column_parts(columns):
    tile = column_tile(columns)
    if tile != columns or columns <= 512:
        return [(0, tile, columns // tile)]
    whole = columns // 256 * 256
    return [(0, 256, whole // 256), (whole, columns - whole, 1)]


def by_columns(columns, body):
    for start, size, steps in column_parts(columns):
        if steps == 1:
            body(pl.ds(start, size))
        else:

            def column(step, _, start=start, size=size):
                body(pl.ds(pl.multiple_of(start + step * size, 128), size))
                return 0

            lax.fori_loop(0, steps, column, 0)


def take_errands(kinds, refs, inputs, outputs):
    extra = len(kinds)
    sources = refs[inputs : inputs + extra]
    targets = refs[inputs + extra + outputs : inputs + 2 * extra + outputs]
    last = len(refs) - 3 - sum(kind.buffers for kind in kinds)
    errands = make_errands(kinds, sources, targets, *refs[-3:], refs[last:-3])
    rest = (
        *refs[:inputs], *refs[inputs + extra : inputs + extra + outputs],
        *refs[inputs + 2 * extra + outputs : last],
    )
    return rest[0], rest[1:], errands


class Ring:
    def __init__(self, held, send, recv, cut=None, block=None):
        self.block = block
        self.held, self.send, self.recv = held, send, recv
        own, wide, deep, far = (slot_of(0, *at) for at in ((0, 0), (0, 1), (1, 0), (1, 1)))
        rows = held.shape[1]
        cut = cut or rows // 2
        rest = rows - cut
        self.moves = (
            ("x", own, wide, 0, cut), ("zl", own, deep, cut, rest),
            ("x", own, wide, cut, rest), ("zl", own, deep, 0, cut),
            ("core", own, slot_of(1, 0, 0), 0, rows),
            ("zl", wide, far, 0, cut), ("x", deep, far, cut, rest),
            ("core", wide, slot_of(1, 0, 1), 0, rows),
            ("core", deep, slot_of(1, 1, 0), 0, rows),
            ("core", far, slot_of(1, 1, 1), 0, cut),
            ("core", far, slot_of(1, 1, 1), cut, rest),
        )

    def move(self, index, landing=False):
        axis, source, target, start, size = self.moves[index]
        view = self.held.at[target if landing else source, pl.ds(start, size)]
        from_block = self.block is not None and index < 5
        return pltpu.make_async_remote_copy(
            src_ref=self.block.at[pl.ds(start, size)] if from_block else view,
            dst_ref=view, send_sem=self.send.at[index],
            recv_sem=self.recv.at[index], device_id=neighbour(axis), device_id_type=MESH,
        )

    def launch(self, *indices):
        for index in indices:
            self.move(index).start()

    def arrived(self, *indices):
        for index in indices:
            self.move(index, True).wait_recv()

    def run(self, work, beside):
        self.launch(0, 1, 2, 3, 4)
        beside(0)
        work(slot_of(0, 0, 0))
        self.arrived(4)
        work(slot_of(1, 0, 0))
        beside(1)
        self.arrived(0)
        self.launch(5)
        self.arrived(1)
        self.launch(6)
        self.arrived(2)
        self.launch(7)
        self.arrived(3)
        self.launch(8)
        work(slot_of(0, 0, 1))
        work(slot_of(0, 1, 0))
        self.arrived(7)
        work(slot_of(1, 0, 1))
        self.arrived(8)
        work(slot_of(1, 1, 0))
        beside(2)
        self.arrived(5)
        self.launch(9)
        self.arrived(6)
        self.launch(10)
        work(slot_of(0, 1, 1))
        self.arrived(9, 10)
        work(slot_of(1, 1, 1))

    def finish(self):
        for index in range(len(self.moves)):
            self.move(index).wait_send()


def ring_scratch(rows, depth):
    return [
        pltpu.VMEM((8, rows, depth), BF16),
        pltpu.SemaphoreType.DMA((11,)),
        pltpu.SemaphoreType.DMA((11,)),
    ]


class Stores:
    def __init__(self, sems):
        self.sems, self.made = sems, []

    def add(self, source, target):
        copy = pltpu.make_async_copy(source, target, self.sems.at[len(self.made)])
        copy.start()
        self.made.append(copy)

    def finish(self):
        for copy in self.made:
            copy.wait()


def run_beside(errands, starts, middles):
    def beside(point):
        for errand in errands:
            if point == starts:
                errand.start()
            if point == middles:
                errand.middle()

    return beside


def gather_body(dims, count, kinds, *refs):
    block_ref, refs, errands = take_errands(kinds, refs, 1 + count, 1 + count)
    weight_refs, gathered_ref, product_refs = refs[:count], refs[count], refs[count + 1 : 2 * count + 1]
    held, send, recv = refs[2 * count + 1 : 2 * count + 4]
    weights, results = refs[2 * count + 4 : 3 * count + 4], refs[3 * count + 4 : 4 * count + 4]
    (local,) = refs[4 * count + 4 :]
    own = slot_of(0, 0, 0)
    loads = [pltpu.make_async_copy(block_ref, held.at[own], local.at[0])]
    for i, (ref, weight) in enumerate(zip(weight_refs, weights)):
        loads.append(pltpu.make_async_copy(ref, weight, local.at[1 + i]))
    for load in loads:
        load.start()
    greet(bool(kinds))
    for load in loads:
        load.wait()
    ring = Ring(held, send, recv, None)
    stores = Stores(local.at[pl.ds(1 + count, 8 * (1 + count))])

    def work(slot):
        stores.add(held.at[slot], gathered_ref.at[slot])
        for weight, result, product_ref in zip(weights, results, product_refs):

            def column(at):
                right = weight[:, at] if dims == NN else weight[at, :]
                result[slot, :, at] = dot(held[slot], right, dims).astype(result.dtype)

            by_columns(result.shape[2], column)
            stores.add(result.at[slot], product_ref.at[slot])

    ring.run(work, run_beside(errands, 0, 2))
    ring.finish()
    stores.finish()
    for errand in errands:
        errand.finish()


def gather_multiply(block, weights, dims, collective_id, name, errands=(), out_type=F32):
    rows, depth = block.shape
    widths = [w.shape[1] if dims == NN else w.shape[0] for w in weights]
    count = len(weights)
    kinds, sources = [e[0] for e in errands], [e[1] for e in errands]
    gathered, *products = pl.pallas_call(
        functools.partial(gather_body, dims, count, kinds),
        in_specs=[pl.BlockSpec(memory_space=pl.ANY)] * (1 + count + len(kinds)),
        out_specs=[pl.BlockSpec(memory_space=pl.ANY)] * (1 + count + len(kinds)),
        out_shape=[jax.ShapeDtypeStruct((8, rows, depth), BF16)]
        + [jax.ShapeDtypeStruct((8, rows, width), out_type) for width in widths]
        + [errand_target(*errand) for errand in errands],
        scratch_shapes=ring_scratch(rows, depth)
        + [pltpu.VMEM(w.shape, BF16) for w in weights]
        + [pltpu.VMEM((8, rows, width), out_type) for width in widths]
        + [
            pltpu.SemaphoreType.DMA((1 + count + 8 * (1 + count),)),
            *errand_scratch(kinds, sources),
        ],
        compiler_params=pltpu.CompilerParams(
            collective_id=collective_id, has_side_effects=True, vmem_limit_bytes=56 * 2**20
        ),
        name=name,
    )(block, *weights, *sources)
    flat = [v.reshape(8 * rows, v.shape[2]) for v in (gathered, *products[:count])]
    return (*flat, *products[count:])


def feed_body(kinds, *refs):
    block_ref, refs, errands = take_errands(kinds, refs, 5, 4)
    sources, refs = refs[:4], refs[4:]
    gathered_ref, hidden_ref, gate_grad_ref, up_grad_ref, *refs = refs
    held, send, recv, w_gate, w_up, w_down, grads, hidden_grad, hidden, gate_grad, up_grad = refs[:11]
    (local,) = refs[11:]
    own = slot_of(0, 0, 0)
    loads = [pltpu.make_async_copy(block_ref, held.at[own], local.at[0])]
    for i, (source, target) in enumerate(zip(sources, (w_gate, w_up, w_down, grads))):
        loads.append(pltpu.make_async_copy(source, target, local.at[1 + i]))
    for load in loads:
        load.start()
    greet(bool(kinds))
    for load in loads:
        load.wait()
    ring = Ring(held, send, recv)
    stores = Stores(local.at[pl.ds(5, 32)])
    units = hidden.shape[2]

    def back(slot):
        def column(at):
            hidden_grad[slot, :, at] = dot(grads[slot], w_down[at, :], NT)

        by_columns(units, column)

    def work(slot):
        stores.add(held.at[slot], gathered_ref.at[slot])

        def column(at):
            gate = dot(held[slot], w_gate[at, :], NT)
            up = dot(held[slot], w_up[at, :], NT)
            smooth = sigmoid(gate)
            active = gate * smooth
            grad = hidden_grad[slot, :, at]
            hidden[slot, :, at] = (active * up).astype(BF16)
            gate_grad[slot, :, at] = (grad * up * smooth * (1.0 + gate * (1.0 - smooth))).astype(BF16)
            up_grad[slot, :, at] = (grad * active).astype(BF16)

        by_columns(units, column)
        stores.add(hidden.at[slot], hidden_ref.at[slot])
        stores.add(gate_grad.at[slot], gate_grad_ref.at[slot])
        stores.add(up_grad.at[slot], up_grad_ref.at[slot])

    def beside(point):
        for errand in errands:
            if point == 0:
                errand.start()
            elif point == 2:
                errand.middle()
        if point == 0:
            back(slot_of(0, 0, 0))
            back(slot_of(1, 0, 0))
        elif point == 1:
            for at in ((0, 0, 1), (0, 1, 0), (1, 0, 1), (1, 1, 0), (0, 1, 1), (1, 1, 1)):
                back(slot_of(*at))

    ring.run(work, beside)
    ring.finish()
    stores.finish()
    for errand in errands:
        errand.finish()


def feed(block, w_gate, w_up, w_down, grads, collective_id, errands=()):
    rows, depth = block.shape
    units = w_gate.shape[0]
    kinds, sources = [e[0] for e in errands], [e[1] for e in errands]
    hbm = pl.BlockSpec(memory_space=pl.ANY)
    by_unit = jax.ShapeDtypeStruct((8, rows, units), BF16)
    gathered, *parts = pl.pallas_call(
        functools.partial(feed_body, kinds),
        in_specs=[hbm] * (5 + len(kinds)),
        out_specs=[hbm] * (4 + len(kinds)),
        out_shape=[jax.ShapeDtypeStruct((8, rows, depth), BF16), by_unit, by_unit, by_unit]
        + [errand_target(*errand) for errand in errands],
        scratch_shapes=[
            *ring_scratch(rows, depth),
            *[pltpu.VMEM(w_gate.shape, BF16)] * 3,
            pltpu.VMEM((8, rows, depth), BF16),
            pltpu.VMEM((8, rows, units), F32),
            *[pltpu.VMEM((8, rows, units), BF16)] * 3,
            pltpu.SemaphoreType.DMA((37,)),
            *errand_scratch(kinds, sources),
        ],
        compiler_params=pltpu.CompilerParams(
            collective_id=collective_id, has_side_effects=True, vmem_limit_bytes=58 * 2**20
        ),
        name="feed",
    )(block, w_gate, w_up, w_down, grads, *sources)
    flat = [v.reshape(8 * rows, v.shape[2]) for v in (gathered, *parts[:3])]
    return (*flat, *parts[3:])


def block_of(ref, slot, rows):
    if len(ref.shape) == 3:
        return ref[slot]
    return ref[pl.ds(pl.multiple_of(slot * rows, rows), rows)]


def scatter_core(dims, lefts, weights, buffers, beside, cut=None):
    sending, crossing, partial, far_recv, side_recv, total, send, recv = buffers
    rows, width = total.shape
    cut = cut or rows // 2

    def move(index, axis, src, dst):
        return pltpu.make_async_remote_copy(
            src_ref=src, dst_ref=dst, send_sem=send.at[index], recv_sem=recv.at[index],
            device_id=neighbour(axis), device_id_type=MESH,
        )

    sends = []

    def launch(*args):
        copy = move(*args)
        copy.start()
        sends.append(copy)

    def multiply(slot, write):
        def column(at):
            value = None
            for left, weight in zip(lefts, weights):
                right = weight[:, at] if dims == NN else weight[at, :]
                term = dot(block_of(left, slot, rows), right, dims)
                value = term if value is None else value + term
            write(at, value)

        by_columns(width, column)

    places = ((1, 1), (0, 1), (1, 0), (0, 0))

    def cross(index):
        def write(at, value):
            sending[index, :, at] = value.astype(BF16)

        multiply(slot_of(1, *places[index]), write)
        launch(index, "core", sending.at[index], crossing.at[index])

    def crossed(index):
        move(index, "core", sending.at[index], crossing.at[index]).wait_recv()

    def local_sum(index):
        crossed(index)

        def write(at, value):
            partial[index, :, at] = (value + crossing[index, :, at].astype(F32)).astype(BF16)

        multiply(slot_of(0, *places[index]), write)

    first, second = pl.ds(0, cut), pl.ds(cut, rows - cut)
    cross(0)
    beside(0)
    cross(1)
    local_sum(0)
    launch(4, "x", partial.at[0, first], far_recv.at[0, first])
    launch(5, "zl", partial.at[0, second], far_recv.at[1, second])
    beside("far sent")
    cross(2)
    local_sum(1)
    launch(6, "x", partial.at[1, first], side_recv.at[0, first])
    local_sum(2)
    launch(7, "zl", partial.at[2, second], side_recv.at[1, second])
    beside("side sent")
    cross(3)
    beside(1)
    move(4, "x", partial.at[0, first], far_recv.at[0, first]).wait_recv()
    partial[2, first] = (partial[2, first].astype(F32) + far_recv[0, first].astype(F32)).astype(BF16)
    launch(8, "zl", partial.at[2, first], side_recv.at[1, first])
    move(5, "zl", partial.at[0, second], far_recv.at[1, second]).wait_recv()
    partial[1, second] = (partial[1, second].astype(F32) + far_recv[1, second].astype(F32)).astype(BF16)
    launch(9, "x", partial.at[1, second], side_recv.at[0, second])
    beside(2)
    crossed(3)

    def write(at, value):
        total[:, at] = value + crossing[3, :, at].astype(F32)

    multiply(slot_of(0, 0, 0), write)
    move(6, "x", partial.at[1, first], side_recv.at[0, first]).wait_recv()
    total[first] += side_recv[0, first].astype(F32)
    move(7, "zl", partial.at[2, second], side_recv.at[1, second]).wait_recv()
    total[second] += side_recv[1, second].astype(F32)
    beside(3)
    move(8, "zl", partial.at[2, first], side_recv.at[1, first]).wait_recv()
    total[first] += side_recv[1, first].astype(F32)
    move(9, "x", partial.at[1, second], side_recv.at[0, second]).wait_recv()
    total[second] += side_recv[0, second].astype(F32)
    return sends


def scatter_scratch(rows, width):
    return [
        pltpu.VMEM((4, rows, width), BF16),
        pltpu.VMEM((4, rows, width), BF16),
        pltpu.VMEM((3, rows, width), BF16),
        pltpu.VMEM((2, rows, width), BF16),
        pltpu.VMEM((2, rows, width), BF16),
        pltpu.VMEM((rows, width), F32),
        pltpu.SemaphoreType.DMA((10,)),
        pltpu.SemaphoreType.DMA((10,)),
    ]


def scatter_body(dims, count, kinds, *refs):
    first_ref, refs, errands = take_errands(kinds, refs, 2 * count, 1)
    refs = (first_ref, *refs)
    total_ref = refs[2 * count]
    operands = refs[2 * count + 1 : 4 * count + 1]
    buffers, local = refs[4 * count + 1 : -1], refs[-1]
    loads = [
        pltpu.make_async_copy(ref, operand, local.at[i])
        for i, (ref, operand) in enumerate(zip(refs[: 2 * count], operands))
    ]
    for load in loads:
        load.start()
    greet(bool(kinds))
    for load in loads:
        load.wait()

    def beside(point):
        for errand in errands:
            if point == 0:
                errand.start()
            elif point == 2 and hasattr(errand, "early"):
                errand.early()
            elif point == 3:
                errand.late() if hasattr(errand, "early") else errand.middle()

    cut = SCATTER_CUT if Across in kinds or Swap in kinds else None
    sends = scatter_core(dims, operands[:count], operands[count:], buffers, beside, cut)
    store = pltpu.make_async_copy(buffers[5], total_ref, local.at[2 * count])
    store.start()
    for copy in sends:
        copy.wait_send()
    store.wait()
    for errand in errands:
        errand.finish()


def multiply_scatter(lefts, weights, dims, collective_id, name, errands=()):
    rows = lefts[0].shape[0] // 8
    width = weights[0].shape[1] if dims == NN else weights[0].shape[0]
    count = len(lefts)
    lefts = [left.reshape(8, rows, left.shape[1]) for left in lefts]
    kinds, sources = [e[0] for e in errands], [e[1] for e in errands]
    return pl.pallas_call(
        functools.partial(scatter_body, dims, count, kinds),
        in_specs=[pl.BlockSpec(memory_space=pl.ANY)] * (2 * count + len(kinds)),
        out_specs=[pl.BlockSpec(memory_space=pl.ANY)] * (1 + len(kinds)),
        out_shape=[jax.ShapeDtypeStruct((rows, width), F32)]
        + [errand_target(*errand) for errand in errands],
        scratch_shapes=[pltpu.VMEM(v.shape, BF16) for v in (*lefts, *weights)]
        + [
            *scatter_scratch(rows, width),
            pltpu.SemaphoreType.DMA((2 * count + 1,)),
            *errand_scratch(kinds, sources),
        ],
        compiler_params=pltpu.CompilerParams(
            collective_id=collective_id, has_side_effects=True, vmem_limit_bytes=56 * 2**20
        ),
        name=name,
    )(*lefts, *weights, *sources)


def begin_body(kinds, *refs):
    tokens_ref, refs, errands = take_errands(kinds, refs, 8, 5)
    gain_ref, conv_ref, *refs = refs
    weight_refs, refs = refs[:5], refs[5:]
    moved_ref, gathered_ref, product_ref, weights_ref, new_conv_ref, *refs = refs
    tokens, held, weights, result, send, recv, errand_send, errand_recv, local = refs
    rows = tokens_ref.shape[0]
    half = rows // 2
    starts = [0]
    for ref in weight_refs:
        starts.append(starts[-1] + ref.shape[1])
    parts = [pl.ds(start, ref.shape[1]) for start, ref in zip(starts, weight_refs)]
    greet(True)
    own_kinds = [Exchange, Exchange] + [Swap] * 5
    targets = [tokens, new_conv_ref] + [weights.at[:, part] for part in parts]
    block, taps, *swaps = make_errands(
        own_kinds, [tokens_ref, conv_ref, *weight_refs], targets, errand_send, errand_recv, local
    )
    block.start()
    taps.start()
    swaps[0].start()
    block.finish()
    for swap in swaps[1:]:
        swap.start()
    for errand in errands:
        errand.start()
    own = slot_of(0, 0, 0)
    values = tokens[...].astype(F32)
    scale = lax.rsqrt(jnp.mean(values * values, -1, keepdims=True) + 1e-05)
    held[own] = (values * scale * gain_ref[...]).astype(BF16)
    keep = pltpu.make_async_copy(tokens, moved_ref, local.at[7])
    keep.start()

    ring = Ring(held, send, recv)
    ring.launch(0, 1, 2, 3, 4)
    ring.arrived(0)
    ring.launch(5)
    ring.arrived(1)
    ring.launch(6)
    swaps[0].middle()
    ring.arrived(2)
    ring.launch(7)
    ring.arrived(3)
    ring.launch(8)
    swaps[1].middle()
    ring.arrived(5)
    ring.launch(9)
    ring.arrived(6)
    ring.launch(10)
    ring.arrived(4, 7, 8, 9, 10)
    store = pltpu.make_async_copy(held, gathered_ref, local.at[8])
    store.start()
    stores = []
    for index, (swap, part) in enumerate(zip(swaps, parts)):
        if index + 2 < len(swaps):
            swaps[index + 2].middle()
        swap.finish()
        if index == len(swaps) - 1:
            for errand in errands:
                errand.middle()

        def multiply(slot, _, part=part):
            result[slot, :, part] = dot(held[slot], weights[:, part], NN)
            return 0

        lax.fori_loop(0, 8, multiply, 0)
        for view, out, sem in (
            (result.at[:, :, part], product_ref.at[:, :, part], 9 + 2 * index),
            (weights.at[:, part], weights_ref.at[:, part], 10 + 2 * index),
        ):
            copy = pltpu.make_async_copy(view, out, local.at[sem])
            copy.start()
            stores.append(copy)
    taps.finish()
    ring.finish()
    keep.wait()
    store.wait()
    for copy in stores:
        copy.wait()
    for errand in errands:
        errand.finish()


def begin(tokens, gain, conv, weights, collective_id, errands=()):
    rows, depth = tokens.shape
    width = sum(w.shape[1] for w in weights)
    kinds, sources = [e[0] for e in errands], [e[1] for e in errands]
    hbm = pl.BlockSpec(memory_space=pl.ANY)
    moved, gathered, product, weights, conv, *more = pl.pallas_call(
        functools.partial(begin_body, kinds),
        in_specs=[hbm, pl.BlockSpec(memory_space=pltpu.VMEM)]
        + [hbm] * (1 + len(weights) + len(kinds)),
        out_specs=[hbm] * (5 + len(kinds)),
        out_shape=[
            jax.ShapeDtypeStruct(tokens.shape, BF16),
            jax.ShapeDtypeStruct((8, rows, depth), BF16),
            jax.ShapeDtypeStruct((8, rows, width), F32),
            jax.ShapeDtypeStruct((depth, width), BF16),
            jax.ShapeDtypeStruct(conv.shape, conv.dtype),
            *[errand_target(*errand) for errand in errands],
        ],
        scratch_shapes=[
            pltpu.VMEM((rows, depth), BF16),
            pltpu.VMEM((8, rows, depth), BF16),
            pltpu.VMEM((depth, width), BF16),
            pltpu.VMEM((8, rows, width), F32),
            pltpu.SemaphoreType.DMA((11,)),
            pltpu.SemaphoreType.DMA((11,)),
            pltpu.SemaphoreType.DMA((22,)),
            pltpu.SemaphoreType.DMA((22,)),
            pltpu.SemaphoreType.DMA((19,)),
            *errand_scratch(kinds, sources),
        ],
        compiler_params=pltpu.CompilerParams(
            collective_id=collective_id, has_side_effects=True, vmem_limit_bytes=56 * 2**20
        ),
        name="begin",
    )(tokens, gain, conv, *weights, *sources)
    flat = gathered.reshape(8 * rows, depth), product.reshape(8 * rows, width)
    return (moved, *flat, weights, conv, *more)


def turned_product(turned, right, out, columns):
    def column(at):
        out[:, at] = dot(turned[...], right[:, at], NN).astype(BF16)

    by_columns(columns, column)


def mlp_body(kinds, *refs):
    first_ref, refs, errands = take_errands(kinds, refs, 6, 5)
    sources, refs = (first_ref, *refs[:5]), refs[5:]
    total_ref, down_ref, gate_ref, up_ref, came_ref, *refs = refs
    hidden, weight, rights, lefts, turned, outs = refs[:6]
    buffers, refs = refs[6:14], refs[14:]
    half_send, half_recv, local = refs
    hidden_ref, weight_ref, grads_ref, gate_grad_ref, up_grad_ref, rows_ref = sources

    def load(source, target, index):
        return pltpu.make_async_copy(source, target, local.at[index])

    early = [
        load(hidden_ref, hidden, 0), load(weight_ref, weight, 1), load(grads_ref, rights, 2),
        load(gate_grad_ref, lefts.at[0], 3), load(up_grad_ref, lefts.at[1], 4),
    ]
    reload = load(rows_ref, rights, 5)
    for copy in early:
        copy.start()
    greet(True)
    for copy in early:
        copy.wait()
    stores = Stores(local.at[pl.ds(6, 4)])
    rows = hidden.shape[1]
    columns = rights.shape[1]

    def turn(left):
        for slot in range(8):
            turned[:, slot * rows : (slot + 1) * rows] = left[slot].T

    y = lax.axis_index("y")
    half = pltpu.make_async_remote_copy(
        src_ref=row_half(outs.at[0], 1 - y), dst_ref=came_ref, send_sem=half_send.at[0],
        recv_sem=half_recv.at[0], device_id=neighbour("y"), device_id_type=MESH,
    )

    def beside(point):
        if point == 0:
            for errand in errands:
                errand.start()
        elif point == "side sent":
            turn(hidden)
            turned_product(turned, rights, outs.at[0], columns)
            reload.start()
            half.start()
            stores.add(outs.at[0], down_ref)
        elif point == 2:
            turn(lefts.at[0])
            reload.wait()
            turned_product(turned, rights, outs.at[1], columns)
            stores.add(outs.at[1], gate_ref)
            turn(lefts.at[1])
            turned_product(turned, rights, outs.at[2], columns)
            stores.add(outs.at[2], up_ref)
            for errand in errands:
                errand.middle()

    sends = scatter_core(NN, [hidden], [weight], buffers, beside)
    stores.add(buffers[5], total_ref)
    for copy in sends:
        copy.wait_send()
    half.wait()
    stores.finish()
    for errand in errands:
        errand.finish()


def mlp_scatter(hidden, weight, grads, gate_grad, up_grad, gathered, collective_id, errands=()):
    tokens, units = hidden.shape
    rows, depth = tokens // 8, weight.shape[1]
    kinds, sources = [e[0] for e in errands], [e[1] for e in errands]
    hbm = pl.BlockSpec(memory_space=pl.ANY)
    by_unit = jax.ShapeDtypeStruct(weight.shape, BF16)
    blocks = [v.reshape(8, rows, units) for v in (hidden, gate_grad, up_grad)]
    return pl.pallas_call(
        functools.partial(mlp_body, kinds),
        in_specs=[hbm] * (6 + len(kinds)),
        out_specs=[hbm] * (5 + len(kinds)),
        out_shape=[
            jax.ShapeDtypeStruct((rows, depth), F32), by_unit, by_unit, by_unit,
            jax.ShapeDtypeStruct((units // 2, depth), BF16),
            *[errand_target(*errand) for errand in errands],
        ],
        scratch_shapes=[
            pltpu.VMEM((8, rows, units), BF16),
            pltpu.VMEM(weight.shape, BF16),
            pltpu.VMEM((tokens, depth), BF16),
            pltpu.VMEM((2, 8, rows, units), BF16),
            pltpu.VMEM((units, tokens), BF16),
            pltpu.VMEM((3, *weight.shape), BF16),
            *scatter_scratch(rows, depth),
            pltpu.SemaphoreType.DMA((1,)),
            pltpu.SemaphoreType.DMA((1,)),
            pltpu.SemaphoreType.DMA((10,)),
            *errand_scratch(kinds, sources),
        ],
        compiler_params=pltpu.CompilerParams(
            collective_id=collective_id, has_side_effects=True, vmem_limit_bytes=60 * 2**20
        ),
        name="scatter_mlp",
    )(blocks[0], weight, grads, blocks[1], blocks[2], gathered, *sources)


CHUNKS = 8


def finish_body(kinds, *refs):
    first_ref, refs, errands = take_errands(kinds, refs, 8, 4)
    left_ref, (weight_ref, rows_ref, tokens_ref, resid_ref, gain_ref) = first_ref, refs[:5]
    small_refs, tokens_grad_ref, total_grad_ref = refs[5:7], *refs[7:9]
    taps_out_ref, gains_out_ref, *refs = refs[9:]
    left, weight, gathered, turned, mine, other, came, far, tokens = refs[:9]
    resid, moving, taps, taps_recv, gains, gains_recv, *refs = refs[9:]
    buffers, refs = refs[:8], refs[8:]
    chain_send, chain_recv, sum_send, sum_recv, move_send, move_recv, local = refs
    loads = [
        pltpu.make_async_copy(source, target, local.at[i])
        for i, (source, target) in enumerate(
            (
                (left_ref, left), (weight_ref, weight), (rows_ref, gathered), (tokens_ref, tokens),
                (resid_ref, resid), (small_refs[0], taps), (small_refs[1], gains),
            )
        )
    ]
    for load in loads:
        load.start()
    greet(True)
    y = lax.axis_index("y")
    moved = is_moved()
    stays = jnp.logical_not(moved)
    size = mine.shape[0] // CHUNKS

    def chain(stage, index, source, target, axis):
        return pltpu.make_async_remote_copy(
            src_ref=source, dst_ref=target, send_sem=chain_send.at[stage, index],
            recv_sem=chain_recv.at[stage, index], device_id=neighbour(axis), device_id_type=MESH,
        )

    def total_rows(index, owner):
        start = owner * (size * CHUNKS) + index * size
        return total_grad_ref.at[pl.ds(pl.multiple_of(start, 16), size)]

    def chunk(ref, index):
        return ref.at[pl.ds(index * size, size)]

    def over(index):
        return chain(0, index, chunk(other, index), chunk(came, index), "y")

    def across(index):
        return chain(1, index, chunk(mine, index), chunk(far, index), "zh")

    def back(index):
        return chain(2, index, chunk(mine, index), total_rows(index, y), "y")

    def landing(index):
        return chain(2, index, total_rows(index, 1 - y), total_rows(index, 1 - y), "y")

    def cross(index):
        return chain(3, index, chunk(mine, index), total_rows(index, y), "core")

    def pass_on(index):
        return chain(4, index, total_rows(index, 1 - y), total_rows(index, 1 - y), "core")

    def near(index):
        return pltpu.make_async_copy(chunk(mine, index), total_rows(index, y), local.at[8 + index])

    def add(index, source):
        at, more = chunk(mine, index), chunk(source, index)
        at[...] = (at[...].astype(F32) + more[...].astype(F32)).astype(BF16)

    def sum_y(index):
        over(index).wait_recv()
        add(index, came)
        pl.when(moved)(lambda: across(index).start())

    def sum_z(index):
        @pl.when(stays)
        def _():
            across(index).wait_recv()
            add(index, far)
            back(index).start()
            cross(index).start()
            near(index).start()

    def forward(index):
        @pl.when(stays)
        def _():
            landing(index).wait_recv()
            pass_on(index).start()

    def weight_grad(owner, index, target):
        start = pl.multiple_of(owner * (size * CHUNKS) + index * size, size)
        turned[...] = gathered[:, pl.ds(start, size)].T
        turned_product(turned, left, chunk(target, index), left.shape[1])

    def sum_step(values, received, first, axes, index):
        def round_of(index):
            return pltpu.make_async_remote_copy(
                src_ref=values, dst_ref=received.at[index], send_sem=sum_send.at[first + index],
                recv_sem=sum_recv.at[first + index], device_id=neighbour(axes[index]),
                device_id_type=MESH,
            )

        if index > 0:
            round_of(index - 1).wait()
            values[...] += received[index - 1]
        if index < len(axes):
            round_of(index).start()

    def taps_step(index):
        sum_step(taps, taps_recv, 0, ("y", "zh"), index)

    def gains_step(index):
        sum_step(gains, gains_recv, 2, ("zh", "y", "core", "x", "zl"), index)

    def far_part(index):
        weight_grad(1 - y, index, other)
        over(index).start()

    def near_part(index):
        weight_grad(y, index, mine)
        sum_y(index)

    for load in loads:
        load.wait()
    for errand in errands:
        errand.start()
    taps_step(0)
    far_part(0)
    far_part(1)

    def beside(point):
        if point == 0:
            far_part(2)
            far_part(3)
            taps_step(1)
        elif point == "far sent":
            far_part(4)
            far_part(5)
            near_part(0)
        elif point == "side sent":
            far_part(6)
            far_part(7)
            taps_step(2)
            near_part(1)
            for errand in errands:
                errand.middle()
        elif point == 1:
            near_part(2)
        elif point == 2:
            near_part(3)
            sum_z(0)
        elif point == 3:
            near_part(4)

    sends = scatter_core(NT, [left], [weight], buffers, beside, SCATTER_CUT)
    total = buffers[5]
    gain = gain_ref[...]

    def backward(step, along):
        at = pl.ds(pl.multiple_of(step * 32, 32), 32)
        values = tokens[at].astype(F32)
        scale = lax.rsqrt(jnp.mean(values * values, -1, keepdims=True) + 1e-05)
        grad = total[at]
        scaled = grad * gain
        mean = jnp.mean(values * scaled, -1, keepdims=True)
        change = scale * scaled - values * (scale * scale * scale * mean)
        moving[at] = (resid[at] + change).astype(BF16)
        return along + jnp.sum(grad * values * scale, 0, keepdims=True)

    along = lax.fori_loop(
        0, total.shape[0] // 32, backward, jnp.zeros((1, total.shape[1]), F32)
    )
    wide = gains.shape[1]
    for index in range(along.shape[1] // wide):
        gains[index : index + 1, :] = along[:, index * wide : (index + 1) * wide]
    gains_step(0)
    near_part(5)
    sum_z(1)
    near_part(6)
    gains_step(1)
    move = make_errands(
        [Exchange], [moving], [tokens_grad_ref], move_send, move_recv,
        local.at[pl.ds(9 + CHUNKS, 1)],
    )[0]
    stores = Stores(local.at[pl.ds(10 + CHUNKS, 2)])
    stores.add(taps, taps_out_ref)
    sum_z(2)
    near_part(7)
    move.start()
    gains_step(2)
    sum_z(3)
    forward(0)
    gains_step(3)
    forward(1)
    sum_z(4)
    gains_step(4)
    forward(2)
    sum_z(5)
    gains_step(5)
    stores.add(gains, gains_out_ref)
    forward(3)
    sum_z(6)
    forward(4)
    sum_z(7)
    forward(5)
    forward(6)
    forward(7)
    for copy in sends:
        copy.wait_send()
    for index in range(CHUNKS):
        over(index).wait_send()

        @pl.when(moved)
        def _(index=index):
            across(index).wait_send()
            cross(index).wait_recv()
            pass_on(index).wait_recv()

        @pl.when(stays)
        def _(index=index):
            back(index).wait_send()
            cross(index).wait_send()
            pass_on(index).wait_send()
            near(index).wait()

    move.finish()
    for errand in errands:
        errand.finish()
    stores.finish()


def finish(
    left, weight, gathered, tokens, resid_grad, gain, taps, gains, collective_id,
    errands=(),
):
    rows, width = tokens.shape
    kinds, sources = [e[0] for e in errands], [e[1] for e in errands]
    hbm = pl.BlockSpec(memory_space=pl.ANY)
    depth, columns = weight.shape
    half = pltpu.VMEM((depth // 2, columns), BF16)
    return pl.pallas_call(
        functools.partial(finish_body, kinds),
        in_specs=[hbm] * 5 + [pl.BlockSpec(memory_space=pltpu.VMEM)] + [hbm] * (2 + len(kinds)),
        out_specs=[hbm] * (4 + len(kinds)),
        out_shape=[
            jax.ShapeDtypeStruct(tokens.shape, BF16),
            jax.ShapeDtypeStruct(weight.shape, BF16),
            jax.ShapeDtypeStruct(taps.shape, F32),
            jax.ShapeDtypeStruct(gains.shape, F32),
            *[errand_target(*errand) for errand in errands],
        ],
        scratch_shapes=[
            pltpu.VMEM(left.shape, BF16),
            pltpu.VMEM(weight.shape, BF16),
            pltpu.VMEM(gathered.shape, BF16),
            pltpu.VMEM((depth // 2 // CHUNKS, gathered.shape[0]), BF16),
            half,
            half,
            half,
            half,
            pltpu.VMEM((rows, width), BF16),
            pltpu.VMEM((rows, width), F32),
            pltpu.VMEM((rows, width), BF16),
            pltpu.VMEM(taps.shape, F32),
            pltpu.VMEM((2, *taps.shape), F32),
            pltpu.VMEM(gains.shape, F32),
            pltpu.VMEM((5, *gains.shape), F32),
            *scatter_scratch(rows, width),
            pltpu.SemaphoreType.DMA((5, CHUNKS)),
            pltpu.SemaphoreType.DMA((5, CHUNKS)),
            pltpu.SemaphoreType.DMA((7,)),
            pltpu.SemaphoreType.DMA((7,)),
            pltpu.SemaphoreType.DMA((1,)),
            pltpu.SemaphoreType.DMA((1,)),
            pltpu.SemaphoreType.DMA((12 + CHUNKS,)),
            *errand_scratch(kinds, sources),
        ],
        compiler_params=pltpu.CompilerParams(
            collective_id=collective_id, has_side_effects=True, vmem_limit_bytes=60 * 2**20
        ),
        name="finish",
    )(left, weight, gathered, tokens, resid_grad, gain, taps, gains, *sources)


def rms_scale(values, gain):
    return values * lax.rsqrt(jnp.mean(values * values, -1, keepdims=True) + 1e-05) * gain


def swiglu(gate, up_vals):
    return jax.nn.silu(gate) * up_vals


def left_product(left, right):
    return dot(left, right, TN)


def token_scales(group_ids, mixture_counts):
    group_cols = lax.broadcasted_iota(jnp.int32, (1, GROUPS), 1)
    counts = mixture_counts.astype(F32)
    group_scale = jnp.sqrt(jnp.mean(counts) / counts)
    return jnp.sum(jnp.where(group_ids[:, None] == group_cols, group_scale[None, :], 0.0), 1)


def mixer_weights(w_query, w_key, w_value, w_gate_mix, w_beta):
    padded = jnp.pad(w_beta, ((0, 0), (0, 128 - w_beta.shape[1])))
    return jnp.concatenate([w_query, w_key, w_value, w_gate_mix, padded], 1)


ALL = ("y", "core", "zh", "zl", "x")
SIZES = (2, 2, 2, 2, 2)


CORE_PAIRS = [(i, i ^ 8) for i in range(32)]


FORWARD_PLAN = (
    (0, 0, "start"), (0, 1, "start"), (0, 2, "start"), (3, 1, "middle"), (4, 0, "early"),
    (5, 2, "early"), (6, 0, "middle"), (7, 2, "late"), (7, 0, "late"),
    (7, 0, "finish"), (7, 1, "finish"), (7, 2, "finish"),
)
BACKWARD_PLAN = (
    (0, 0, "start"), (0, 3, "start"), (0, 1, "start"), (0, 2, "start"),
    (1, 0, "launch"), (2, 3, "launch"), (4, 1, "middle"), (6, 2, "middle"), (7, 0, "settle"),
    (7, 3, "settle_late"), (7, 0, "forward"), (7, 3, "forward"),
    (7, 0, "finish"), (7, 1, "finish"), (7, 2, "finish"), (7, 3, "finish"),
)


def halves_sum(values, came):
    rows = came.shape[0]
    mine = lax.dynamic_slice_in_dim(values, lax.axis_index("y") * rows, rows, 0)
    return (mine.astype(F32) + came.astype(F32)).astype(BF16)


def total_of(part, far):
    return (part.astype(F32) + far.astype(F32)).astype(BF16)


def shards_ring(
    tokens, group_ids, mixture_counts, grad_out, norm1_gain, w_query, w_key, w_value, w_gate_mix,
    w_beta, conv_query, conv_key, conv_value, out_gain, w_out, norm2_gain, w_gate, w_up, w_down,
):
    heads = w_beta.shape[1]
    head_cols = w_query.shape[1]
    gain = out_gain.astype(F32)[None]
    gain1 = norm1_gain.astype(F32)[None]
    conv = jnp.concatenate([conv_query, conv_key, conv_value], 1).astype(F32)
    conv = jnp.pad(conv, ((0, 4), (0, 0)))
    grad_mlp = grad_out.astype(F32) * token_scales(group_ids, mixture_counts)[:, None]
    padded_beta = jnp.pad(w_beta, ((0, 0), (0, 128 - heads)))
    tokens, gathered, projected, mix_weights, conv, grad_mlp = begin(
        tokens, gain1, conv, [w_query, w_key, w_value, w_gate_mix, padded_beta], 1,
        [(Exchange, grad_mlp.astype(BF16))],
    )
    inputs = tokens.astype(F32)
    mixed, *kept, gathered_grad, w_out, w_gate = mixer_forward(
        projected, conv, gain, heads,
        [(Gather, grad_mlp), (Swap, w_out), (Swap, w_gate.T)], FORWARD_PLAN, 2,
    )
    grad_rows = grad_mlp.astype(F32)
    attn, w_up, w_down = multiply_scatter(
        [mixed], [w_out], NN, 3, "scatter_attn", [(Swap, w_up.T), (Swap, w_down)]
    )
    resid = inputs + attn
    normed_mlp, norm2_back = jax.vjp(rms_scale, resid, norm2_gain.astype(F32))
    gathered_mlp, hidden, gate_grad, up_grad = feed(
        normed_mlp.astype(BF16), w_gate, w_up, w_down, gathered_grad, 4
    )
    gathered_grad = gathered_grad.reshape(-1, gathered_grad.shape[2])
    mlp_out, down_grad, gate_wgrad, up_wgrad, down_came = mlp_scatter(
        hidden, w_down, gathered_grad, gate_grad, up_grad, gathered_mlp, 5
    )
    output = (resid + mlp_out).astype(BF16)
    down_part = halves_sum(down_grad, down_came)
    normed_mlp_grad, gate_came, down_far = multiply_scatter(
        [gate_grad, up_grad], [w_gate, w_up], NN, 6, "scatter_normed_mlp_grad",
        [(HalfOverY, gate_wgrad), (Across, down_part)],
    )
    resid_norm_grad, norm2_grad = norm2_back(normed_mlp_grad)
    resid_grad = grad_rows + resid_norm_grad
    gate_part = halves_sum(gate_wgrad, gate_came)
    gathered_attn, mixed_grad, up_came, gate_far = gather_multiply(
        resid_grad.astype(BF16), [w_out], NT, 7, "gather_attn_grad",
        [(HalfOverY, up_wgrad), (Across, gate_part)],
    )
    up_part = halves_sum(up_wgrad, up_came)
    out_grad = left_product(mixed, gathered_attn).astype(BF16)
    raw_grad, conv_grad, gain_grad, up_total, down_total, gate_total, out_total = (
        mixer_backward(
            projected, conv, gain, mixed_grad, *kept, heads,
            [
                (Chain, up_part), (Spread, total_of(down_part, down_far)),
                (Spread, total_of(gate_part, gate_far)), (FullChain, out_grad),
            ],
            BACKWARD_PLAN, 8,
        )
    )
    width = tokens.shape[1]
    wide = width // 2
    gains = jnp.concatenate(
        [
            jnp.zeros((2, wide), F32), norm2_grad.reshape(2, wide),
            jnp.pad(gain_grad[:1], ((0, 3), (0, wide - gain_grad.shape[1]))),
        ],
        0,
    )
    grad_tokens, mix_total, taps, gains, output = finish(
        raw_grad, mix_weights, gathered, tokens, resid_grad, gain1, conv_grad, gains, 9,
        [(Exchange, output)],
    )
    other_taps = lax.ppermute(taps, ALL, CORE_PAIRS)
    conv_total = jnp.where(lax.axis_index("core") == lax.axis_index("zh"), taps, other_taps)[:4]
    mix_total = mix_total.astype(F32)
    return (
        output,
        grad_tokens,
        gains[:2].reshape(width),
        mix_total[:, 0:head_cols],
        mix_total[:, head_cols : 2 * head_cols],
        mix_total[:, 2 * head_cols : 3 * head_cols],
        mix_total[:, 3 * head_cols : 4 * head_cols],
        mix_total[:, 4 * head_cols : 4 * head_cols + heads],
        conv_total[:, 0:head_cols],
        conv_total[:, head_cols : 2 * head_cols],
        conv_total[:, 2 * head_cols :],
        gains[4, :HEAD_DIM],
        out_total.astype(F32),
        gains[2:4].reshape(width),
        gate_total.astype(F32).T,
        up_total.astype(F32).T,
        down_total.astype(F32),
    )


def right_product(left, right):
    return dot(left, right, NT)


def make_fold(kept_rows, weight, piece):
    weight_grad = left_product(kept_rows, piece)
    rows_grad = right_product(piece, weight)
    return (weight_grad, rows_grad)


def make_rows(source, weight, transposed):
    if transposed:
        return right_product(source, weight)
    return jnp.dot(source, weight, preferred_element_type=F32)


def shards(
    tokens,
    group_ids,
    mixture_counts,
    grad_out,
    norm1_gain,
    w_query,
    w_key,
    w_value,
    w_gate_mix,
    w_beta,
    conv_query,
    conv_key,
    conv_value,
    out_gain,
    w_out,
    norm2_gain,
    w_gate,
    w_up,
    w_down,
):
    inputs = tokens.astype(F32)
    normed, norm1_back = jax.vjp(rms_scale, inputs, norm1_gain.astype(F32))
    gathered = lax.all_gather(normed.astype(BF16), "tp", axis=0, tiled=True)
    heads = w_beta.shape[1]
    mix_weights = mixer_weights(w_query, w_key, w_value, w_gate_mix, w_beta)
    projected = jnp.dot(gathered, mix_weights, preferred_element_type=F32)
    head_cols = w_query.shape[1]
    conv = jnp.concatenate([conv_query, conv_key, conv_value], 1).astype(F32)
    gain = out_gain.astype(F32)[None]
    mixed, *kept = mixer_forward(projected, conv, gain, heads)
    attn = lax.psum_scatter(
        make_rows(mixed, w_out, False).astype(jnp.bfloat16), "tp", scatter_dimension=0, tiled=True
    ).astype(jnp.float32)
    resid = inputs + attn
    normed_mlp, norm2_back = jax.vjp(rms_scale, resid, norm2_gain.astype(F32))
    gathered_mlp = lax.all_gather(normed_mlp.astype(BF16), "tp", axis=0, tiled=True)
    pair_weights = jnp.concatenate([w_gate, w_up], 1)
    ff_cols = w_gate.shape[1]
    paired = jnp.dot(gathered_mlp, pair_weights, preferred_element_type=F32)
    hidden_full, swiglu_back = jax.vjp(swiglu, paired[:, :ff_cols], paired[:, ff_cols:])
    hidden = hidden_full.astype(BF16)
    mlp_out = lax.psum_scatter(
        make_rows(hidden, w_down, False).astype(jnp.bfloat16), "tp", scatter_dimension=0, tiled=True
    ).astype(jnp.float32)
    output = (resid + mlp_out).astype(BF16)
    token_scale = token_scales(group_ids, mixture_counts)
    grad_rows = grad_out.astype(F32) * token_scale[:, None]
    grad_mlp = grad_rows.astype(BF16)
    grad_w_down, hidden_grad = make_fold(
        hidden, w_down, lax.all_gather(grad_mlp, "tp", axis=0, tiled=True)
    )
    gate_grad, up_grad = swiglu_back(hidden_grad)
    pair_grad = jnp.concatenate([gate_grad, up_grad], 1).astype(BF16)
    pair_weight_grad = left_product(gathered_mlp, pair_grad)
    normed_mlp_grad = lax.psum_scatter(
        make_rows(pair_grad, pair_weights, True).astype(jnp.bfloat16),
        "tp",
        scatter_dimension=0,
        tiled=True,
    ).astype(jnp.float32)
    resid_norm_grad, norm2_grad = norm2_back(normed_mlp_grad)
    resid_grad = grad_rows + resid_norm_grad
    attn_grad = resid_grad.astype(BF16)
    grad_w_out, mixed_grad = make_fold(
        mixed, w_out, lax.all_gather(attn_grad, "tp", axis=0, tiled=True)
    )
    raw_grad, conv_grad, gain_grad = mixer_backward(
        projected, conv, gain, mixed_grad, *kept, heads
    )
    mix_weight_grad = left_product(gathered, raw_grad)
    normed_grad = lax.psum_scatter(
        make_rows(raw_grad, mix_weights, True).astype(jnp.bfloat16),
        "tp",
        scatter_dimension=0,
        tiled=True,
    ).astype(jnp.float32)
    input_norm_grad, norm1_grad = norm1_back(normed_grad)
    grad_tokens = (resid_grad + input_norm_grad).astype(BF16)
    summed = (
        lax.psum(mix_weight_grad.astype(jnp.bfloat16), "dp").astype(jnp.float32),
        lax.psum(grad_w_out.astype(jnp.bfloat16), "dp").astype(jnp.float32),
        lax.psum(pair_weight_grad.astype(jnp.bfloat16), "dp").astype(jnp.float32),
        lax.psum(grad_w_down.astype(jnp.bfloat16), "dp").astype(jnp.float32),
    )
    conv_total = lax.psum(conv_grad[:4], "dp")
    gains = lax.psum((norm1_grad, gain_grad[0], norm2_grad), ("dp", "tp"))
    mix_total = summed[0]
    pair_total = summed[2]
    return (
        output,
        grad_tokens,
        gains[0],
        mix_total[:, 0:head_cols],
        mix_total[:, head_cols : 2 * head_cols],
        mix_total[:, 2 * head_cols : 3 * head_cols],
        mix_total[:, 3 * head_cols : 4 * head_cols],
        mix_total[:, 4 * head_cols : 4 * head_cols + heads],
        conv_total[:, 0:head_cols],
        conv_total[:, head_cols : 2 * head_cols],
        conv_total[:, 2 * head_cols :],
        gains[1],
        summed[1],
        gains[2],
        pair_total[:, :ff_cols],
        pair_total[:, ff_cols:],
        summed[3],
    )


def solution(mesh):
    rows, cols, all_rows = "tp", "tp", ("dp", "tp")
    body = shards
    if dict(mesh.shape) == {"dp": 4, "tp": 8}:
        mesh = Mesh(mesh.devices.reshape(SIZES), ALL)
        rows = cols = ("zh", "zl", "x")
        all_rows = ALL
        body = shards_ring
    by_row, by_col, by_token = P(rows, None), P(None, cols), P(all_rows, None)
    return jax.shard_map(
        body,
        mesh=mesh,
        in_specs=(
            by_token, P(all_rows), P(), by_token, P(), by_col, by_col, by_col, by_col, by_col,
            by_col, by_col, by_col, P(), by_row, P(), by_col, by_col, by_row,
        ),
        out_specs=(
            by_token, by_token, P(), by_col, by_col, by_col, by_col, by_col, by_col, by_col,
            by_col, P(), by_row, P(), by_col, by_col, by_row,
        ),
        check_vma=False,
    )
```

```python
import functools

import jax
import jax.numpy as jnp
from jax import lax
from jax.experimental import pallas as pl
from jax.experimental.pallas import tpu as pltpu
from jax.sharding import Mesh
from jax.sharding import PartitionSpec as P

GROUPS = 8
HEAD_DIM = 128
SPAN = 64
SEQ_LEN = 2048
TILE = 256
F32 = jnp.float32
BF16 = jnp.bfloat16
NN = ((1,), (0,))
NT = ((1,), (1,))
TN = ((0,), (0,))


def split(values):
    high = values.astype(BF16)
    return high, (values - high.astype(F32)).astype(BF16)


def dot(left, right, dims):
    return lax.dot_general(left, right, (dims, ((), ())), preferred_element_type=F32)


def product(left, right, dims):
    return (
        dot(left[0], right[0], dims)
        + (dot(left[0], right[1], dims) + dot(left[1], right[0], dims))
    )


def quick(left, right, dims):
    return dot(left[0], right[0], dims)


def rows_of(pair, start, size):
    return pair[0][start : start + size], pair[1][start : start + size]


def sigmoid(values):
    return 1.0 / (1.0 + jnp.exp(-values))


def tile_masks():
    row = lax.broadcasted_iota(jnp.int32, (TILE, TILE), 0)
    col = lax.broadcasted_iota(jnp.int32, (TILE, TILE), 1)
    return row, col


def invert_all(lowers, row, col, refine=False):
    def level(size):
        return (row // (2 * size) == col // (2 * size)) & (row // size > col // size)

    first = level(1)
    eye = jnp.where(row == col, 1.0, 0.0)
    inverses = [eye - jnp.where(first, lower, 0.0) for lower in lowers]
    size = 2
    while size < SPAN:
        mask = level(size)
        parts = [split(jnp.where(mask, lower, 0.0)) for lower in lowers]
        held = [split(inverse) for inverse in inverses]
        firsts = [quick(part, h, NN) for part, h in zip(parts, held)]
        seconds = [quick(h, split(f), NN) for h, f in zip(held, firsts)]
        inverses = [inverse - second for inverse, second in zip(inverses, seconds)]
        size *= 2
    if True:
        held = [split(inverse) for inverse in inverses]
        rest = [
            eye - inverse - product(split(lower), h, NN)
            for lower, inverse, h in zip(lowers, inverses, held)
        ]
        inverses = [
            inverse + quick(h, split(r), NN) for inverse, h, r in zip(inverses, held, rest)
        ]
    return inverses


def conv_rows(buffer, taps):
    total = taps[0:1] * buffer[pl.ds(5, TILE), :]
    for offset in range(1, 4):
        total = total + taps[offset : offset + 1] * buffer[pl.ds(5 + offset, TILE), :]
    return total


LATE_PHASES = ("settle_late", "late_after", "forward", "finish")


def run_errands(errands, plan, step, late):
    if not errands:
        return
    if not late:
        pl.when(step == 0)(lambda: greet(True))
    for at in sorted({entry[0] for entry in plan}):

        @pl.when(step == at)
        def _(at=at):
            for when, index, phase in plan:
                if when == at and (phase in LATE_PHASES) == late:
                    getattr(errands[index], phase)()


def errand_operands(errands):
    kinds, sources = [e[0] for e in errands], [e[1] for e in errands]
    specs = [pl.BlockSpec(memory_space=pl.ANY)] * len(errands)
    shapes = [errand_target(*errand) for errand in errands]
    return kinds, sources, specs, shapes, errand_scratch(kinds, sources) if errands else []


def mixer_params(errands, collective_id):
    extra = {"collective_id": collective_id, "has_side_effects": True} if errands else {}
    return pltpu.CompilerParams(vmem_limit_bytes=48 * 2**20, **extra)


def mixer_forward_body(heads, kinds, plan, *refs):
    first_ref, refs, errands = take_errands(kinds, refs, 3, 6) if kinds else (refs[0], refs[1:], ())
    proj_ref = first_ref
    conv_ref, gain_ref, mixed_ref, wu_ref, fresh_ref, out_ref, state_ref, inverse_ref, *refs = refs
    rows_buf, state = refs
    tile = pl.program_id(1)
    run_errands(errands, plan, tile, False)
    wide = heads * HEAD_DIM

    @pl.when(tile == 0)
    def _():
        rows_buf[0:8, :] = jnp.zeros((8, 3 * wide), F32)
        state[...] = jnp.zeros_like(state)

    @pl.when(tile > 0)
    def _():
        rows_buf[0:8, :] = rows_buf[TILE : TILE + 8, :]

    rows_buf[8 : 8 + TILE, :] = proj_ref[:, : 3 * wide]
    summed = conv_rows(rows_buf, conv_ref[...])
    active = summed * sigmoid(summed)
    row, col = tile_masks()
    same = row // SPAN == col // SPAN
    held = []
    for head in range(heads):
        lo = head * HEAD_DIM
        query = active[:, lo : lo + HEAD_DIM]
        key = active[:, wide + lo : wide + lo + HEAD_DIM]
        value = active[:, 2 * wide + lo : 2 * wide + lo + HEAD_DIM]
        beta = sigmoid(proj_ref[:, 4 * wide + head : 4 * wide + head + 1])
        query = query * (
            lax.rsqrt(jnp.sum(query * query, -1, keepdims=True) + 1e-06) * HEAD_DIM ** (-0.5)
        )
        key = key * lax.rsqrt(jnp.sum(key * key, -1, keepdims=True) + 1e-06)
        key_beta = key * beta
        held.append((split(query), split(key), key_beta, value * beta))
    lowers = [
        jnp.where(same & (row > col), product(split(key_beta), key_s, NT), 0.0)
        for _, key_s, key_beta, _ in held
    ]
    inverses = invert_all(lowers, row, col)
    boths = [
        product(split(inverse), split(jnp.concatenate([key_beta, value_beta], 1)), NN)
        for inverse, (_, _, key_beta, value_beta) in zip(inverses, held)
    ]
    scores = [
        jnp.where(same & (row >= col), product(query_s, key_s, NT), 0.0)
        for query_s, key_s, _, _ in held
    ]
    weights = [split(both[:, :HEAD_DIM]) for both in boths]
    memories = [state[head] for head in range(heads)]
    fresh_all = [[] for _ in range(heads)]
    carried_all = [[] for _ in range(heads)]
    for block in range(TILE // SPAN):
        start = block * SPAN
        for head in range(heads):
            state_ref[block, head] = memories[head]
        reads = [
            product(
                tuple(
                    jnp.concatenate([a[start : start + SPAN], b[start : start + SPAN]], 0)
                    for a, b in zip(weights[head], held[head][0])
                ),
                split(memories[head]),
                NN,
            )
            for head in range(heads)
        ]
        for head in range(heads):
            fresh_all[head].append(boths[head][start : start + SPAN, HEAD_DIM:] - reads[head][:SPAN])
            carried_all[head].append(reads[head][SPAN:])
        memories = [
            memories[head]
            + product(rows_of(held[head][1], start, SPAN), split(fresh_all[head][-1]), TN)
            for head in range(heads)
        ]
    for head in range(heads):
        lo = head * HEAD_DIM
        state[head] = memories[head]
        inverse_ref[head] = inverses[head]
        wu_ref[:, 2 * lo : 2 * lo + 2 * HEAD_DIM] = boths[head]
        fresh = jnp.concatenate(fresh_all[head], 0)
        fresh_ref[:, lo : lo + HEAD_DIM] = fresh
        out = jnp.concatenate(carried_all[head], 0)
        out = out + product(split(scores[head]), split(fresh), NN)
        out_ref[:, lo : lo + HEAD_DIM] = out
        gate = proj_ref[:, 3 * wide + lo : 3 * wide + lo + HEAD_DIM]
        scale = lax.rsqrt(jnp.mean(out * out, -1, keepdims=True) + 1e-05)
        mixed = out * scale * gain_ref[...] * (gate * sigmoid(gate))
        mixed_ref[:, lo : lo + HEAD_DIM] = mixed.astype(BF16)
    run_errands(errands, plan, tile, True)


def mixer_forward(proj, conv, gain, heads, errands=(), plan=(), collective_id=None):
    rows = proj.shape[0]
    wide = heads * HEAD_DIM
    tiles = SEQ_LEN // TILE
    seqs = rows // SEQ_LEN
    blocks = TILE // SPAN

    def at(seq, tile):
        return (seq * tiles + tile, 0)

    kinds, sources, specs, shapes, scratch = errand_operands(errands)
    return pl.pallas_call(
        functools.partial(mixer_forward_body, heads, kinds, plan),
        grid=(seqs, tiles),
        in_specs=[
            pl.BlockSpec((TILE, proj.shape[1]), at),
            pl.BlockSpec(conv.shape, lambda seq, tile: (0, 0)),
            pl.BlockSpec(gain.shape, lambda seq, tile: (0, 0)),
            *specs,
        ],
        out_specs=[
            pl.BlockSpec((TILE, wide), at),
            pl.BlockSpec((TILE, 2 * wide), at),
            pl.BlockSpec((TILE, wide), at),
            pl.BlockSpec((TILE, wide), at),
            pl.BlockSpec((blocks, heads, HEAD_DIM, HEAD_DIM), lambda s, t: (s * tiles + t, 0, 0, 0)),
            pl.BlockSpec((None, heads, TILE, TILE), lambda s, t: (s * tiles + t, 0, 0, 0)),
            *specs,
        ],
        out_shape=[
            jax.ShapeDtypeStruct((rows, wide), BF16),
            jax.ShapeDtypeStruct((rows, 2 * wide), F32),
            jax.ShapeDtypeStruct((rows, wide), F32),
            jax.ShapeDtypeStruct((rows, wide), F32),
            jax.ShapeDtypeStruct((rows // SPAN, heads, HEAD_DIM, HEAD_DIM), F32),
            jax.ShapeDtypeStruct((rows // TILE, heads, TILE, TILE), F32),
            *shapes,
        ],
        scratch_shapes=[
            pltpu.VMEM((TILE + 8, 3 * wide), F32),
            pltpu.VMEM((heads, HEAD_DIM, HEAD_DIM), F32),
            *scratch,
        ],
        compiler_params=mixer_params(errands, collective_id),
        name="mixer_forward",
    )(proj, conv, gain, *sources)


def unit_back(raw, scale, grad):
    along = jnp.sum(raw * grad, -1, keepdims=True)
    return scale * grad - raw * (scale * scale * scale * along)


def mixer_backward_body(heads, kinds, plan, *refs):
    first_ref, refs, errands = take_errands(kinds, refs, 10, 3) if kinds else (refs[0], refs[1:], ())
    proj_ref = first_ref
    before_ref, conv_ref, gain_ref, grad_ref, wu_ref, fresh_ref, out_ref, *refs = refs
    state_ref, inverse_ref, raw_grad_ref, conv_grad_ref, gain_grad_ref, *refs = refs
    rows_buf, grad_buf, state_grad = refs
    step = pl.program_id(1)
    run_errands(errands, plan, step, False)
    steps = pl.num_programs(1)
    wide = heads * HEAD_DIM

    @pl.when((step == 0) & (pl.program_id(0) == 0))
    def _():
        conv_grad_ref[...] = jnp.zeros_like(conv_grad_ref)
        gain_grad_ref[...] = jnp.zeros_like(gain_grad_ref)

    @pl.when(step == 0)
    def _():
        grad_buf[TILE : TILE + 8, :] = jnp.zeros((8, 3 * wide), F32)
        state_grad[...] = jnp.zeros_like(state_grad)

    @pl.when(step > 0)
    def _():
        grad_buf[TILE : TILE + 8, :] = grad_buf[0:8, :]

    first = step == steps - 1
    rows_buf[0:8, :] = jnp.where(first, 0.0, before_ref[:, : 3 * wide])
    rows_buf[8 : 8 + TILE, :] = proj_ref[:, : 3 * wide]
    summed = conv_rows(rows_buf, conv_ref[...])
    smooth = sigmoid(summed)
    active = summed * smooth
    slope = smooth * (1.0 + summed * (1.0 - smooth))
    row, col = tile_masks()
    same = row // SPAN == col // SPAN
    lane = lax.broadcasted_iota(jnp.int32, (TILE, HEAD_DIM), 1)
    beta_grads = jnp.zeros((TILE, HEAD_DIM), F32)
    gain_total = jnp.zeros((1, HEAD_DIM), F32)
    within = same & (row >= col)
    below = same & (row > col)
    every = range(heads)
    at = [slice(head * HEAD_DIM, (head + 1) * HEAD_DIM) for head in every]
    query_raw = [active[:, lo] for lo in at]
    key_raw = [active[:, wide : 2 * wide][:, lo] for lo in at]
    value = [active[:, 2 * wide :][:, lo] for lo in at]
    beta = [sigmoid(proj_ref[:, 4 * wide + head : 4 * wide + head + 1]) for head in every]
    query_scale = [lax.rsqrt(jnp.sum(q * q, -1, keepdims=True) + 1e-06) for q in query_raw]
    key_scale = [lax.rsqrt(jnp.sum(k * k, -1, keepdims=True) + 1e-06) for k in key_raw]
    key = [k * scale for k, scale in zip(key_raw, key_scale)]
    key_s = [split(k) for k in key]
    query_s = [
        split(q * (scale * HEAD_DIM ** (-0.5))) for q, scale in zip(query_raw, query_scale)
    ]
    out_grad_s = []
    for head, lo in enumerate(at):
        gate = proj_ref[:, 3 * wide + head * HEAD_DIM : 3 * wide + (head + 1) * HEAD_DIM]
        grad = grad_ref[:, lo]
        out = out_ref[:, lo]
        scale = lax.rsqrt(jnp.mean(out * out, -1, keepdims=True) + 1e-05)
        gate_s = sigmoid(gate)
        normed = out * scale
        gain_total = gain_total + jnp.sum(grad * normed * (gate * gate_s), 0, keepdims=True)
        gate_grad = grad * normed * gain_ref[...] * (gate_s * (1.0 + gate * (1.0 - gate_s)))
        normed_grad = grad * gain_ref[...] * (gate * gate_s)
        out_grad = scale * normed_grad - out * (
            scale * scale * scale * jnp.mean(out * normed_grad, -1, keepdims=True)
        )
        out_grad_s.append(split(out_grad))
        raw_grad_ref[:, 3 * wide + head * HEAD_DIM : 3 * wide + (head + 1) * HEAD_DIM] = (
            gate_grad.astype(BF16)
        )
    fresh_s = [split(fresh_ref[:, lo]) for lo in at]
    both_s = [split(wu_ref[:, 2 * head * HEAD_DIM : 2 * (head + 1) * HEAD_DIM]) for head in every]
    weights_s = [(high[:, :HEAD_DIM], low[:, :HEAD_DIM]) for high, low in both_s]
    scores_s = [
        split(jnp.where(within, product(query_s[h], key_s[h], NT), 0.0)) for h in every
    ]
    fresh_grad_in = [product(scores_s[h], out_grad_s[h], TN) for h in every]
    carry = [state_grad[head] for head in every]
    blocks = TILE // SPAN
    parts = [[None] * blocks for _ in every]
    for block in range(blocks - 1, -1, -1):
        start = block * SPAN
        carry_s = [split(c) for c in carry]
        fresh_grad = [
            fresh_grad_in[h][start : start + SPAN]
            + product(rows_of(key_s[h], start, SPAN), carry_s[h], NN)
            for h in every
        ]
        fresh_grad_s = [split(f) for f in fresh_grad]
        out_rows = [rows_of(out_grad_s[h], start, SPAN) for h in every]
        carry = [
            carry[h]
            + (
                product(rows_of(query_s[h], start, SPAN), out_rows[h], TN)
                - product(rows_of(weights_s[h], start, SPAN), fresh_grad_s[h], TN)
            )
            for h in every
        ]
        for h in every:
            stacked = tuple(
                jnp.concatenate([a, b], 0) for a, b in zip(out_rows[h], fresh_grad_s[h])
            )
            back = product(stacked, split(state_ref[block, h]), NT)
            through = product(rows_of(fresh_s[h], start, SPAN), carry_s[h], NT)
            parts[h][block] = (fresh_grad[h], back[:SPAN], -back[SPAN:], through)
    for h in every:
        state_grad[h] = carry[h]
    scores_grad_s = [
        split(jnp.where(within, product(out_grad_s[h], fresh_s[h], NT), 0.0)) for h in every
    ]
    joined = [
        [jnp.concatenate([part[i] for part in parts[h]], 0) for i in range(4)] for h in every
    ]
    query_grad = [joined[h][1] + product(scores_grad_s[h], key_s[h], NN) for h in every]
    key_grad = [joined[h][3] + product(scores_grad_s[h], query_s[h], TN) for h in every]
    right_grad = [
        product(
            split(inverse_ref[h]),
            split(jnp.concatenate([joined[h][2], joined[h][0]], 1)),
            TN,
        )
        for h in every
    ]
    lower_grad_s = [
        split(jnp.where(below, -product(split(right_grad[h]), both_s[h], NT), 0.0)) for h in every
    ]
    key_beta_grad = [
        right_grad[h][:, :HEAD_DIM] + product(lower_grad_s[h], key_s[h], NN) for h in every
    ]
    key_grad = [
        key_grad[h]
        + product(lower_grad_s[h], split(key[h] * beta[h]), TN)
        + key_beta_grad[h] * beta[h]
        for h in every
    ]
    for h, lo in enumerate(at):
        value_beta_grad = right_grad[h][:, HEAD_DIM:]
        beta_grad = jnp.sum(
            key_beta_grad[h] * key[h] + value_beta_grad * value[h], -1, keepdims=True
        )
        beta_grad = beta_grad * (beta[h] * (1.0 - beta[h]))
        beta_grads = jnp.where(lane == h, beta_grad, beta_grads)
        query_back = unit_back(query_raw[h], query_scale[h], query_grad[h] * HEAD_DIM ** (-0.5))
        key_back = unit_back(key_raw[h], key_scale[h], key_grad[h])
        for index, grad in enumerate((query_back, key_back, value_beta_grad * beta[h])):
            first = index * wide + h * HEAD_DIM
            grad_buf[0:TILE, first : first + HEAD_DIM] = grad * slope[:, first : first + HEAD_DIM]
    raw_grad_ref[:, 4 * wide :] = beta_grads.astype(BF16)
    gain_grad_ref[0:1, :] += gain_total
    taps = conv_ref[...]
    here = grad_buf[0:TILE, :]
    total = taps[3:4] * here
    conv_grad_ref[3:4, :] += jnp.sum(here * rows_buf[8 : 8 + TILE, :], 0, keepdims=True)
    for offset in range(3):
        total = total + taps[offset : offset + 1] * grad_buf[pl.ds(3 - offset, TILE), :]
        conv_grad_ref[offset : offset + 1, :] += jnp.sum(
            here * rows_buf[pl.ds(5 + offset, TILE), :], 0, keepdims=True
        )
    raw_grad_ref[:, : 3 * wide] = total.astype(BF16)
    run_errands(errands, plan, step, True)


def mixer_backward(
    proj, conv, gain, grad, wu, fresh, out, states, inverses, heads,
    errands=(), plan=(), collective_id=None,
):
    rows = proj.shape[0]
    wide = heads * HEAD_DIM
    tiles = SEQ_LEN // TILE
    seqs = rows // SEQ_LEN
    blocks = TILE // SPAN

    def index(seq, step):
        return seq * tiles + tiles - 1 - step

    def at(seq, step):
        return (index(seq, step), 0)

    def ahead(seq, step):
        return (jnp.maximum(index(seq, step) * (TILE // 8) - 1, 0), 0)

    def fixed(seq, step):
        return (0, 0)

    kinds, sources, specs, shapes, scratch = errand_operands(errands)
    return pl.pallas_call(
        functools.partial(mixer_backward_body, heads, kinds, plan),
        grid=(seqs, tiles),
        in_specs=[
            pl.BlockSpec((TILE, proj.shape[1]), at),
            pl.BlockSpec((8, proj.shape[1]), ahead),
            pl.BlockSpec(conv.shape, fixed),
            pl.BlockSpec(gain.shape, fixed),
            pl.BlockSpec((TILE, wide), at),
            pl.BlockSpec((TILE, 2 * wide), at),
            pl.BlockSpec((TILE, wide), at),
            pl.BlockSpec((TILE, wide), at),
            pl.BlockSpec(
                (blocks, heads, HEAD_DIM, HEAD_DIM), lambda s, t: (index(s, t), 0, 0, 0)
            ),
            pl.BlockSpec((None, heads, TILE, TILE), lambda s, t: (index(s, t), 0, 0, 0)),
            *specs,
        ],
        out_specs=[
            pl.BlockSpec((TILE, 4 * wide + 128), at),
            pl.BlockSpec((8, 3 * wide), fixed),
            pl.BlockSpec((8, HEAD_DIM), fixed),
            *specs,
        ],
        out_shape=[
            jax.ShapeDtypeStruct((rows, 4 * wide + 128), BF16),
            jax.ShapeDtypeStruct((8, 3 * wide), F32),
            jax.ShapeDtypeStruct((8, HEAD_DIM), F32),
            *shapes,
        ],
        scratch_shapes=[
            pltpu.VMEM((TILE + 8, 3 * wide), F32),
            pltpu.VMEM((TILE + 8, 3 * wide), F32),
            pltpu.VMEM((heads, HEAD_DIM, HEAD_DIM), F32),
            *scratch,
        ],
        compiler_params=mixer_params(errands, collective_id),
        name="mixer_backward",
    )(proj, proj, conv, gain, grad, wu, fresh, out, states, inverses, *sources)


MESH = pl.DeviceIdType.MESH


def place():
    return lax.axis_index("core"), lax.axis_index("zl"), lax.axis_index("x")


def slot_of(core, deep, wide):
    own_core, own_deep, own_wide = place()
    return (
        jnp.where(core, 1 - own_core, own_core) * 4
        + jnp.where(deep, 1 - own_deep, own_deep) * 2
        + jnp.where(wide, 1 - own_wide, own_wide)
    )


def on_part(outer):
    at_end = lax.axis_index("zl") == lax.axis_index("zh")
    return is_moved() & (at_end if outer else jnp.logical_not(at_end))


def is_moved():
    return lax.axis_index("core") != lax.axis_index("zh")


def greet(everyone=False):
    barrier = pltpu.get_barrier_semaphore()
    axes = ("core", "zl", "x", "y", "zh") if everyone else ("core", "zl", "x")
    for axis in axes:
        pl.semaphore_signal(barrier, inc=1, device_id=neighbour(axis), device_id_type=MESH)
    peers = len(axes)
    if everyone:
        pl.when(is_moved())(
            lambda: pl.semaphore_signal(
                barrier, inc=1, device_id=partner(), device_id_type=MESH
            )
        )
        peers = peers + is_moved().astype(jnp.int32)
    pl.semaphore_wait(barrier, peers)


def partner():
    return {"core": lax.axis_index("zh"), "zh": lax.axis_index("core")}


def row_half(ref, index):
    rows = ref.shape[0] // 2
    return ref.at[pl.ds(pl.multiple_of(index * rows, 16), rows)]


class Errand:
    sems = 1
    buffers = 1

    def __init__(self, source, target, send, recv, local, buffers=()):
        self.source, self.target, self.held = source, target, buffers
        self.stage = buffers[0] if buffers else None
        self.send, self.recv, self.local = send, recv, local
        self.y = lax.axis_index("y")

    def remote(self, index, source, target, device):
        return pltpu.make_async_remote_copy(
            src_ref=source, dst_ref=target, send_sem=self.send.at[index],
            recv_sem=self.recv.at[index], device_id=device, device_id_type=MESH,
        )

    @staticmethod
    def buffer_shape(shape):
        return shape

    def start_part(self, outer):
        if outer:
            self.start()

    def start_outer(self):
        self.start_part(True)

    def start_inner(self):
        self.start_part(False)

    def stays(self, action):
        pl.when(jnp.logical_not(is_moved()))(action)

    def own_target(self):
        return self.target

    def here(self):
        source = self.source if self.stage is None else self.stage
        return pltpu.make_async_copy(source, self.own_target(), self.local)

    def stage_in(self):
        return pltpu.make_async_copy(self.source, self.stage, self.local)

    def start_here(self):
        self.stays(lambda: (self.here() if self.stage is None else self.stage_in()).start())

    def pass_here(self):
        def action():
            self.stage_in().wait()
            self.here().start()

        if self.stage is not None:
            self.stays(action)

    def finish_here(self):
        self.stays(lambda: self.here().wait())


class Exchange(Errand):
    def far(self):
        return self.remote(0, self.source, self.target, partner())

    def start(self):
        pl.when(is_moved())(lambda: self.far().start())
        self.start_here()

    def middle(self):
        self.pass_here()

    def finish(self):
        pl.when(is_moved())(lambda: self.far().wait())
        self.finish_here()


class Swap(Errand):
    sems = 4

    def piece(self, ref, owner, index):
        rows = ref.shape[0] // 4
        return ref.at[pl.ds(pl.multiple_of((owner * 2 + index) * rows, 16), rows)]

    def first(self, index):
        return self.remote(
            index, self.piece(self.source, self.y, index), self.piece(self.target, self.y, index),
            partner(),
        )

    def second(self, index, landing=False):
        half = self.piece(self.target, 1 - self.y if landing else self.y, index)
        return self.remote(2 + index, half, half, neighbour("y"))

    def start(self):
        self.start_part(True)
        self.start_part(False)

    def start_part(self, outer):
        @pl.when(on_part(outer))
        def _():
            self.first(0).start()
            self.first(1).start()

        if outer:
            self.start_here()

    def pass_piece(self, index):
        @pl.when(is_moved())
        def _():
            self.first(index).wait_recv()
            self.second(index).start()

    def early(self):
        self.pass_piece(0)
        self.pass_here()

    def late(self):
        self.pass_piece(1)

    def late_after(self):
        self.late()

    def middle(self):
        self.early()
        self.late()

    def finish(self):
        @pl.when(is_moved())
        def _():
            for index in range(2):
                self.first(index).wait_send()
                self.second(index).wait_send()
                self.second(index, True).wait_recv()

        self.finish_here()


class HalfOverY(Errand):
    buffers = 0

    def copy(self):
        return self.remote(0, row_half(self.source, 1 - self.y), self.target, neighbour("y"))

    def start(self):
        self.copy().start()

    def middle(self):
        pass

    def finish(self):
        self.copy().wait()


class Across(Errand):
    buffers = 0

    def copy(self):
        return self.remote(0, self.source, self.target, neighbour("zh"))

    def start(self):
        pl.when(is_moved())(lambda: self.copy().start())

    def start_part(self, outer):
        pl.when(on_part(outer))(lambda: self.copy().start())

    def middle(self):
        pass

    def finish(self):
        pl.when(is_moved())(lambda: self.copy().wait_send())
        self.stays(lambda: self.copy().wait_recv())


SCATTER_CUT = 208


class Gather(Errand):
    sems = 11

    def ring(self):
        return Ring(self.target, self.send, self.recv, 0, self.stage)

    def own(self):
        return pltpu.make_async_copy(self.stage, self.target.at[slot_of(0, 0, 0)], self.local)

    def start(self):
        self.stage_in().start()
        self.stage_in().wait()
        self.own().start()
        self.ring().launch(0, 1, 2, 3, 4)

    def early(self):
        ring = self.ring()
        ring.arrived(0)
        ring.launch(5)
        ring.arrived(1)
        ring.launch(6)

    def middle(self):
        ring = self.ring()
        ring.arrived(2)
        ring.launch(7)
        ring.arrived(3)
        ring.launch(8)

    def late(self):
        ring = self.ring()
        ring.arrived(5)
        ring.launch(9)
        ring.arrived(6)
        ring.launch(10)

    def finish(self):
        ring = self.ring()
        ring.arrived(4, 7, 8, 9, 10)
        ring.finish()
        self.own().wait()


class Spread(Errand):
    sems = 3

    def own_target(self):
        return row_half(self.target, self.y)

    def over(self):
        return self.remote(0, self.source, self.own_target(), neighbour("y"))

    def other(self, index, axis):
        view = row_half(self.target, 1 - self.y)
        return self.remote(index, view, view, neighbour(axis))

    def cross(self):
        return self.remote(1, self.source, self.own_target(), neighbour("core"))

    def start(self):
        @pl.when(jnp.logical_not(is_moved()))
        def _():
            self.over().start()
            self.cross().start()

        self.start_here()

    def middle(self):
        @pl.when(jnp.logical_not(is_moved()))
        def _():
            self.other(0, "y").wait_recv()
            self.other(2, "core").start()

        self.pass_here()

    def finish(self):
        @pl.when(jnp.logical_not(is_moved()))
        def _():
            self.over().wait_send()
            self.cross().wait_send()
            self.other(2, "core").wait_send()

        @pl.when(is_moved())
        def _():
            self.cross().wait_recv()
            self.other(2, "core").wait_recv()

        self.finish_here()


class Chain(Errand):
    sems = 5
    buffers = 2

    def mine(self):
        return self.held[0]

    def load(self):
        return pltpu.make_async_copy(self.source, self.mine(), self.local)

    def across(self):
        return self.remote(0, self.mine(), self.held[1], neighbour("zh"))

    def own_rows(self):
        return row_half(self.target, self.y)

    def near(self):
        return pltpu.make_async_copy(self.mine(), self.own_rows(), self.local)

    def over(self):
        return self.remote(1, self.mine(), self.own_rows(), neighbour("y"))

    def cross(self):
        return self.remote(2, self.mine(), self.own_rows(), neighbour("core"))

    def other(self, index, axis):
        view = row_half(self.target, 1 - self.y)
        return self.remote(index, view, view, neighbour(axis))

    def add(self, more):
        mine = self.mine()
        mine[...] = (mine[...].astype(F32) + more[...].astype(F32)).astype(BF16)

    def start(self):
        self.load().start()

    def launch(self):
        self.load().wait()
        pl.when(is_moved())(lambda: self.across().start())

    def settle(self):
        @pl.when(jnp.logical_not(is_moved()))
        def _():
            self.across().wait_recv()
            self.add(self.held[1])
            self.over().start()
            self.cross().start()
            self.near().start()

    def settle_late(self):
        self.settle()

    def forward(self):
        @pl.when(jnp.logical_not(is_moved()))
        def _():
            self.other(1, "y").wait_recv()
            self.other(3, "core").start()

    def finish(self):
        @pl.when(jnp.logical_not(is_moved()))
        def _():
            self.near().wait()
            self.over().wait_send()
            self.cross().wait_send()
            self.other(3, "core").wait_send()

        @pl.when(is_moved())
        def _():
            self.across().wait_send()
            self.cross().wait_recv()
            self.other(3, "core").wait_recv()


class FullChain(Chain):
    buffers = 3

    @staticmethod
    def buffer_shape(shape):
        return (shape[0] // 2, *shape[1:])

    def load(self):
        return pltpu.make_async_copy(row_half(self.source, self.y), self.mine(), self.local)

    def halves(self):
        return self.remote(4, row_half(self.source, 1 - self.y), self.held[2], neighbour("y"))

    def start(self):
        self.halves().start()
        self.load().start()

    def launch(self):
        self.load().wait()
        self.halves().wait()
        self.add(self.held[2])
        pl.when(is_moved())(lambda: self.across().start())


def errand_target(kind, source):
    if kind is Gather:
        return jax.ShapeDtypeStruct((8, *source.shape), source.dtype)
    rows = source.shape[0]
    rows = {HalfOverY: rows // 2, Spread: 2 * rows, Chain: 2 * rows}.get(kind, rows)
    return jax.ShapeDtypeStruct((rows, *source.shape[1:]), source.dtype)


def errand_scratch(kinds, sources=()):
    total = max(1, sum(kind.sems for kind in kinds))
    places = [
        pltpu.VMEM(kind.buffer_shape(source.shape), BF16)
        for kind, source in zip(kinds, sources)
        for _ in range(kind.buffers)
    ]
    return [
        *places,
        pltpu.SemaphoreType.DMA((total,)),
        pltpu.SemaphoreType.DMA((total,)),
        pltpu.SemaphoreType.DMA((max(1, len(kinds)),)),
    ]


def make_errands(kinds, sources, targets, send, recv, local, places=()):
    made, at, used = [], 0, 0
    for index, (kind, source, target) in enumerate(zip(kinds, sources, targets)):
        view = pl.ds(at, kind.sems)
        held = places[used : used + kind.buffers] if places else ()
        made.append(kind(source, target, send.at[view], recv.at[view], local.at[index], held))
        at += kind.sems
        used += kind.buffers
    return made


def neighbour(axis):
    return {axis: 1 - lax.axis_index(axis)}


def column_tile(columns):
    for size in (512, 384, 256, 128):
        if columns % size == 0:
            return size
    return columns


def column_parts(columns):
    tile = column_tile(columns)
    if tile != columns or columns <= 512:
        return [(0, tile, columns // tile)]
    whole = columns // 256 * 256
    return [(0, 256, whole // 256), (whole, columns - whole, 1)]


def by_columns(columns, body):
    for start, size, steps in column_parts(columns):
        if steps == 1:
            body(pl.ds(start, size))
        else:

            def column(step, _, start=start, size=size):
                body(pl.ds(pl.multiple_of(start + step * size, 128), size))
                return 0

            lax.fori_loop(0, steps, column, 0)


def take_errands(kinds, refs, inputs, outputs):
    extra = len(kinds)
    sources = refs[inputs : inputs + extra]
    targets = refs[inputs + extra + outputs : inputs + 2 * extra + outputs]
    last = len(refs) - 3 - sum(kind.buffers for kind in kinds)
    errands = make_errands(kinds, sources, targets, *refs[-3:], refs[last:-3])
    rest = (
        *refs[:inputs], *refs[inputs + extra : inputs + extra + outputs],
        *refs[inputs + 2 * extra + outputs : last],
    )
    return rest[0], rest[1:], errands


class Ring:
    def __init__(self, held, send, recv, cut=None, block=None):
        self.block = block
        self.held, self.send, self.recv = held, send, recv
        own, wide, deep, far = (slot_of(0, *at) for at in ((0, 0), (0, 1), (1, 0), (1, 1)))
        rows = held.shape[1]
        cut = rows // 2 if cut is None else cut
        rest = rows - cut
        self.moves = (
            ("x", own, wide, 0, cut), ("zl", own, deep, cut, rest),
            ("x", own, wide, cut, rest), ("zl", own, deep, 0, cut),
            ("core", own, slot_of(1, 0, 0), 0, rows),
            ("zl", wide, far, 0, cut), ("x", deep, far, cut, rest),
            ("core", wide, slot_of(1, 0, 1), 0, rows),
            ("core", deep, slot_of(1, 1, 0), 0, rows),
            ("core", far, slot_of(1, 1, 1), 0, cut),
            ("core", far, slot_of(1, 1, 1), cut, rest),
        )

    def move(self, index, landing=False):
        axis, source, target, start, size = self.moves[index]
        view = self.held.at[target if landing else source, pl.ds(start, size)]
        from_block = self.block is not None and index < 5
        return pltpu.make_async_remote_copy(
            src_ref=self.block.at[pl.ds(start, size)] if from_block else view,
            dst_ref=view, send_sem=self.send.at[index],
            recv_sem=self.recv.at[index], device_id=neighbour(axis), device_id_type=MESH,
        )

    def live(self, indices):
        return [index for index in indices if self.moves[index][4]]

    def launch(self, *indices):
        for index in self.live(indices):
            self.move(index).start()

    def arrived(self, *indices):
        for index in self.live(indices):
            self.move(index, True).wait_recv()

    def run(self, work, beside):
        self.launch(0, 1, 2, 3, 4)
        beside(0)
        work(slot_of(0, 0, 0))
        self.arrived(4)
        work(slot_of(1, 0, 0))
        beside(1)
        self.arrived(0)
        self.launch(5)
        self.arrived(1)
        self.launch(6)
        self.arrived(2)
        self.launch(7)
        self.arrived(3)
        self.launch(8)
        work(slot_of(0, 0, 1))
        work(slot_of(0, 1, 0))
        self.arrived(7)
        work(slot_of(1, 0, 1))
        self.arrived(8)
        work(slot_of(1, 1, 0))
        beside(2)
        self.arrived(5)
        self.launch(9)
        self.arrived(6)
        self.launch(10)
        work(slot_of(0, 1, 1))
        self.arrived(9, 10)
        work(slot_of(1, 1, 1))

    def finish(self):
        for index in self.live(range(len(self.moves))):
            self.move(index).wait_send()


def ring_scratch(rows, depth):
    return [
        pltpu.VMEM((8, rows, depth), BF16),
        pltpu.SemaphoreType.DMA((11,)),
        pltpu.SemaphoreType.DMA((11,)),
    ]


class Stores:
    def __init__(self, sems):
        self.sems, self.made = sems, []

    def add(self, source, target):
        copy = pltpu.make_async_copy(source, target, self.sems.at[len(self.made)])
        copy.start()
        self.made.append(copy)

    def finish(self):
        for copy in self.made:
            copy.wait()


def run_beside(errands, starts, middles):
    def beside(point):
        for errand in errands:
            if point == starts:
                errand.start()
            if point == middles:
                errand.middle()

    return beside


def gather_body(dims, count, kinds, *refs):
    block_ref, refs, errands = take_errands(kinds, refs, 1 + count, 1 + count)
    weight_refs, gathered_ref, product_refs = refs[:count], refs[count], refs[count + 1 : 2 * count + 1]
    held, send, recv = refs[2 * count + 1 : 2 * count + 4]
    weights, results = refs[2 * count + 4 : 3 * count + 4], refs[3 * count + 4 : 4 * count + 4]
    (local,) = refs[4 * count + 4 :]
    own = slot_of(0, 0, 0)
    loads = [pltpu.make_async_copy(block_ref, held.at[own], local.at[0])]
    for i, (ref, weight) in enumerate(zip(weight_refs, weights)):
        loads.append(pltpu.make_async_copy(ref, weight, local.at[1 + i]))
    for load in loads:
        load.start()
    greet(bool(kinds))
    for load in loads:
        load.wait()
    ring = Ring(held, send, recv)
    stores = Stores(local.at[pl.ds(1 + count, 8 * (1 + count))])

    def work(slot):
        stores.add(held.at[slot], gathered_ref.at[slot])
        for weight, result, product_ref in zip(weights, results, product_refs):

            def column(at):
                right = weight[:, at] if dims == NN else weight[at, :]
                result[slot, :, at] = dot(held[slot], right, dims).astype(result.dtype)

            by_columns(result.shape[2], column)
            stores.add(result.at[slot], product_ref.at[slot])

    ring.run(work, run_beside(errands, 0, 2))
    ring.finish()
    stores.finish()
    for errand in errands:
        errand.finish()


def gather_multiply(block, weights, dims, collective_id, name, errands=(), out_type=F32):
    rows, depth = block.shape
    widths = [w.shape[1] if dims == NN else w.shape[0] for w in weights]
    count = len(weights)
    kinds, sources = [e[0] for e in errands], [e[1] for e in errands]
    gathered, *products = pl.pallas_call(
        functools.partial(gather_body, dims, count, kinds),
        in_specs=[pl.BlockSpec(memory_space=pl.ANY)] * (1 + count + len(kinds)),
        out_specs=[pl.BlockSpec(memory_space=pl.ANY)] * (1 + count + len(kinds)),
        out_shape=[jax.ShapeDtypeStruct((8, rows, depth), BF16)]
        + [jax.ShapeDtypeStruct((8, rows, width), out_type) for width in widths]
        + [errand_target(*errand) for errand in errands],
        scratch_shapes=ring_scratch(rows, depth)
        + [pltpu.VMEM(w.shape, BF16) for w in weights]
        + [pltpu.VMEM((8, rows, width), out_type) for width in widths]
        + [
            pltpu.SemaphoreType.DMA((1 + count + 8 * (1 + count),)),
            *errand_scratch(kinds, sources),
        ],
        compiler_params=pltpu.CompilerParams(
            collective_id=collective_id, has_side_effects=True, vmem_limit_bytes=56 * 2**20
        ),
        name=name,
    )(block, *weights, *sources)
    flat = [v.reshape(8 * rows, v.shape[2]) for v in (gathered, *products[:count])]
    return (*flat, *products[count:])


def feed_body(kinds, *refs):
    block_ref, refs, errands = take_errands(kinds, refs, 5, 4)
    sources, refs = refs[:4], refs[4:]
    gathered_ref, hidden_ref, gate_grad_ref, up_grad_ref, *refs = refs
    held, send, recv, w_gate, w_up, w_down, grads, hidden_grad, hidden, gate_grad, up_grad = refs[:11]
    (local,) = refs[11:]
    own = slot_of(0, 0, 0)
    loads = [pltpu.make_async_copy(block_ref, held.at[own], local.at[0])]
    for i, (source, target) in enumerate(zip(sources, (w_gate, w_up, w_down, grads))):
        loads.append(pltpu.make_async_copy(source, target, local.at[1 + i]))
    for load in loads:
        load.start()
    greet(bool(kinds))
    for load in loads:
        load.wait()
    ring = Ring(held, send, recv)
    stores = Stores(local.at[pl.ds(5, 32)])
    units = hidden.shape[2]

    def back(slot):
        def column(at):
            hidden_grad[slot, :, at] = dot(grads[slot], w_down[at, :], NT)

        by_columns(units, column)

    def work(slot):
        stores.add(held.at[slot], gathered_ref.at[slot])

        def column(at):
            gate = dot(held[slot], w_gate[at, :], NT)
            up = dot(held[slot], w_up[at, :], NT)
            smooth = sigmoid(gate)
            active = gate * smooth
            grad = hidden_grad[slot, :, at]
            hidden[slot, :, at] = (active * up).astype(BF16)
            gate_grad[slot, :, at] = (grad * up * smooth * (1.0 + gate * (1.0 - smooth))).astype(BF16)
            up_grad[slot, :, at] = (grad * active).astype(BF16)

        by_columns(units, column)
        stores.add(hidden.at[slot], hidden_ref.at[slot])
        stores.add(gate_grad.at[slot], gate_grad_ref.at[slot])
        stores.add(up_grad.at[slot], up_grad_ref.at[slot])

    def beside(point):
        for errand in errands:
            if point == 0:
                errand.start()
            elif point == 2:
                errand.middle()
        if point == 0:
            back(slot_of(0, 0, 0))
            back(slot_of(1, 0, 0))
        elif point == 1:
            for at in ((0, 0, 1), (0, 1, 0), (1, 0, 1), (1, 1, 0), (0, 1, 1), (1, 1, 1)):
                back(slot_of(*at))

    ring.run(work, beside)
    ring.finish()
    stores.finish()
    for errand in errands:
        errand.finish()


def feed(block, w_gate, w_up, w_down, grads, collective_id, errands=()):
    rows, depth = block.shape
    units = w_gate.shape[0]
    kinds, sources = [e[0] for e in errands], [e[1] for e in errands]
    hbm = pl.BlockSpec(memory_space=pl.ANY)
    by_unit = jax.ShapeDtypeStruct((8, rows, units), BF16)
    gathered, *parts = pl.pallas_call(
        functools.partial(feed_body, kinds),
        in_specs=[hbm] * (5 + len(kinds)),
        out_specs=[hbm] * (4 + len(kinds)),
        out_shape=[jax.ShapeDtypeStruct((8, rows, depth), BF16), by_unit, by_unit, by_unit]
        + [errand_target(*errand) for errand in errands],
        scratch_shapes=[
            *ring_scratch(rows, depth),
            *[pltpu.VMEM(w_gate.shape, BF16)] * 3,
            pltpu.VMEM((8, rows, depth), BF16),
            pltpu.VMEM((8, rows, units), F32),
            *[pltpu.VMEM((8, rows, units), BF16)] * 3,
            pltpu.SemaphoreType.DMA((37,)),
            *errand_scratch(kinds, sources),
        ],
        compiler_params=pltpu.CompilerParams(
            collective_id=collective_id, has_side_effects=True, vmem_limit_bytes=58 * 2**20
        ),
        name="feed",
    )(block, w_gate, w_up, w_down, grads, *sources)
    flat = [v.reshape(8 * rows, v.shape[2]) for v in (gathered, *parts[:3])]
    return (*flat, *parts[3:])


def block_of(ref, slot, rows):
    if len(ref.shape) == 3:
        return ref[slot]
    return ref[pl.ds(pl.multiple_of(slot * rows, rows), rows)]


def scatter_core(dims, lefts, weights, buffers, beside, cut=None):
    sending, crossing, partial, far_recv, side_recv, total, send, recv = buffers
    rows, width = total.shape
    cut = cut or rows // 2
    rest = rows - cut

    def move(index, axis, src, dst):
        return pltpu.make_async_remote_copy(
            src_ref=src, dst_ref=dst, send_sem=send.at[index], recv_sem=recv.at[index],
            device_id=neighbour(axis), device_id_type=MESH,
        )

    sends = []

    def launch(*args):
        copy = move(*args)
        copy.start()
        sends.append(copy)

    def multiply(slot, write):
        def column(at):
            value = None
            for left, weight in zip(lefts, weights):
                right = weight[:, at] if dims == NN else weight[at, :]
                term = dot(block_of(left, slot, rows), right, dims)
                value = term if value is None else value + term
            write(at, value)

        by_columns(width, column)

    places = ((1, 1), (0, 1), (1, 0), (0, 0))

    def cross(index):
        def write(at, value):
            sending[index, :, at] = value.astype(BF16)

        multiply(slot_of(1, *places[index]), write)
        launch(index, "core", sending.at[index], crossing.at[index])

    def crossed(index):
        move(index, "core", sending.at[index], crossing.at[index]).wait_recv()

    def local_sum(index):
        crossed(index)

        def write(at, value):
            partial[index, :, at] = (value + crossing[index, :, at].astype(F32)).astype(BF16)

        multiply(slot_of(0, *places[index]), write)

    first, second = pl.ds(0, cut), pl.ds(cut, rows - cut)
    cross(0)
    beside(0)
    cross(1)
    local_sum(0)
    launch(4, "x", partial.at[0, first], far_recv.at[0, first])
    if rest:
        launch(5, "zl", partial.at[0, second], far_recv.at[1, second])
    beside("far sent")
    cross(2)
    local_sum(1)
    launch(6, "x", partial.at[1, first], side_recv.at[0, first])
    local_sum(2)
    if rest:
        launch(7, "zl", partial.at[2, second], side_recv.at[1, second])
    beside("side sent")
    cross(3)
    beside(1)
    move(4, "x", partial.at[0, first], far_recv.at[0, first]).wait_recv()
    partial[2, first] = (partial[2, first].astype(F32) + far_recv[0, first].astype(F32)).astype(BF16)
    launch(8, "zl", partial.at[2, first], side_recv.at[1, first])
    if rest:
        move(5, "zl", partial.at[0, second], far_recv.at[1, second]).wait_recv()
        partial[1, second] = (partial[1, second].astype(F32) + far_recv[1, second].astype(F32)).astype(BF16)
        launch(9, "x", partial.at[1, second], side_recv.at[0, second])
    beside(2)
    crossed(3)

    def write(at, value):
        total[:, at] = value + crossing[3, :, at].astype(F32)

    multiply(slot_of(0, 0, 0), write)
    move(6, "x", partial.at[1, first], side_recv.at[0, first]).wait_recv()
    total[first] += side_recv[0, first].astype(F32)
    if rest:
        move(7, "zl", partial.at[2, second], side_recv.at[1, second]).wait_recv()
        total[second] += side_recv[1, second].astype(F32)
    beside(3)
    move(8, "zl", partial.at[2, first], side_recv.at[1, first]).wait_recv()
    total[first] += side_recv[1, first].astype(F32)
    if rest:
        move(9, "x", partial.at[1, second], side_recv.at[0, second]).wait_recv()
        total[second] += side_recv[0, second].astype(F32)
    return sends


def scatter_scratch(rows, width):
    return [
        pltpu.VMEM((4, rows, width), BF16),
        pltpu.VMEM((4, rows, width), BF16),
        pltpu.VMEM((3, rows, width), BF16),
        pltpu.VMEM((2, rows, width), BF16),
        pltpu.VMEM((2, rows, width), BF16),
        pltpu.VMEM((rows, width), F32),
        pltpu.SemaphoreType.DMA((10,)),
        pltpu.SemaphoreType.DMA((10,)),
    ]


def norm_back(values, grad, gain):
    scale = lax.rsqrt(jnp.mean(values * values, -1, keepdims=True) + 1e-05)
    scaled = grad * gain
    mean = jnp.mean(values * scaled, -1, keepdims=True)
    return scale * scaled - values * (scale * scale * scale * mean), grad * values * scale


def by_rows(rows, body, carry=0):
    def step(index, carry):
        return body(pl.ds(pl.multiple_of(index * 32, 32), 32), carry)

    return lax.fori_loop(0, rows // 32, step, carry)


def attn_tail(total, extras, outs):
    tokens, gain = extras
    resid, normed = outs

    def body(at, carry):
        values = tokens[at].astype(F32) + total[at]
        scale = lax.rsqrt(jnp.mean(values * values, -1, keepdims=True) + 1e-05)
        resid[at] = values
        normed[at] = (values * scale * gain[0:1]).astype(BF16)
        return carry

    by_rows(total.shape[0], body)


def grad_tail(total, extras, outs):
    resid, grad_rows, gain = extras
    resid_grad, attn_grad, gain_grad = outs

    def body(at, along):
        change, terms = norm_back(resid[at], total[at], gain[0:1])
        value = grad_rows[at].astype(F32) + change
        resid_grad[at] = value
        attn_grad[at] = value.astype(BF16)
        return along + jnp.sum(terms, 0, keepdims=True)

    along = by_rows(total.shape[0], body, jnp.zeros((1, total.shape[1]), F32))
    gain_grad[...] = jnp.broadcast_to(along, gain_grad.shape)


def scatter_body(dims, count, extra, out_count, tail, kinds, *refs):
    first_ref, refs, errands = take_errands(kinds, refs, 2 * count + extra, out_count)
    refs = (first_ref, *refs)
    inputs = 2 * count + extra
    out_refs, held = refs[inputs : inputs + out_count], refs[inputs + out_count :]
    operands, extras = held[: 2 * count], held[2 * count : inputs]
    outs, held = held[inputs : inputs + out_count], held[inputs + out_count :]
    buffers, local = held[:-1], held[-1]
    loads = [
        pltpu.make_async_copy(ref, place, local.at[i])
        for i, (ref, place) in enumerate(zip(refs[:inputs], (*operands, *extras)))
    ]
    for load in loads:
        load.start()
    greet(bool(kinds))
    for load in loads[: 2 * count]:
        load.wait()

    def beside(point):
        for errand in errands:
            if point == 0:
                errand.start()
            elif point == 2 and hasattr(errand, "early"):
                errand.early()
            elif point == 3:
                errand.late() if hasattr(errand, "early") else errand.middle()

    cut = SCATTER_CUT if Across in kinds or Swap in kinds else None
    sends = scatter_core(dims, operands[:count], operands[count:], buffers, beside, cut)
    for load in loads[2 * count :]:
        load.wait()
    tail(buffers[5], extras, outs)
    stores = Stores(local.at[pl.ds(inputs, out_count)])
    for place, ref in zip(outs, out_refs):
        stores.add(place, ref)
    for copy in sends:
        copy.wait_send()
    stores.finish()
    for errand in errands:
        errand.finish()


def multiply_scatter(lefts, weights, extras, outs, tail, dims, collective_id, name, errands=()):
    rows = lefts[0].shape[0] // 8
    width = weights[0].shape[1] if dims == NN else weights[0].shape[0]
    count = len(lefts)
    lefts = [left.reshape(8, rows, left.shape[1]) for left in lefts]
    kinds, sources = [e[0] for e in errands], [e[1] for e in errands]
    inputs = (*lefts, *weights, *extras)
    hbm = pl.BlockSpec(memory_space=pl.ANY)
    return pl.pallas_call(
        functools.partial(scatter_body, dims, count, len(extras), len(outs), tail, kinds),
        in_specs=[hbm] * (len(inputs) + len(kinds)),
        out_specs=[hbm] * (len(outs) + len(kinds)),
        out_shape=[*outs, *[errand_target(*errand) for errand in errands]],
        scratch_shapes=[
            *[pltpu.VMEM(v.shape, v.dtype) for v in (*inputs, *outs)],
            *scatter_scratch(rows, width),
            pltpu.SemaphoreType.DMA((len(inputs) + len(outs),)),
            *errand_scratch(kinds, sources),
        ],
        compiler_params=pltpu.CompilerParams(
            collective_id=collective_id, has_side_effects=True, vmem_limit_bytes=58 * 2**20
        ),
        name=name,
    )(*inputs, *sources)


def begin_body(kinds, *refs):
    tokens_ref, refs, errands = take_errands(kinds, refs, 8, 5)
    gain_ref, conv_ref, *refs = refs
    weight_refs, refs = refs[:5], refs[5:]
    moved_ref, gathered_ref, product_ref, weights_ref, new_conv_ref, *refs = refs
    tokens, held, weights, result, send, recv, errand_send, errand_recv, local = refs
    rows = tokens_ref.shape[0]
    half = rows // 2
    starts = [0]
    for ref in weight_refs:
        starts.append(starts[-1] + ref.shape[1])
    parts = [pl.ds(start, ref.shape[1]) for start, ref in zip(starts, weight_refs)]
    greet(True)
    own_kinds = [Exchange, Exchange] + [Swap] * 5
    targets = [tokens, new_conv_ref] + [weights.at[:, part] for part in parts]
    block, taps, *swaps = make_errands(
        own_kinds, [tokens_ref, conv_ref, *weight_refs], targets, errand_send, errand_recv, local
    )
    block.start()
    taps.start()
    block.finish()
    own = slot_of(0, 0, 0)
    values = tokens[...].astype(F32)
    scale = lax.rsqrt(jnp.mean(values * values, -1, keepdims=True) + 1e-05)
    held[own] = (values * scale * gain_ref[...]).astype(BF16)
    keep = pltpu.make_async_copy(tokens, moved_ref, local.at[7])
    keep.start()

    ring = Ring(held, send, recv, 0)
    ring.launch(0, 1, 2, 3, 4)
    for swap in swaps:
        swap.start()
    for errand in errands:
        errand.start()
    ring.arrived(0)
    ring.launch(5)
    ring.arrived(1)
    ring.launch(6)
    swaps[0].middle()
    ring.arrived(2)
    ring.launch(7)
    ring.arrived(3)
    ring.launch(8)
    swaps[1].middle()
    ring.arrived(5)
    ring.launch(9)
    ring.arrived(6)
    ring.launch(10)
    ring.arrived(4, 7, 8, 9, 10)
    store = pltpu.make_async_copy(held, gathered_ref, local.at[8])
    store.start()
    stores = []
    for index, (swap, part) in enumerate(zip(swaps, parts)):
        if index + 2 < len(swaps):
            swaps[index + 2].middle()
        swap.finish()
        if index == len(swaps) - 1:
            for errand in errands:
                errand.middle()

        def multiply(slot, _, part=part):
            result[slot, :, part] = dot(held[slot], weights[:, part], NN)
            return 0

        lax.fori_loop(0, 8, multiply, 0)
        for view, out, sem in (
            (result.at[:, :, part], product_ref.at[:, :, part], 9 + 2 * index),
            (weights.at[:, part], weights_ref.at[:, part], 10 + 2 * index),
        ):
            copy = pltpu.make_async_copy(view, out, local.at[sem])
            copy.start()
            stores.append(copy)
    taps.finish()
    ring.finish()
    keep.wait()
    store.wait()
    for copy in stores:
        copy.wait()
    for errand in errands:
        errand.finish()


def begin(tokens, gain, conv, weights, collective_id, errands=()):
    rows, depth = tokens.shape
    width = sum(w.shape[1] for w in weights)
    kinds, sources = [e[0] for e in errands], [e[1] for e in errands]
    hbm = pl.BlockSpec(memory_space=pl.ANY)
    moved, gathered, product, weights, conv, *more = pl.pallas_call(
        functools.partial(begin_body, kinds),
        in_specs=[hbm, pl.BlockSpec(memory_space=pltpu.VMEM)]
        + [hbm] * (1 + len(weights) + len(kinds)),
        out_specs=[hbm] * (5 + len(kinds)),
        out_shape=[
            jax.ShapeDtypeStruct(tokens.shape, BF16),
            jax.ShapeDtypeStruct((8, rows, depth), BF16),
            jax.ShapeDtypeStruct((8, rows, width), F32),
            jax.ShapeDtypeStruct((depth, width), BF16),
            jax.ShapeDtypeStruct(conv.shape, conv.dtype),
            *[errand_target(*errand) for errand in errands],
        ],
        scratch_shapes=[
            pltpu.VMEM((rows, depth), BF16),
            pltpu.VMEM((8, rows, depth), BF16),
            pltpu.VMEM((depth, width), BF16),
            pltpu.VMEM((8, rows, width), F32),
            pltpu.SemaphoreType.DMA((11,)),
            pltpu.SemaphoreType.DMA((11,)),
            pltpu.SemaphoreType.DMA((22,)),
            pltpu.SemaphoreType.DMA((22,)),
            pltpu.SemaphoreType.DMA((19,)),
            *errand_scratch(kinds, sources),
        ],
        compiler_params=pltpu.CompilerParams(
            collective_id=collective_id, has_side_effects=True, vmem_limit_bytes=56 * 2**20
        ),
        name="begin",
    )(tokens, gain, conv, *weights, *sources)
    flat = gathered.reshape(8 * rows, depth), product.reshape(8 * rows, width)
    return (moved, *flat, weights, conv, *more)


def turned_product(turned, right, out, columns):
    def column(at):
        out[:, at] = dot(turned[...], right[:, at], NN).astype(BF16)

    by_columns(columns, column)


def mlp_body(kinds, *refs):
    first_ref, refs, errands = take_errands(kinds, refs, 6, 5)
    sources, refs = (first_ref, *refs[:5]), refs[5:]
    total_ref, down_ref, gate_ref, up_ref, came_ref, *refs = refs
    hidden, weight, rights, lefts, turned, outs = refs[:6]
    buffers, refs = refs[6:14], refs[14:]
    half_send, half_recv, local = refs
    hidden_ref, weight_ref, grads_ref, gate_grad_ref, up_grad_ref, rows_ref = sources

    def load(source, target, index):
        return pltpu.make_async_copy(source, target, local.at[index])

    early = [
        load(hidden_ref, hidden, 0), load(weight_ref, weight, 1), load(grads_ref, rights, 2),
        load(gate_grad_ref, lefts.at[0], 3), load(up_grad_ref, lefts.at[1], 4),
    ]
    reload = load(rows_ref, rights, 5)
    for copy in early:
        copy.start()
    greet(True)
    for copy in early:
        copy.wait()
    stores = Stores(local.at[pl.ds(6, 4)])
    rows = hidden.shape[1]
    columns = rights.shape[1]

    def turn(left):
        for slot in range(8):
            turned[:, slot * rows : (slot + 1) * rows] = left[slot].T

    y = lax.axis_index("y")
    half = pltpu.make_async_remote_copy(
        src_ref=row_half(outs.at[0], 1 - y), dst_ref=came_ref, send_sem=half_send.at[0],
        recv_sem=half_recv.at[0], device_id=neighbour("y"), device_id_type=MESH,
    )

    def beside(point):
        if point == 0:
            for errand in errands:
                errand.start()
        elif point == "side sent":
            turn(hidden)
            turned_product(turned, rights, outs.at[0], columns)
            reload.start()
            half.start()
            stores.add(outs.at[0], down_ref)
        elif point == 2:
            turn(lefts.at[0])
            reload.wait()
            turned_product(turned, rights, outs.at[1], columns)
            stores.add(outs.at[1], gate_ref)
            turn(lefts.at[1])
            turned_product(turned, rights, outs.at[2], columns)
            stores.add(outs.at[2], up_ref)
            for errand in errands:
                errand.middle()

    sends = scatter_core(NN, [hidden], [weight], buffers, beside)
    stores.add(buffers[5], total_ref)
    for copy in sends:
        copy.wait_send()
    half.wait()
    stores.finish()
    for errand in errands:
        errand.finish()


def mlp_scatter(hidden, weight, grads, gate_grad, up_grad, gathered, collective_id, errands=()):
    tokens, units = hidden.shape
    rows, depth = tokens // 8, weight.shape[1]
    kinds, sources = [e[0] for e in errands], [e[1] for e in errands]
    hbm = pl.BlockSpec(memory_space=pl.ANY)
    by_unit = jax.ShapeDtypeStruct(weight.shape, BF16)
    blocks = [v.reshape(8, rows, units) for v in (hidden, gate_grad, up_grad)]
    return pl.pallas_call(
        functools.partial(mlp_body, kinds),
        in_specs=[hbm] * (6 + len(kinds)),
        out_specs=[hbm] * (5 + len(kinds)),
        out_shape=[
            jax.ShapeDtypeStruct((rows, depth), F32), by_unit, by_unit, by_unit,
            jax.ShapeDtypeStruct((units // 2, depth), BF16),
            *[errand_target(*errand) for errand in errands],
        ],
        scratch_shapes=[
            pltpu.VMEM((8, rows, units), BF16),
            pltpu.VMEM(weight.shape, BF16),
            pltpu.VMEM((tokens, depth), BF16),
            pltpu.VMEM((2, 8, rows, units), BF16),
            pltpu.VMEM((units, tokens), BF16),
            pltpu.VMEM((3, *weight.shape), BF16),
            *scatter_scratch(rows, depth),
            pltpu.SemaphoreType.DMA((1,)),
            pltpu.SemaphoreType.DMA((1,)),
            pltpu.SemaphoreType.DMA((10,)),
            *errand_scratch(kinds, sources),
        ],
        compiler_params=pltpu.CompilerParams(
            collective_id=collective_id, has_side_effects=True, vmem_limit_bytes=60 * 2**20
        ),
        name="scatter_mlp",
    )(blocks[0], weight, grads, blocks[1], blocks[2], gathered, *sources)


CHUNKS = 8


def finish_body(kinds, *refs):
    first_ref, refs, errands = take_errands(kinds, refs, 8, 4)
    left_ref, (weight_ref, rows_ref, tokens_ref, resid_ref, gain_ref) = first_ref, refs[:5]
    small_refs, tokens_grad_ref, total_grad_ref = refs[5:7], *refs[7:9]
    taps_out_ref, gains_out_ref, *refs = refs[9:]
    left, weight, gathered, turned, mine, other, came, far, tokens = refs[:9]
    resid, moving, taps, taps_recv, gains, gains_recv, *refs = refs[9:]
    buffers, refs = refs[:8], refs[8:]
    chain_send, chain_recv, sum_send, sum_recv, local = refs
    loads = [
        pltpu.make_async_copy(source, target, local.at[i])
        for i, (source, target) in enumerate(
            (
                (left_ref, left), (weight_ref, weight), (rows_ref, gathered), (tokens_ref, tokens),
                (resid_ref, resid), (small_refs[0], taps), (small_refs[1], gains),
            )
        )
    ]
    for load in loads:
        load.start()
    greet(True)
    y = lax.axis_index("y")
    moved = is_moved()
    stays = jnp.logical_not(moved)
    size = mine.shape[0] // CHUNKS

    def chain(stage, index, source, target, axis):
        return pltpu.make_async_remote_copy(
            src_ref=source, dst_ref=target, send_sem=chain_send.at[stage, index],
            recv_sem=chain_recv.at[stage, index], device_id=neighbour(axis), device_id_type=MESH,
        )

    def total_rows(index, owner):
        start = owner * (size * CHUNKS) + index * size
        return total_grad_ref.at[pl.ds(pl.multiple_of(start, 16), size)]

    def chunk(ref, index):
        return ref.at[pl.ds(index * size, size)]

    def over(index):
        return chain(0, index, chunk(other, index), chunk(came, index), "y")

    def across(index):
        return chain(1, index, chunk(mine, index), chunk(far, index), "zh")

    def back(index):
        return chain(2, index, chunk(mine, index), total_rows(index, y), "y")

    def landing(index):
        return chain(2, index, total_rows(index, 1 - y), total_rows(index, 1 - y), "y")

    def cross(index):
        return chain(3, index, chunk(mine, index), total_rows(index, y), "core")

    def pass_on(index):
        return chain(4, index, total_rows(index, 1 - y), total_rows(index, 1 - y), "core")

    def near(index):
        return pltpu.make_async_copy(chunk(mine, index), total_rows(index, y), local.at[8 + index])

    def add(index, source):
        at, more = chunk(mine, index), chunk(source, index)
        at[...] = (at[...].astype(F32) + more[...].astype(F32)).astype(BF16)

    def sum_y(index):
        over(index).wait_recv()
        add(index, came)
        pl.when(moved)(lambda: across(index).start())

    def sum_z(index):
        @pl.when(stays)
        def _():
            across(index).wait_recv()
            add(index, far)
            back(index).start()
            cross(index).start()
            near(index).start()

    def forward(index):
        @pl.when(stays)
        def _():
            landing(index).wait_recv()
            pass_on(index).start()

    def weight_grad(owner, index, target):
        start = pl.multiple_of(owner * (size * CHUNKS) + index * size, size)
        turned[...] = gathered[:, pl.ds(start, size)].T
        turned_product(turned, left, chunk(target, index), left.shape[1])

    def sum_step(values, received, first, axes, index):
        def round_of(index):
            return pltpu.make_async_remote_copy(
                src_ref=values, dst_ref=received.at[index], send_sem=sum_send.at[first + index],
                recv_sem=sum_recv.at[first + index], device_id=neighbour(axes[index]),
                device_id_type=MESH,
            )

        if index > 0:
            round_of(index - 1).wait()
            values[...] += received[index - 1]
        if index < len(axes):
            round_of(index).start()

    def taps_step(index):
        sum_step(taps, taps_recv, 0, ("y", "zh"), index)

    def gains_step(index):
        sum_step(gains, gains_recv, 2, ("zh", "y", "core", "x", "zl"), index)

    def far_part(index):
        weight_grad(1 - y, index, other)
        over(index).start()

    def near_part(index):
        weight_grad(y, index, mine)
        sum_y(index)

    for load in loads:
        load.wait()
    for errand in errands:
        errand.start()
    taps_step(0)
    far_part(0)
    far_part(1)

    def beside(point):
        if point == 0:
            far_part(2)
            far_part(3)
            taps_step(1)
        elif point == "far sent":
            far_part(4)
            far_part(5)
            near_part(0)
        elif point == "side sent":
            far_part(6)
            far_part(7)
            taps_step(2)
            near_part(1)
            for errand in errands:
                errand.middle()
        elif point == 1:
            near_part(2)
        elif point == 2:
            near_part(3)
            sum_z(0)
        elif point == 3:
            near_part(4)

    sends = scatter_core(NT, [left], [weight], buffers, beside, SCATTER_CUT)
    total = buffers[5]
    gain = gain_ref[...]

    def backward(at, along):
        change, terms = norm_back(tokens[at].astype(F32), total[at], gain)
        moving[at] = (resid[at] + change).astype(BF16)
        return along + jnp.sum(terms, 0, keepdims=True)

    along = by_rows(total.shape[0], backward, jnp.zeros((1, total.shape[1]), F32))
    wide = gains.shape[1]
    for index in range(along.shape[1] // wide):
        gains[index : index + 1, :] = along[:, index * wide : (index + 1) * wide]
    gains_step(0)
    near_part(5)
    sum_z(1)
    near_part(6)
    gains_step(1)
    stores = Stores(local.at[pl.ds(9 + CHUNKS, 3)])
    stores.add(taps, taps_out_ref)
    sum_z(2)
    near_part(7)
    stores.add(moving, tokens_grad_ref)
    gains_step(2)
    sum_z(3)
    forward(0)
    gains_step(3)
    forward(1)
    sum_z(4)
    gains_step(4)
    forward(2)
    sum_z(5)
    gains_step(5)
    stores.add(gains, gains_out_ref)
    forward(3)
    sum_z(6)
    forward(4)
    sum_z(7)
    forward(5)
    forward(6)
    forward(7)
    for copy in sends:
        copy.wait_send()
    for index in range(CHUNKS):
        over(index).wait_send()

        @pl.when(moved)
        def _(index=index):
            across(index).wait_send()
            cross(index).wait_recv()
            pass_on(index).wait_recv()

        @pl.when(stays)
        def _(index=index):
            back(index).wait_send()
            cross(index).wait_send()
            pass_on(index).wait_send()
            near(index).wait()

    for errand in errands:
        errand.finish()
    stores.finish()


def finish(
    left, weight, gathered, tokens, resid_grad, gain, taps, gains, collective_id,
    errands=(),
):
    rows, width = tokens.shape
    kinds, sources = [e[0] for e in errands], [e[1] for e in errands]
    hbm = pl.BlockSpec(memory_space=pl.ANY)
    depth, columns = weight.shape
    half = pltpu.VMEM((depth // 2, columns), BF16)
    return pl.pallas_call(
        functools.partial(finish_body, kinds),
        in_specs=[hbm] * 5 + [pl.BlockSpec(memory_space=pltpu.VMEM)] + [hbm] * (2 + len(kinds)),
        out_specs=[hbm] * (4 + len(kinds)),
        out_shape=[
            jax.ShapeDtypeStruct(tokens.shape, BF16),
            jax.ShapeDtypeStruct(weight.shape, BF16),
            jax.ShapeDtypeStruct(taps.shape, F32),
            jax.ShapeDtypeStruct(gains.shape, F32),
            *[errand_target(*errand) for errand in errands],
        ],
        scratch_shapes=[
            pltpu.VMEM(left.shape, BF16),
            pltpu.VMEM(weight.shape, BF16),
            pltpu.VMEM(gathered.shape, BF16),
            pltpu.VMEM((depth // 2 // CHUNKS, gathered.shape[0]), BF16),
            half,
            half,
            half,
            half,
            pltpu.VMEM((rows, width), BF16),
            pltpu.VMEM((rows, width), F32),
            pltpu.VMEM((rows, width), BF16),
            pltpu.VMEM(taps.shape, F32),
            pltpu.VMEM((2, *taps.shape), F32),
            pltpu.VMEM(gains.shape, F32),
            pltpu.VMEM((5, *gains.shape), F32),
            *scatter_scratch(rows, width),
            pltpu.SemaphoreType.DMA((5, CHUNKS)),
            pltpu.SemaphoreType.DMA((5, CHUNKS)),
            pltpu.SemaphoreType.DMA((7,)),
            pltpu.SemaphoreType.DMA((7,)),
            pltpu.SemaphoreType.DMA((12 + CHUNKS,)),
            *errand_scratch(kinds, sources),
        ],
        compiler_params=pltpu.CompilerParams(
            collective_id=collective_id, has_side_effects=True, vmem_limit_bytes=60 * 2**20
        ),
        name="finish",
    )(left, weight, gathered, tokens, resid_grad, gain, taps, gains, *sources)


def rms_scale(values, gain):
    return values * lax.rsqrt(jnp.mean(values * values, -1, keepdims=True) + 1e-05) * gain


def swiglu(gate, up_vals):
    return jax.nn.silu(gate) * up_vals


def left_product(left, right):
    return dot(left, right, TN)


def token_scales(group_ids, mixture_counts):
    group_cols = lax.broadcasted_iota(jnp.int32, (1, GROUPS), 1)
    counts = mixture_counts.astype(F32)
    group_scale = jnp.sqrt(jnp.mean(counts) / counts)
    return jnp.sum(jnp.where(group_ids[:, None] == group_cols, group_scale[None, :], 0.0), 1)


def mixer_weights(w_query, w_key, w_value, w_gate_mix, w_beta):
    padded = jnp.pad(w_beta, ((0, 0), (0, 128 - w_beta.shape[1])))
    return jnp.concatenate([w_query, w_key, w_value, w_gate_mix, padded], 1)


ALL = ("y", "core", "zh", "zl", "x")
SIZES = (2, 2, 2, 2, 2)


CORE_PAIRS = [(i, i ^ 8) for i in range(32)]
EXCHANGE_PAIRS = [(i, i & 19 | (i & 8) >> 1 | (i & 4) << 1) for i in range(32)]


FORWARD_PLAN = (
    (0, 0, "start"), (0, 1, "start"), (0, 2, "start"), (0, 3, "start"),
    (3, 1, "middle"), (4, 0, "early"), (5, 2, "early"), (6, 0, "middle"), (7, 2, "late"),
    (7, 0, "late"), (7, 3, "early"), (7, 3, "late_after"),
    (7, 0, "finish"), (7, 1, "finish"), (7, 2, "finish"), (7, 3, "finish"),
)
BACKWARD_PLAN = (
    (0, 0, "start"), (0, 2, "start"), (0, 0, "launch"), (0, 1, "start"), (4, 1, "middle"),
    (6, 0, "settle"), (6, 2, "launch"),
    (7, 0, "forward"), (7, 2, "settle_late"), (7, 2, "forward"),
    (7, 0, "finish"), (7, 1, "finish"), (7, 2, "finish"),
)


def halves_sum(values, came):
    rows = came.shape[0]
    mine = lax.dynamic_slice_in_dim(values, lax.axis_index("y") * rows, rows, 0)
    return (mine.astype(F32) + came.astype(F32)).astype(BF16)


def total_of(part, far):
    return (part.astype(F32) + far.astype(F32)).astype(BF16)


def shards_ring(
    tokens, group_ids, mixture_counts, grad_out, norm1_gain, w_query, w_key, w_value, w_gate_mix,
    w_beta, conv_query, conv_key, conv_value, out_gain, w_out, norm2_gain, w_gate, w_up, w_down,
):
    heads = w_beta.shape[1]
    head_cols = w_query.shape[1]
    gain = out_gain.astype(F32)[None]
    gain1 = norm1_gain.astype(F32)[None]
    conv = jnp.concatenate([conv_query, conv_key, conv_value], 1).astype(F32)
    conv = jnp.pad(conv, ((0, 4), (0, 0)))
    grad_mlp = grad_out.astype(F32) * token_scales(group_ids, mixture_counts)[:, None]
    padded_beta = jnp.pad(w_beta, ((0, 0), (0, 128 - heads)))
    tokens, gathered, projected, mix_weights, conv, grad_mlp = begin(
        tokens, gain1, conv, [w_query, w_key, w_value, w_gate_mix, padded_beta], 1,
        [(Exchange, grad_mlp.astype(BF16))],
    )
    mixed, *kept, gathered_grad, w_out, w_gate, w_up = mixer_forward(
        projected, conv, gain, heads,
        [(Gather, grad_mlp), (Swap, w_out), (Swap, w_gate.T), (Swap, w_up.T)], FORWARD_PLAN, 2,
    )
    block = jax.ShapeDtypeStruct(tokens.shape, F32)
    block_low = jax.ShapeDtypeStruct(tokens.shape, BF16)
    gain2 = jnp.broadcast_to(norm2_gain.astype(F32), (8, norm2_gain.shape[0]))
    resid, normed_mlp, w_down = multiply_scatter(
        [mixed], [w_out], [tokens, gain2], [block, block_low], attn_tail, NN, 3, "scatter_attn",
        [(Swap, w_down)],
    )
    gathered_mlp, hidden, gate_grad, up_grad = feed(
        normed_mlp, w_gate, w_up, w_down, gathered_grad, 4
    )
    gathered_grad = gathered_grad.reshape(-1, gathered_grad.shape[2])
    mlp_out, down_grad, gate_wgrad, up_wgrad, down_came = mlp_scatter(
        hidden, w_down, gathered_grad, gate_grad, up_grad, gathered_mlp, 5
    )
    output = (resid + mlp_out).astype(BF16)
    down_part = halves_sum(down_grad, down_came)
    resid_grad, attn_grad, norm2_grad, gate_came, down_far = multiply_scatter(
        [gate_grad, up_grad], [w_gate, w_up], [resid, grad_mlp, gain2],
        [block, block_low, jax.ShapeDtypeStruct(gain2.shape, F32)], grad_tail, NN, 6,
        "scatter_normed_mlp_grad", [(HalfOverY, gate_wgrad), (Across, down_part)],
    )
    gate_part = halves_sum(gate_wgrad, gate_came)
    gathered_attn, mixed_grad, up_came, gate_far, down_total = gather_multiply(
        attn_grad, [w_out], NT, 7, "gather_attn_grad",
        [(HalfOverY, up_wgrad), (Across, gate_part), (Spread, total_of(down_part, down_far))],
    )
    up_part = halves_sum(up_wgrad, up_came)
    out_grad = left_product(mixed, gathered_attn).astype(BF16)
    raw_grad, conv_grad, gain_grad, up_total, gate_total, out_total = (
        mixer_backward(
            projected, conv, gain, mixed_grad, *kept, heads,
            [
                (Chain, up_part), (Spread, total_of(gate_part, gate_far)), (FullChain, out_grad),
            ],
            BACKWARD_PLAN, 8,
        )
    )
    width = tokens.shape[1]
    wide = width // 2
    gains = jnp.concatenate(
        [
            jnp.zeros((2, wide), F32), norm2_grad[0].reshape(2, wide),
            jnp.pad(gain_grad[:1], ((0, 3), (0, wide - gain_grad.shape[1]))),
        ],
        0,
    )
    grad_tokens, mix_total, taps, gains, output = finish(
        raw_grad, mix_weights, gathered, tokens, resid_grad, gain1, conv_grad, gains, 9,
        [(Exchange, output)],
    )
    grad_tokens = lax.ppermute(grad_tokens, ALL, EXCHANGE_PAIRS)
    other_taps = lax.ppermute(taps, ALL, CORE_PAIRS)
    conv_total = jnp.where(lax.axis_index("core") == lax.axis_index("zh"), taps, other_taps)[:4]
    mix_total = mix_total.astype(F32)
    return (
        output,
        grad_tokens,
        gains[:2].reshape(width),
        mix_total[:, 0:head_cols],
        mix_total[:, head_cols : 2 * head_cols],
        mix_total[:, 2 * head_cols : 3 * head_cols],
        mix_total[:, 3 * head_cols : 4 * head_cols],
        mix_total[:, 4 * head_cols : 4 * head_cols + heads],
        conv_total[:, 0:head_cols],
        conv_total[:, head_cols : 2 * head_cols],
        conv_total[:, 2 * head_cols :],
        gains[4, :HEAD_DIM],
        out_total.astype(F32),
        gains[2:4].reshape(width),
        gate_total.astype(F32).T,
        up_total.astype(F32).T,
        down_total.astype(F32),
    )


def right_product(left, right):
    return dot(left, right, NT)


def make_fold(kept_rows, weight, piece):
    weight_grad = left_product(kept_rows, piece)
    rows_grad = right_product(piece, weight)
    return (weight_grad, rows_grad)


def make_rows(source, weight, transposed):
    if transposed:
        return right_product(source, weight)
    return jnp.dot(source, weight, preferred_element_type=F32)


def shards(
    tokens,
    group_ids,
    mixture_counts,
    grad_out,
    norm1_gain,
    w_query,
    w_key,
    w_value,
    w_gate_mix,
    w_beta,
    conv_query,
    conv_key,
    conv_value,
    out_gain,
    w_out,
    norm2_gain,
    w_gate,
    w_up,
    w_down,
):
    inputs = tokens.astype(F32)
    normed, norm1_back = jax.vjp(rms_scale, inputs, norm1_gain.astype(F32))
    gathered = lax.all_gather(normed.astype(BF16), "tp", axis=0, tiled=True)
    heads = w_beta.shape[1]
    mix_weights = mixer_weights(w_query, w_key, w_value, w_gate_mix, w_beta)
    projected = jnp.dot(gathered, mix_weights, preferred_element_type=F32)
    head_cols = w_query.shape[1]
    conv = jnp.concatenate([conv_query, conv_key, conv_value], 1).astype(F32)
    gain = out_gain.astype(F32)[None]
    mixed, *kept = mixer_forward(projected, conv, gain, heads)
    attn = lax.psum_scatter(
        make_rows(mixed, w_out, False).astype(jnp.bfloat16), "tp", scatter_dimension=0, tiled=True
    ).astype(jnp.float32)
    resid = inputs + attn
    normed_mlp, norm2_back = jax.vjp(rms_scale, resid, norm2_gain.astype(F32))
    gathered_mlp = lax.all_gather(normed_mlp.astype(BF16), "tp", axis=0, tiled=True)
    pair_weights = jnp.concatenate([w_gate, w_up], 1)
    ff_cols = w_gate.shape[1]
    paired = jnp.dot(gathered_mlp, pair_weights, preferred_element_type=F32)
    hidden_full, swiglu_back = jax.vjp(swiglu, paired[:, :ff_cols], paired[:, ff_cols:])
    hidden = hidden_full.astype(BF16)
    mlp_out = lax.psum_scatter(
        make_rows(hidden, w_down, False).astype(jnp.bfloat16), "tp", scatter_dimension=0, tiled=True
    ).astype(jnp.float32)
    output = (resid + mlp_out).astype(BF16)
    token_scale = token_scales(group_ids, mixture_counts)
    grad_rows = grad_out.astype(F32) * token_scale[:, None]
    grad_mlp = grad_rows.astype(BF16)
    grad_w_down, hidden_grad = make_fold(
        hidden, w_down, lax.all_gather(grad_mlp, "tp", axis=0, tiled=True)
    )
    gate_grad, up_grad = swiglu_back(hidden_grad)
    pair_grad = jnp.concatenate([gate_grad, up_grad], 1).astype(BF16)
    pair_weight_grad = left_product(gathered_mlp, pair_grad)
    normed_mlp_grad = lax.psum_scatter(
        make_rows(pair_grad, pair_weights, True).astype(jnp.bfloat16),
        "tp",
        scatter_dimension=0,
        tiled=True,
    ).astype(jnp.float32)
    resid_norm_grad, norm2_grad = norm2_back(normed_mlp_grad)
    resid_grad = grad_rows + resid_norm_grad
    attn_grad = resid_grad.astype(BF16)
    grad_w_out, mixed_grad = make_fold(
        mixed, w_out, lax.all_gather(attn_grad, "tp", axis=0, tiled=True)
    )
    raw_grad, conv_grad, gain_grad = mixer_backward(
        projected, conv, gain, mixed_grad, *kept, heads
    )
    mix_weight_grad = left_product(gathered, raw_grad)
    normed_grad = lax.psum_scatter(
        make_rows(raw_grad, mix_weights, True).astype(jnp.bfloat16),
        "tp",
        scatter_dimension=0,
        tiled=True,
    ).astype(jnp.float32)
    input_norm_grad, norm1_grad = norm1_back(normed_grad)
    grad_tokens = (resid_grad + input_norm_grad).astype(BF16)
    summed = (
        lax.psum(mix_weight_grad.astype(jnp.bfloat16), "dp").astype(jnp.float32),
        lax.psum(grad_w_out.astype(jnp.bfloat16), "dp").astype(jnp.float32),
        lax.psum(pair_weight_grad.astype(jnp.bfloat16), "dp").astype(jnp.float32),
        lax.psum(grad_w_down.astype(jnp.bfloat16), "dp").astype(jnp.float32),
    )
    conv_total = lax.psum(conv_grad[:4], "dp")
    gains = lax.psum((norm1_grad, gain_grad[0], norm2_grad), ("dp", "tp"))
    mix_total = summed[0]
    pair_total = summed[2]
    return (
        output,
        grad_tokens,
        gains[0],
        mix_total[:, 0:head_cols],
        mix_total[:, head_cols : 2 * head_cols],
        mix_total[:, 2 * head_cols : 3 * head_cols],
        mix_total[:, 3 * head_cols : 4 * head_cols],
        mix_total[:, 4 * head_cols : 4 * head_cols + heads],
        conv_total[:, 0:head_cols],
        conv_total[:, head_cols : 2 * head_cols],
        conv_total[:, 2 * head_cols :],
        gains[1],
        summed[1],
        gains[2],
        pair_total[:, :ff_cols],
        pair_total[:, ff_cols:],
        summed[3],
    )


def solution(mesh):
    rows, cols, all_rows = "tp", "tp", ("dp", "tp")
    body = shards
    if dict(mesh.shape) == {"dp": 4, "tp": 8}:
        mesh = Mesh(mesh.devices.reshape(SIZES), ALL)
        rows = cols = ("zh", "zl", "x")
        all_rows = ALL
        body = shards_ring
    by_row, by_col, by_token = P(rows, None), P(None, cols), P(all_rows, None)
    return jax.shard_map(
        body,
        mesh=mesh,
        in_specs=(
            by_token, P(all_rows), P(), by_token, P(), by_col, by_col, by_col, by_col, by_col,
            by_col, by_col, by_col, P(), by_row, P(), by_col, by_col, by_row,
        ),
        out_specs=(
            by_token, by_token, P(), by_col, by_col, by_col, by_col, by_col, by_col, by_col,
            by_col, P(), by_row, P(), by_col, by_col, by_row,
        ),
        check_vma=False,
    )
```

```python
import functools

import jax
import jax.numpy as jnp
from jax import lax
from jax.experimental import pallas as pl
from jax.experimental.pallas import tpu as pltpu
from jax.sharding import Mesh
from jax.sharding import PartitionSpec as P

GROUPS = 8
HEAD_DIM = 128
SPAN = 64
SEQ_LEN = 2048
TILE = 256
F32 = jnp.float32
BF16 = jnp.bfloat16
NN = ((1,), (0,))
NT = ((1,), (1,))
TN = ((0,), (0,))


def split(values):
    high = values.astype(BF16)
    return high, (values - high.astype(F32)).astype(BF16)


def dot(left, right, dims):
    return lax.dot_general(left, right, (dims, ((), ())), preferred_element_type=F32)


def product(left, right, dims):
    return (
        dot(left[0], right[0], dims)
        + (dot(left[0], right[1], dims) + dot(left[1], right[0], dims))
    )


def quick(left, right, dims):
    return dot(left[0], right[0], dims)


def rows_of(pair, start, size):
    return pair[0][start : start + size], pair[1][start : start + size]


def sigmoid(values):
    return 1.0 / (1.0 + jnp.exp(-values))


def tile_masks():
    row = lax.broadcasted_iota(jnp.int32, (TILE, TILE), 0)
    col = lax.broadcasted_iota(jnp.int32, (TILE, TILE), 1)
    return row, col


def invert_all(lowers, row, col, refine=False):
    def level(size):
        return (row // (2 * size) == col // (2 * size)) & (row // size > col // size)

    first = level(1)
    eye = jnp.where(row == col, 1.0, 0.0)
    inverses = [eye - jnp.where(first, lower, 0.0) for lower in lowers]
    size = 2
    while size < SPAN:
        mask = level(size)
        parts = [split(jnp.where(mask, lower, 0.0)) for lower in lowers]
        held = [split(inverse) for inverse in inverses]
        firsts = [quick(part, h, NN) for part, h in zip(parts, held)]
        seconds = [quick(h, split(f), NN) for h, f in zip(held, firsts)]
        inverses = [inverse - second for inverse, second in zip(inverses, seconds)]
        size *= 2
    if True:
        held = [split(inverse) for inverse in inverses]
        rest = [
            eye - inverse - product(split(lower), h, NN)
            for lower, inverse, h in zip(lowers, inverses, held)
        ]
        inverses = [
            inverse + quick(h, split(r), NN) for inverse, h, r in zip(inverses, held, rest)
        ]
    return inverses


def conv_rows(buffer, taps):
    total = taps[0:1] * buffer[pl.ds(5, TILE), :]
    for offset in range(1, 4):
        total = total + taps[offset : offset + 1] * buffer[pl.ds(5 + offset, TILE), :]
    return total


LATE_PHASES = ("middle_late", "settle_late", "late_after", "forward", "finish")


def run_errands(errands, plan, step, late):
    if not errands:
        return
    if not late:
        pl.when(step == 0)(lambda: greet(True))
    for at in sorted({entry[0] for entry in plan}):

        @pl.when(step == at)
        def _(at=at):
            for when, index, phase in plan:
                if when == at and (phase in LATE_PHASES) == late:
                    getattr(errands[index], phase)()


def errand_operands(errands):
    kinds, sources = [e[0] for e in errands], [e[1] for e in errands]
    specs = [pl.BlockSpec(memory_space=pl.ANY)] * len(errands)
    shapes = [errand_target(*errand) for errand in errands]
    return kinds, sources, specs, shapes, errand_scratch(kinds, sources) if errands else []


def mixer_params(errands, collective_id):
    extra = {"collective_id": collective_id, "has_side_effects": True} if errands else {}
    return pltpu.CompilerParams(vmem_limit_bytes=60 * 2**20, **extra)


def mixer_forward_body(heads, kinds, plan, *refs):
    first_ref, refs, errands = take_errands(kinds, refs, 3, 6) if kinds else (refs[0], refs[1:], ())
    proj_ref = first_ref
    conv_ref, gain_ref, mixed_ref, wu_ref, fresh_ref, out_ref, state_ref, inverse_ref, *refs = refs
    rows_buf, state = refs
    tile = pl.program_id(1)
    run_errands(errands, plan, tile, False)
    wide = heads * HEAD_DIM

    @pl.when(tile == 0)
    def _():
        rows_buf[0:8, :] = jnp.zeros((8, 3 * wide), F32)
        state[...] = jnp.zeros_like(state)

    @pl.when(tile > 0)
    def _():
        rows_buf[0:8, :] = rows_buf[TILE : TILE + 8, :]

    rows_buf[8 : 8 + TILE, :] = proj_ref[:, : 3 * wide]
    summed = conv_rows(rows_buf, conv_ref[...])
    active = summed * sigmoid(summed)
    row, col = tile_masks()
    same = row // SPAN == col // SPAN
    held = []
    for head in range(heads):
        lo = head * HEAD_DIM
        query = active[:, lo : lo + HEAD_DIM]
        key = active[:, wide + lo : wide + lo + HEAD_DIM]
        value = active[:, 2 * wide + lo : 2 * wide + lo + HEAD_DIM]
        beta = sigmoid(proj_ref[:, 4 * wide + head : 4 * wide + head + 1])
        query = query * (
            lax.rsqrt(jnp.sum(query * query, -1, keepdims=True) + 1e-06) * HEAD_DIM ** (-0.5)
        )
        key = key * lax.rsqrt(jnp.sum(key * key, -1, keepdims=True) + 1e-06)
        key_beta = key * beta
        held.append((split(query), split(key), key_beta, value * beta))
    lowers = [
        jnp.where(same & (row > col), product(split(key_beta), key_s, NT), 0.0)
        for _, key_s, key_beta, _ in held
    ]
    inverses = invert_all(lowers, row, col)
    boths = [
        product(split(inverse), split(jnp.concatenate([key_beta, value_beta], 1)), NN)
        for inverse, (_, _, key_beta, value_beta) in zip(inverses, held)
    ]
    scores = [
        jnp.where(same & (row >= col), product(query_s, key_s, NT), 0.0)
        for query_s, key_s, _, _ in held
    ]
    weights = [split(both[:, :HEAD_DIM]) for both in boths]
    memories = [state[head] for head in range(heads)]
    fresh_all = [[] for _ in range(heads)]
    carried_all = [[] for _ in range(heads)]
    for block in range(TILE // SPAN):
        start = block * SPAN
        for head in range(heads):
            state_ref[block, head] = memories[head]
        reads = [
            product(
                tuple(
                    jnp.concatenate([a[start : start + SPAN], b[start : start + SPAN]], 0)
                    for a, b in zip(weights[head], held[head][0])
                ),
                split(memories[head]),
                NN,
            )
            for head in range(heads)
        ]
        for head in range(heads):
            fresh_all[head].append(boths[head][start : start + SPAN, HEAD_DIM:] - reads[head][:SPAN])
            carried_all[head].append(reads[head][SPAN:])
        memories = [
            memories[head]
            + product(rows_of(held[head][1], start, SPAN), split(fresh_all[head][-1]), TN)
            for head in range(heads)
        ]
    for head in range(heads):
        lo = head * HEAD_DIM
        state[head] = memories[head]
        inverse_ref[head] = inverses[head]
        wu_ref[:, 2 * lo : 2 * lo + 2 * HEAD_DIM] = boths[head]
        fresh = jnp.concatenate(fresh_all[head], 0)
        fresh_ref[:, lo : lo + HEAD_DIM] = fresh
        out = jnp.concatenate(carried_all[head], 0)
        out = out + product(split(scores[head]), split(fresh), NN)
        out_ref[:, lo : lo + HEAD_DIM] = out
        gate = proj_ref[:, 3 * wide + lo : 3 * wide + lo + HEAD_DIM]
        scale = lax.rsqrt(jnp.mean(out * out, -1, keepdims=True) + 1e-05)
        mixed = out * scale * gain_ref[...] * (gate * sigmoid(gate))
        mixed_ref[:, lo : lo + HEAD_DIM] = mixed.astype(BF16)
    run_errands(errands, plan, tile, True)


def mixer_forward(proj, conv, gain, heads, errands=(), plan=(), collective_id=None):
    rows = proj.shape[0]
    wide = heads * HEAD_DIM
    tiles = SEQ_LEN // TILE
    seqs = rows // SEQ_LEN
    blocks = TILE // SPAN

    def at(seq, tile):
        return (seq * tiles + tile, 0)

    kinds, sources, specs, shapes, scratch = errand_operands(errands)
    return pl.pallas_call(
        functools.partial(mixer_forward_body, heads, kinds, plan),
        grid=(seqs, tiles),
        in_specs=[
            pl.BlockSpec((TILE, proj.shape[1]), at),
            pl.BlockSpec(conv.shape, lambda seq, tile: (0, 0)),
            pl.BlockSpec(gain.shape, lambda seq, tile: (0, 0)),
            *specs,
        ],
        out_specs=[
            pl.BlockSpec((TILE, wide), at),
            pl.BlockSpec((TILE, 2 * wide), at),
            pl.BlockSpec((TILE, wide), at),
            pl.BlockSpec((TILE, wide), at),
            pl.BlockSpec((blocks, heads, HEAD_DIM, HEAD_DIM), lambda s, t: (s * tiles + t, 0, 0, 0)),
            pl.BlockSpec((None, heads, TILE, TILE), lambda s, t: (s * tiles + t, 0, 0, 0)),
            *specs,
        ],
        out_shape=[
            jax.ShapeDtypeStruct((rows, wide), BF16),
            jax.ShapeDtypeStruct((rows, 2 * wide), F32),
            jax.ShapeDtypeStruct((rows, wide), F32),
            jax.ShapeDtypeStruct((rows, wide), F32),
            jax.ShapeDtypeStruct((rows // SPAN, heads, HEAD_DIM, HEAD_DIM), F32),
            jax.ShapeDtypeStruct((rows // TILE, heads, TILE, TILE), F32),
            *shapes,
        ],
        scratch_shapes=[
            pltpu.VMEM((TILE + 8, 3 * wide), F32),
            pltpu.VMEM((heads, HEAD_DIM, HEAD_DIM), F32),
            *scratch,
        ],
        compiler_params=mixer_params(errands, collective_id),
        name="mixer_forward",
    )(proj, conv, gain, *sources)


def unit_back(raw, scale, grad):
    along = jnp.sum(raw * grad, -1, keepdims=True)
    return scale * grad - raw * (scale * scale * scale * along)


def mixer_backward_body(heads, kinds, plan, *refs):
    first_ref, refs, errands = take_errands(kinds, refs, 10, 3) if kinds else (refs[0], refs[1:], ())
    proj_ref = first_ref
    before_ref, conv_ref, gain_ref, grad_ref, wu_ref, fresh_ref, out_ref, *refs = refs
    state_ref, inverse_ref, raw_grad_ref, conv_grad_ref, gain_grad_ref, *refs = refs
    rows_buf, grad_buf, state_grad = refs
    step = pl.program_id(1)
    run_errands(errands, plan, step, False)
    steps = pl.num_programs(1)
    wide = heads * HEAD_DIM

    @pl.when((step == 0) & (pl.program_id(0) == 0))
    def _():
        conv_grad_ref[...] = jnp.zeros_like(conv_grad_ref)
        gain_grad_ref[...] = jnp.zeros_like(gain_grad_ref)

    @pl.when(step == 0)
    def _():
        grad_buf[TILE : TILE + 8, :] = jnp.zeros((8, 3 * wide), F32)
        state_grad[...] = jnp.zeros_like(state_grad)

    @pl.when(step > 0)
    def _():
        grad_buf[TILE : TILE + 8, :] = grad_buf[0:8, :]

    first = step == steps - 1
    rows_buf[0:8, :] = jnp.where(first, 0.0, before_ref[:, : 3 * wide])
    rows_buf[8 : 8 + TILE, :] = proj_ref[:, : 3 * wide]
    summed = conv_rows(rows_buf, conv_ref[...])
    smooth = sigmoid(summed)
    active = summed * smooth
    slope = smooth * (1.0 + summed * (1.0 - smooth))
    row, col = tile_masks()
    same = row // SPAN == col // SPAN
    lane = lax.broadcasted_iota(jnp.int32, (TILE, HEAD_DIM), 1)
    beta_grads = jnp.zeros((TILE, HEAD_DIM), F32)
    gain_total = jnp.zeros((1, HEAD_DIM), F32)
    within = same & (row >= col)
    below = same & (row > col)
    every = range(heads)
    at = [slice(head * HEAD_DIM, (head + 1) * HEAD_DIM) for head in every]
    query_raw = [active[:, lo] for lo in at]
    key_raw = [active[:, wide : 2 * wide][:, lo] for lo in at]
    value = [active[:, 2 * wide :][:, lo] for lo in at]
    beta = [sigmoid(proj_ref[:, 4 * wide + head : 4 * wide + head + 1]) for head in every]
    query_scale = [lax.rsqrt(jnp.sum(q * q, -1, keepdims=True) + 1e-06) for q in query_raw]
    key_scale = [lax.rsqrt(jnp.sum(k * k, -1, keepdims=True) + 1e-06) for k in key_raw]
    key = [k * scale for k, scale in zip(key_raw, key_scale)]
    key_s = [split(k) for k in key]
    query_s = [
        split(q * (scale * HEAD_DIM ** (-0.5))) for q, scale in zip(query_raw, query_scale)
    ]
    out_grad_s = []
    for head, lo in enumerate(at):
        gate = proj_ref[:, 3 * wide + head * HEAD_DIM : 3 * wide + (head + 1) * HEAD_DIM]
        grad = grad_ref[:, lo]
        out = out_ref[:, lo]
        scale = lax.rsqrt(jnp.mean(out * out, -1, keepdims=True) + 1e-05)
        gate_s = sigmoid(gate)
        normed = out * scale
        gain_total = gain_total + jnp.sum(grad * normed * (gate * gate_s), 0, keepdims=True)
        gate_grad = grad * normed * gain_ref[...] * (gate_s * (1.0 + gate * (1.0 - gate_s)))
        normed_grad = grad * gain_ref[...] * (gate * gate_s)
        out_grad = scale * normed_grad - out * (
            scale * scale * scale * jnp.mean(out * normed_grad, -1, keepdims=True)
        )
        out_grad_s.append(split(out_grad))
        raw_grad_ref[:, 3 * wide + head * HEAD_DIM : 3 * wide + (head + 1) * HEAD_DIM] = (
            gate_grad.astype(BF16)
        )
    fresh_s = [split(fresh_ref[:, lo]) for lo in at]
    both_s = [split(wu_ref[:, 2 * head * HEAD_DIM : 2 * (head + 1) * HEAD_DIM]) for head in every]
    weights_s = [(high[:, :HEAD_DIM], low[:, :HEAD_DIM]) for high, low in both_s]
    scores_s = [
        split(jnp.where(within, product(query_s[h], key_s[h], NT), 0.0)) for h in every
    ]
    fresh_grad_in = [product(scores_s[h], out_grad_s[h], TN) for h in every]
    carry = [state_grad[head] for head in every]
    blocks = TILE // SPAN
    parts = [[None] * blocks for _ in every]
    for block in range(blocks - 1, -1, -1):
        start = block * SPAN
        carry_s = [split(c) for c in carry]
        fresh_grad = [
            fresh_grad_in[h][start : start + SPAN]
            + product(rows_of(key_s[h], start, SPAN), carry_s[h], NN)
            for h in every
        ]
        fresh_grad_s = [split(f) for f in fresh_grad]
        out_rows = [rows_of(out_grad_s[h], start, SPAN) for h in every]
        carry = [
            carry[h]
            + (
                product(rows_of(query_s[h], start, SPAN), out_rows[h], TN)
                - product(rows_of(weights_s[h], start, SPAN), fresh_grad_s[h], TN)
            )
            for h in every
        ]
        for h in every:
            stacked = tuple(
                jnp.concatenate([a, b], 0) for a, b in zip(out_rows[h], fresh_grad_s[h])
            )
            back = product(stacked, split(state_ref[block, h]), NT)
            through = product(rows_of(fresh_s[h], start, SPAN), carry_s[h], NT)
            parts[h][block] = (fresh_grad[h], back[:SPAN], -back[SPAN:], through)
    for h in every:
        state_grad[h] = carry[h]
    scores_grad_s = [
        split(jnp.where(within, product(out_grad_s[h], fresh_s[h], NT), 0.0)) for h in every
    ]
    joined = [
        [jnp.concatenate([part[i] for part in parts[h]], 0) for i in range(4)] for h in every
    ]
    query_grad = [joined[h][1] + product(scores_grad_s[h], key_s[h], NN) for h in every]
    key_grad = [joined[h][3] + product(scores_grad_s[h], query_s[h], TN) for h in every]
    right_grad = [
        product(
            split(inverse_ref[h]),
            split(jnp.concatenate([joined[h][2], joined[h][0]], 1)),
            TN,
        )
        for h in every
    ]
    lower_grad_s = [
        split(jnp.where(below, -product(split(right_grad[h]), both_s[h], NT), 0.0)) for h in every
    ]
    key_beta_grad = [
        right_grad[h][:, :HEAD_DIM] + product(lower_grad_s[h], key_s[h], NN) for h in every
    ]
    key_grad = [
        key_grad[h]
        + product(lower_grad_s[h], split(key[h] * beta[h]), TN)
        + key_beta_grad[h] * beta[h]
        for h in every
    ]
    for h, lo in enumerate(at):
        value_beta_grad = right_grad[h][:, HEAD_DIM:]
        beta_grad = jnp.sum(
            key_beta_grad[h] * key[h] + value_beta_grad * value[h], -1, keepdims=True
        )
        beta_grad = beta_grad * (beta[h] * (1.0 - beta[h]))
        beta_grads = jnp.where(lane == h, beta_grad, beta_grads)
        query_back = unit_back(query_raw[h], query_scale[h], query_grad[h] * HEAD_DIM ** (-0.5))
        key_back = unit_back(key_raw[h], key_scale[h], key_grad[h])
        for index, grad in enumerate((query_back, key_back, value_beta_grad * beta[h])):
            first = index * wide + h * HEAD_DIM
            grad_buf[0:TILE, first : first + HEAD_DIM] = grad * slope[:, first : first + HEAD_DIM]
    raw_grad_ref[:, 4 * wide :] = beta_grads.astype(BF16)
    gain_grad_ref[0:1, :] += gain_total
    taps = conv_ref[...]
    here = grad_buf[0:TILE, :]
    total = taps[3:4] * here
    conv_grad_ref[3:4, :] += jnp.sum(here * rows_buf[8 : 8 + TILE, :], 0, keepdims=True)
    for offset in range(3):
        total = total + taps[offset : offset + 1] * grad_buf[pl.ds(3 - offset, TILE), :]
        conv_grad_ref[offset : offset + 1, :] += jnp.sum(
            here * rows_buf[pl.ds(5 + offset, TILE), :], 0, keepdims=True
        )
    raw_grad_ref[:, : 3 * wide] = total.astype(BF16)
    run_errands(errands, plan, step, True)


def mixer_backward(
    proj, conv, gain, grad, wu, fresh, out, states, inverses, heads,
    errands=(), plan=(), collective_id=None,
):
    rows = proj.shape[0]
    wide = heads * HEAD_DIM
    tiles = SEQ_LEN // TILE
    seqs = rows // SEQ_LEN
    blocks = TILE // SPAN

    def index(seq, step):
        return seq * tiles + tiles - 1 - step

    def at(seq, step):
        return (index(seq, step), 0)

    def ahead(seq, step):
        return (jnp.maximum(index(seq, step) * (TILE // 8) - 1, 0), 0)

    def fixed(seq, step):
        return (0, 0)

    kinds, sources, specs, shapes, scratch = errand_operands(errands)
    return pl.pallas_call(
        functools.partial(mixer_backward_body, heads, kinds, plan),
        grid=(seqs, tiles),
        in_specs=[
            pl.BlockSpec((TILE, proj.shape[1]), at),
            pl.BlockSpec((8, proj.shape[1]), ahead),
            pl.BlockSpec(conv.shape, fixed),
            pl.BlockSpec(gain.shape, fixed),
            pl.BlockSpec((TILE, wide), at),
            pl.BlockSpec((TILE, 2 * wide), at),
            pl.BlockSpec((TILE, wide), at),
            pl.BlockSpec((TILE, wide), at),
            pl.BlockSpec(
                (blocks, heads, HEAD_DIM, HEAD_DIM), lambda s, t: (index(s, t), 0, 0, 0)
            ),
            pl.BlockSpec((None, heads, TILE, TILE), lambda s, t: (index(s, t), 0, 0, 0)),
            *specs,
        ],
        out_specs=[
            pl.BlockSpec((TILE, 4 * wide + 128), at),
            pl.BlockSpec((8, 3 * wide), fixed),
            pl.BlockSpec((8, HEAD_DIM), fixed),
            *specs,
        ],
        out_shape=[
            jax.ShapeDtypeStruct((rows, 4 * wide + 128), BF16),
            jax.ShapeDtypeStruct((8, 3 * wide), F32),
            jax.ShapeDtypeStruct((8, HEAD_DIM), F32),
            *shapes,
        ],
        scratch_shapes=[
            pltpu.VMEM((TILE + 8, 3 * wide), F32),
            pltpu.VMEM((TILE + 8, 3 * wide), F32),
            pltpu.VMEM((heads, HEAD_DIM, HEAD_DIM), F32),
            *scratch,
        ],
        compiler_params=mixer_params(errands, collective_id),
        name="mixer_backward",
    )(proj, proj, conv, gain, grad, wu, fresh, out, states, inverses, *sources)


MESH = pl.DeviceIdType.MESH


def place():
    return lax.axis_index("core"), lax.axis_index("zl"), lax.axis_index("x")


def slot_of(core, deep, wide):
    own_core, own_deep, own_wide = place()
    return (
        jnp.where(core, 1 - own_core, own_core) * 4
        + jnp.where(deep, 1 - own_deep, own_deep) * 2
        + jnp.where(wide, 1 - own_wide, own_wide)
    )


def on_part(outer):
    at_end = lax.axis_index("zl") == lax.axis_index("zh")
    return is_moved() & (at_end if outer else jnp.logical_not(at_end))


def is_moved():
    return lax.axis_index("core") != lax.axis_index("zh")


def greet(everyone=False):
    barrier = pltpu.get_barrier_semaphore()
    axes = ("core", "zl", "x", "y", "zh") if everyone else ("core", "zl", "x")
    for axis in axes:
        pl.semaphore_signal(barrier, inc=1, device_id=neighbour(axis), device_id_type=MESH)
    peers = len(axes)
    if everyone:
        pl.when(is_moved())(
            lambda: pl.semaphore_signal(
                barrier, inc=1, device_id=partner(), device_id_type=MESH
            )
        )
        peers = peers + is_moved().astype(jnp.int32)
    pl.semaphore_wait(barrier, peers)


def partner():
    return {"core": lax.axis_index("zh"), "zh": lax.axis_index("core")}


def row_half(ref, index):
    rows = ref.shape[0] // 2
    return ref.at[pl.ds(pl.multiple_of(index * rows, 16), rows)]


class Errand:
    sems = 1
    buffers = 1

    def __init__(self, source, target, send, recv, local, buffers=()):
        self.source, self.target, self.held = source, target, buffers
        self.stage = buffers[0] if buffers else None
        self.send, self.recv, self.local = send, recv, local
        self.y = lax.axis_index("y")

    def remote(self, index, source, target, device):
        return pltpu.make_async_remote_copy(
            src_ref=source, dst_ref=target, send_sem=self.send.at[index],
            recv_sem=self.recv.at[index], device_id=device, device_id_type=MESH,
        )

    @staticmethod
    def buffer_shape(shape):
        return shape

    def start_part(self, outer):
        if outer:
            self.start()

    def start_outer(self):
        self.start_part(True)

    def start_inner(self):
        self.start_part(False)

    def stays(self, action):
        pl.when(jnp.logical_not(is_moved()))(action)

    def own_target(self):
        return self.target

    def here(self):
        source = self.source if self.stage is None else self.stage
        return pltpu.make_async_copy(source, self.own_target(), self.local)

    def stage_in(self):
        return pltpu.make_async_copy(self.source, self.stage, self.local)

    def start_here(self):
        self.stays(lambda: (self.here() if self.stage is None else self.stage_in()).start())

    def pass_here(self):
        def action():
            self.stage_in().wait()
            self.here().start()

        if self.stage is not None:
            self.stays(action)

    def finish_here(self):
        self.stays(lambda: self.here().wait())


class Exchange(Errand):
    def far(self):
        return self.remote(0, self.source, self.target, partner())

    def start(self):
        pl.when(is_moved())(lambda: self.far().start())
        self.start_here()

    def middle(self):
        self.pass_here()

    def middle_late(self):
        self.middle()

    def finish(self):
        pl.when(is_moved())(lambda: self.far().wait())
        self.finish_here()


class Swap(Errand):
    sems = 4

    def piece(self, ref, owner, index):
        rows = ref.shape[0] // 4
        return ref.at[pl.ds(pl.multiple_of((owner * 2 + index) * rows, 16), rows)]

    def first(self, index):
        return self.remote(
            index, self.piece(self.source, self.y, index), self.piece(self.target, self.y, index),
            partner(),
        )

    def second(self, index, landing=False):
        half = self.piece(self.target, 1 - self.y if landing else self.y, index)
        return self.remote(2 + index, half, half, neighbour("y"))

    def start(self):
        self.start_part(True)
        self.start_part(False)

    def start_part(self, outer):
        @pl.when(on_part(outer))
        def _():
            self.first(0).start()
            self.first(1).start()

        if outer:
            self.start_here()

    def pass_piece(self, index):
        @pl.when(is_moved())
        def _():
            self.first(index).wait_recv()
            self.second(index).start()

    def early(self):
        self.pass_piece(0)
        self.pass_here()

    def late(self):
        self.pass_piece(1)

    def late_after(self):
        self.late()

    def middle(self):
        self.early()
        self.late()

    def finish(self):
        @pl.when(is_moved())
        def _():
            for index in range(2):
                self.first(index).wait_send()
                self.second(index).wait_send()
                self.second(index, True).wait_recv()

        self.finish_here()


class HalfOverY(Errand):
    buffers = 0

    def copy(self):
        return self.remote(0, row_half(self.source, 1 - self.y), self.target, neighbour("y"))

    def start(self):
        self.copy().start()

    def middle(self):
        pass

    def finish(self):
        self.copy().wait()


class Across(Errand):
    buffers = 0

    def copy(self):
        return self.remote(0, self.source, self.target, neighbour("zh"))

    def start(self):
        pl.when(is_moved())(lambda: self.copy().start())

    def start_part(self, outer):
        pl.when(on_part(outer))(lambda: self.copy().start())

    def middle(self):
        pass

    def finish(self):
        pl.when(is_moved())(lambda: self.copy().wait_send())
        self.stays(lambda: self.copy().wait_recv())


SCATTER_CUT = 208


class Gather(Errand):
    sems = 11

    def ring(self):
        return Ring(self.target, self.send, self.recv, 0, self.stage)

    def own(self):
        return pltpu.make_async_copy(self.stage, self.target.at[slot_of(0, 0, 0)], self.local)

    def start(self):
        self.stage_in().start()
        self.stage_in().wait()
        self.own().start()
        self.ring().launch(0, 1, 2, 3, 4)

    def early(self):
        ring = self.ring()
        ring.arrived(0)
        ring.launch(5)
        ring.arrived(1)
        ring.launch(6)

    def middle(self):
        ring = self.ring()
        ring.arrived(2)
        ring.launch(7)
        ring.arrived(3)
        ring.launch(8)

    def late(self):
        ring = self.ring()
        ring.arrived(5)
        ring.launch(9)
        ring.arrived(6)
        ring.launch(10)

    def finish(self):
        ring = self.ring()
        ring.arrived(4, 7, 8, 9, 10)
        ring.finish()
        self.own().wait()


class HalfSum(HalfOverY):
    buffers = 2

    @staticmethod
    def buffer_shape(shape):
        return (shape[0] // 2, *shape[1:])

    def copy(self):
        return self.remote(0, row_half(self.source, 1 - self.y), self.held[1], neighbour("y"))

    def load(self):
        return pltpu.make_async_copy(row_half(self.source, self.y), self.held[0], self.local)

    def start(self):
        self.copy().start()
        self.load().start()

    def store_sum(self):
        mine, more = self.held
        mine[...] = (mine[...].astype(F32) + more[...].astype(F32)).astype(BF16)
        store = pltpu.make_async_copy(mine, self.target, self.local)
        store.start()
        store.wait()

    def finish(self):
        self.copy().wait()
        self.load().wait()
        self.store_sum()


class AcrossTotal(HalfSum):
    @staticmethod
    def buffer_shape(shape):
        return shape

    def copy(self):
        return self.remote(0, self.source, self.held[1], neighbour("zh"))

    def load(self):
        return pltpu.make_async_copy(self.source, self.held[0], self.local)

    def start(self):
        pl.when(is_moved())(lambda: self.copy().start())
        self.stays(lambda: self.load().start())

    def finish(self):
        pl.when(is_moved())(lambda: self.copy().wait_send())

        @pl.when(jnp.logical_not(is_moved()))
        def _():
            self.copy().wait_recv()
            self.load().wait()
            self.store_sum()


class Spread(Errand):
    sems = 3

    def own_target(self):
        return row_half(self.target, self.y)

    def over(self):
        return self.remote(0, self.source, self.own_target(), neighbour("y"))

    def other(self, index, axis):
        view = row_half(self.target, 1 - self.y)
        return self.remote(index, view, view, neighbour(axis))

    def cross(self):
        return self.remote(1, self.source, self.own_target(), neighbour("core"))

    def start(self):
        @pl.when(jnp.logical_not(is_moved()))
        def _():
            self.over().start()
            self.cross().start()

        self.start_here()

    def middle(self):
        @pl.when(jnp.logical_not(is_moved()))
        def _():
            self.other(0, "y").wait_recv()
            self.other(2, "core").start()

        self.pass_here()

    def finish(self):
        @pl.when(jnp.logical_not(is_moved()))
        def _():
            self.over().wait_send()
            self.cross().wait_send()
            self.other(2, "core").wait_send()

        @pl.when(is_moved())
        def _():
            self.cross().wait_recv()
            self.other(2, "core").wait_recv()

        self.finish_here()


class Chain(Errand):
    sems = 5
    buffers = 2

    def mine(self):
        return self.held[0]

    def load(self):
        return pltpu.make_async_copy(self.source, self.mine(), self.local)

    def across(self):
        return self.remote(0, self.mine(), self.held[1], neighbour("zh"))

    def own_rows(self):
        return row_half(self.target, self.y)

    def near(self):
        return pltpu.make_async_copy(self.mine(), self.own_rows(), self.local)

    def over(self):
        return self.remote(1, self.mine(), self.own_rows(), neighbour("y"))

    def cross(self):
        return self.remote(2, self.mine(), self.own_rows(), neighbour("core"))

    def other(self, index, axis):
        view = row_half(self.target, 1 - self.y)
        return self.remote(index, view, view, neighbour(axis))

    def add(self, more):
        mine = self.mine()
        mine[...] = (mine[...].astype(F32) + more[...].astype(F32)).astype(BF16)

    def start(self):
        self.load().start()

    def launch(self):
        self.load().wait()
        pl.when(is_moved())(lambda: self.across().start())

    def settle(self):
        @pl.when(jnp.logical_not(is_moved()))
        def _():
            self.across().wait_recv()
            self.add(self.held[1])
            self.over().start()
            self.cross().start()
            self.near().start()

    def settle_late(self):
        self.settle()

    def forward(self):
        @pl.when(jnp.logical_not(is_moved()))
        def _():
            self.other(1, "y").wait_recv()
            self.other(3, "core").start()

    def finish(self):
        @pl.when(jnp.logical_not(is_moved()))
        def _():
            self.near().wait()
            self.over().wait_send()
            self.cross().wait_send()
            self.other(3, "core").wait_send()

        @pl.when(is_moved())
        def _():
            self.across().wait_send()
            self.cross().wait_recv()
            self.other(3, "core").wait_recv()


class FullChain(Chain):
    buffers = 3

    @staticmethod
    def buffer_shape(shape):
        return (shape[0] // 2, *shape[1:])

    def load(self):
        return pltpu.make_async_copy(row_half(self.source, self.y), self.mine(), self.local)

    def halves(self):
        return self.remote(4, row_half(self.source, 1 - self.y), self.held[2], neighbour("y"))

    def start(self):
        self.halves().start()
        self.load().start()

    def launch(self):
        self.load().wait()
        self.halves().wait()
        self.add(self.held[2])
        pl.when(is_moved())(lambda: self.across().start())


def errand_target(kind, source):
    if kind is Gather:
        return jax.ShapeDtypeStruct((8, *source.shape), source.dtype)
    rows = source.shape[0]
    rows = {HalfSum: rows // 2, Spread: 2 * rows, Chain: 2 * rows}.get(kind, rows)
    return jax.ShapeDtypeStruct((rows, *source.shape[1:]), source.dtype)


def errand_scratch(kinds, sources=()):
    total = max(1, sum(kind.sems for kind in kinds))
    places = [
        pltpu.VMEM(kind.buffer_shape(source.shape), BF16)
        for kind, source in zip(kinds, sources)
        for _ in range(kind.buffers)
    ]
    return [
        *places,
        pltpu.SemaphoreType.DMA((total,)),
        pltpu.SemaphoreType.DMA((total,)),
        pltpu.SemaphoreType.DMA((max(1, len(kinds)),)),
    ]


def make_errands(kinds, sources, targets, send, recv, local, places=()):
    made, at, used = [], 0, 0
    for index, (kind, source, target) in enumerate(zip(kinds, sources, targets)):
        view = pl.ds(at, kind.sems)
        held = places[used : used + kind.buffers] if places else ()
        made.append(kind(source, target, send.at[view], recv.at[view], local.at[index], held))
        at += kind.sems
        used += kind.buffers
    return made


def neighbour(axis):
    return {axis: 1 - lax.axis_index(axis)}


def column_tile(columns):
    for size in (512, 384, 256, 128):
        if columns % size == 0:
            return size
    return columns


def column_parts(columns):
    tile = column_tile(columns)
    if tile != columns or columns <= 512:
        return [(0, tile, columns // tile)]
    whole = columns // 256 * 256
    return [(0, 256, whole // 256), (whole, columns - whole, 1)]


def by_columns(columns, body):
    for start, size, steps in column_parts(columns):
        if steps == 1:
            body(pl.ds(start, size))
        else:

            def column(step, _, start=start, size=size):
                body(pl.ds(pl.multiple_of(start + step * size, 128), size))
                return 0

            lax.fori_loop(0, steps, column, 0)


def take_errands(kinds, refs, inputs, outputs):
    extra = len(kinds)
    sources = refs[inputs : inputs + extra]
    targets = refs[inputs + extra + outputs : inputs + 2 * extra + outputs]
    last = len(refs) - 3 - sum(kind.buffers for kind in kinds)
    errands = make_errands(kinds, sources, targets, *refs[-3:], refs[last:-3])
    rest = (
        *refs[:inputs], *refs[inputs + extra : inputs + extra + outputs],
        *refs[inputs + 2 * extra + outputs : last],
    )
    return rest[0], rest[1:], errands


class Ring:
    def __init__(self, held, send, recv, cut=None, block=None):
        self.block = block
        self.held, self.send, self.recv = held, send, recv
        own, wide, deep, far = (slot_of(0, *at) for at in ((0, 0), (0, 1), (1, 0), (1, 1)))
        rows = held.shape[1]
        cut = rows // 2 if cut is None else cut
        rest = rows - cut
        self.moves = (
            ("x", own, wide, 0, cut), ("zl", own, deep, cut, rest),
            ("x", own, wide, cut, rest), ("zl", own, deep, 0, cut),
            ("core", own, slot_of(1, 0, 0), 0, rows),
            ("zl", wide, far, 0, cut), ("x", deep, far, cut, rest),
            ("core", wide, slot_of(1, 0, 1), 0, rows),
            ("core", deep, slot_of(1, 1, 0), 0, rows),
            ("core", far, slot_of(1, 1, 1), 0, cut),
            ("core", far, slot_of(1, 1, 1), cut, rest),
        )

    def move(self, index, landing=False):
        axis, source, target, start, size = self.moves[index]
        view = self.held.at[target if landing else source, pl.ds(start, size)]
        from_block = self.block is not None and index < 5
        return pltpu.make_async_remote_copy(
            src_ref=self.block.at[pl.ds(start, size)] if from_block else view,
            dst_ref=view, send_sem=self.send.at[index],
            recv_sem=self.recv.at[index], device_id=neighbour(axis), device_id_type=MESH,
        )

    def live(self, indices):
        return [index for index in indices if self.moves[index][4]]

    def launch(self, *indices):
        for index in self.live(indices):
            self.move(index).start()

    def arrived(self, *indices):
        for index in self.live(indices):
            self.move(index, True).wait_recv()

    def run(self, work, beside):
        self.launch(0, 1, 2, 3, 4)
        beside(0)
        work(slot_of(0, 0, 0))
        self.arrived(4)
        work(slot_of(1, 0, 0))
        beside(1)
        self.arrived(0)
        self.launch(5)
        self.arrived(1)
        self.launch(6)
        self.arrived(2)
        self.launch(7)
        self.arrived(3)
        self.launch(8)
        work(slot_of(0, 0, 1))
        work(slot_of(0, 1, 0))
        self.arrived(7)
        work(slot_of(1, 0, 1))
        self.arrived(8)
        work(slot_of(1, 1, 0))
        beside(2)
        self.arrived(5)
        self.launch(9)
        self.arrived(6)
        self.launch(10)
        work(slot_of(0, 1, 1))
        self.arrived(9, 10)
        work(slot_of(1, 1, 1))

    def finish(self):
        for index in self.live(range(len(self.moves))):
            self.move(index).wait_send()


def ring_scratch(rows, depth):
    return [
        pltpu.VMEM((8, rows, depth), BF16),
        pltpu.SemaphoreType.DMA((11,)),
        pltpu.SemaphoreType.DMA((11,)),
    ]


class Stores:
    def __init__(self, sems):
        self.sems, self.made = sems, []

    def add(self, source, target):
        copy = pltpu.make_async_copy(source, target, self.sems.at[len(self.made)])
        copy.start()
        self.made.append(copy)

    def finish(self):
        for copy in self.made:
            copy.wait()


def run_beside(errands, starts, middles):
    def beside(point):
        for errand in errands:
            if point == starts:
                errand.start()
            if point == middles:
                errand.middle()

    return beside


def gather_body(dims, kinds, block_ref, *refs):
    block_ref, refs, errands = take_errands(kinds, (block_ref, *refs), 3, 2)
    weight_ref, left_ref, product_ref, grad_ref, *refs = refs
    held, send, recv, weight, result, left, turned, grad, local = refs
    own = slot_of(0, 0, 0)
    loads = [
        pltpu.make_async_copy(source, place, local.at[i])
        for i, (source, place) in enumerate(
            ((block_ref, held.at[own]), (weight_ref, weight), (left_ref, left))
        )
    ]
    for load in loads:
        load.start()
    greet(bool(kinds))
    for load in loads:
        load.wait()
    ring = Ring(held, send, recv)
    stores = Stores(local.at[pl.ds(3, 9)])
    rows, depth = block_ref.shape

    def work(slot):
        def column(at):
            right = weight[:, at] if dims == NN else weight[at, :]
            result[slot, :, at] = dot(held[slot], right, dims)

        by_columns(result.shape[2], column)
        stores.add(result.at[slot], product_ref.at[slot])

    def beside(point):
        run_beside(errands, 0, 2)(point)
        if point == 1:
            for slot in range(8):
                at = slice(slot * rows, (slot + 1) * rows)
                turned[:, at] = left[at, :].T

    ring.run(work, beside)

    def column(at):
        value = dot(turned[:, 0:rows], held[0, :, at], NN)
        for slot in range(1, 8):
            value = value + dot(
                turned[:, slot * rows : (slot + 1) * rows], held[slot, :, at], NN
            )
        grad[:, at] = value.astype(BF16)

    by_columns(depth, column)
    stores.add(grad, grad_ref)
    ring.finish()
    stores.finish()
    for errand in errands:
        errand.finish()


def gather_multiply(block, weight, left, dims, collective_id, name, errands=()):
    rows, depth = block.shape
    columns = weight.shape[1] if dims == NN else weight.shape[0]
    kinds, sources = [e[0] for e in errands], [e[1] for e in errands]
    hbm = pl.BlockSpec(memory_space=pl.ANY)
    turned = (left.shape[1], left.shape[0])
    product, grad, *more = pl.pallas_call(
        functools.partial(gather_body, dims, kinds),
        in_specs=[hbm] * (3 + len(kinds)),
        out_specs=[hbm] * (2 + len(kinds)),
        out_shape=[
            jax.ShapeDtypeStruct((8, rows, columns), F32),
            jax.ShapeDtypeStruct((left.shape[1], depth), BF16),
            *[errand_target(*errand) for errand in errands],
        ],
        scratch_shapes=[
            *ring_scratch(rows, depth),
            pltpu.VMEM(weight.shape, BF16),
            pltpu.VMEM((8, rows, columns), F32),
            pltpu.VMEM(left.shape, BF16),
            pltpu.VMEM(turned, BF16),
            pltpu.VMEM((left.shape[1], depth), BF16),
            pltpu.SemaphoreType.DMA((12,)),
            *errand_scratch(kinds, sources),
        ],
        compiler_params=pltpu.CompilerParams(
            collective_id=collective_id, has_side_effects=True, vmem_limit_bytes=60 * 2**20
        ),
        name=name,
    )(block, weight, left, *sources)
    return (product.reshape(8 * rows, columns), grad, *more)


def feed_body(kinds, *refs):
    block_ref, refs, errands = take_errands(kinds, refs, 5, 4)
    sources, refs = refs[:4], refs[4:]
    gathered_ref, hidden_ref, gate_grad_ref, up_grad_ref, *refs = refs
    held, send, recv, w_gate, w_up, w_down, grads, hidden_grad, hidden, gate_grad, up_grad = refs[:11]
    (local,) = refs[11:]
    own = slot_of(0, 0, 0)
    loads = [pltpu.make_async_copy(block_ref, held.at[own], local.at[0])]
    for i, (source, target) in enumerate(zip(sources, (w_gate, w_up, w_down, grads))):
        loads.append(pltpu.make_async_copy(source, target, local.at[1 + i]))
    for load in loads:
        load.start()
    greet(bool(kinds))
    for load in loads:
        load.wait()
    ring = Ring(held, send, recv)
    stores = Stores(local.at[pl.ds(5, 32)])
    units = hidden.shape[2]

    def back(slot):
        def column(at):
            hidden_grad[slot, :, at] = dot(grads[slot], w_down[at, :], NT)

        by_columns(units, column)

    def work(slot):
        stores.add(held.at[slot], gathered_ref.at[slot])

        def column(at):
            gate = dot(held[slot], w_gate[at, :], NT)
            up = dot(held[slot], w_up[at, :], NT)
            smooth = sigmoid(gate)
            active = gate * smooth
            grad = hidden_grad[slot, :, at]
            hidden[slot, :, at] = (active * up).astype(BF16)
            gate_grad[slot, :, at] = (grad * up * smooth * (1.0 + gate * (1.0 - smooth))).astype(BF16)
            up_grad[slot, :, at] = (grad * active).astype(BF16)

        by_columns(units, column)
        stores.add(hidden.at[slot], hidden_ref.at[slot])
        stores.add(gate_grad.at[slot], gate_grad_ref.at[slot])
        stores.add(up_grad.at[slot], up_grad_ref.at[slot])

    def beside(point):
        for errand in errands:
            if point == 0:
                errand.start()
            elif point == 2:
                errand.middle()
        if point == 0:
            back(slot_of(0, 0, 0))
            back(slot_of(1, 0, 0))
        elif point == 1:
            for at in ((0, 0, 1), (0, 1, 0), (1, 0, 1), (1, 1, 0), (0, 1, 1), (1, 1, 1)):
                back(slot_of(*at))

    ring.run(work, beside)
    ring.finish()
    stores.finish()
    for errand in errands:
        errand.finish()


def feed(block, w_gate, w_up, w_down, grads, collective_id, errands=()):
    rows, depth = block.shape
    units = w_gate.shape[0]
    kinds, sources = [e[0] for e in errands], [e[1] for e in errands]
    hbm = pl.BlockSpec(memory_space=pl.ANY)
    by_unit = jax.ShapeDtypeStruct((8, rows, units), BF16)
    gathered, *parts = pl.pallas_call(
        functools.partial(feed_body, kinds),
        in_specs=[hbm] * (5 + len(kinds)),
        out_specs=[hbm] * (4 + len(kinds)),
        out_shape=[jax.ShapeDtypeStruct((8, rows, depth), BF16), by_unit, by_unit, by_unit]
        + [errand_target(*errand) for errand in errands],
        scratch_shapes=[
            *ring_scratch(rows, depth),
            *[pltpu.VMEM(w_gate.shape, BF16)] * 3,
            pltpu.VMEM((8, rows, depth), BF16),
            pltpu.VMEM((8, rows, units), F32),
            *[pltpu.VMEM((8, rows, units), BF16)] * 3,
            pltpu.SemaphoreType.DMA((37,)),
            *errand_scratch(kinds, sources),
        ],
        compiler_params=pltpu.CompilerParams(
            collective_id=collective_id, has_side_effects=True, vmem_limit_bytes=60 * 2**20
        ),
        name="feed",
    )(block, w_gate, w_up, w_down, grads, *sources)
    flat = [v.reshape(8 * rows, v.shape[2]) for v in (gathered, *parts[:3])]
    return (*flat, *parts[3:])


def block_of(ref, slot, rows):
    if len(ref.shape) == 3:
        return ref[slot]
    return ref[pl.ds(pl.multiple_of(slot * rows, rows), rows)]


def scatter_core(dims, lefts, weights, buffers, beside, cut=None):
    sending, crossing, partial, far_recv, side_recv, total, send, recv = buffers
    rows, width = total.shape
    cut = cut or rows // 2
    rest = rows - cut

    def move(index, axis, src, dst):
        return pltpu.make_async_remote_copy(
            src_ref=src, dst_ref=dst, send_sem=send.at[index], recv_sem=recv.at[index],
            device_id=neighbour(axis), device_id_type=MESH,
        )

    sends = []

    def launch(*args):
        copy = move(*args)
        copy.start()
        sends.append(copy)

    def multiply(slot, write):
        def column(at):
            value = None
            for left, weight in zip(lefts, weights):
                right = weight[:, at] if dims == NN else weight[at, :]
                term = dot(block_of(left, slot, rows), right, dims)
                value = term if value is None else value + term
            write(at, value)

        by_columns(width, column)

    places = ((1, 1), (0, 1), (1, 0), (0, 0))

    def cross(index):
        def write(at, value):
            sending[index, :, at] = value.astype(BF16)

        multiply(slot_of(1, *places[index]), write)
        launch(index, "core", sending.at[index], crossing.at[index])

    def crossed(index):
        move(index, "core", sending.at[index], crossing.at[index]).wait_recv()

    def local_sum(index):
        crossed(index)

        def write(at, value):
            partial[index, :, at] = (value + crossing[index, :, at].astype(F32)).astype(BF16)

        multiply(slot_of(0, *places[index]), write)

    first, second = pl.ds(0, cut), pl.ds(cut, rows - cut)
    cross(0)
    beside(0)
    cross(1)
    local_sum(0)
    launch(4, "x", partial.at[0, first], far_recv.at[0, first])
    if rest:
        launch(5, "zl", partial.at[0, second], far_recv.at[1, second])
    beside("far sent")
    cross(2)
    local_sum(1)
    launch(6, "x", partial.at[1, first], side_recv.at[0, first])
    local_sum(2)
    if rest:
        launch(7, "zl", partial.at[2, second], side_recv.at[1, second])
    beside("side sent")
    cross(3)
    beside(1)
    move(4, "x", partial.at[0, first], far_recv.at[0, first]).wait_recv()
    partial[2, first] = (partial[2, first].astype(F32) + far_recv[0, first].astype(F32)).astype(BF16)
    launch(8, "zl", partial.at[2, first], side_recv.at[1, first])
    if rest:
        move(5, "zl", partial.at[0, second], far_recv.at[1, second]).wait_recv()
        partial[1, second] = (partial[1, second].astype(F32) + far_recv[1, second].astype(F32)).astype(BF16)
        launch(9, "x", partial.at[1, second], side_recv.at[0, second])
    beside(2)
    crossed(3)

    def write(at, value):
        total[:, at] = value + crossing[3, :, at].astype(F32)

    multiply(slot_of(0, 0, 0), write)
    move(6, "x", partial.at[1, first], side_recv.at[0, first]).wait_recv()
    total[first] += side_recv[0, first].astype(F32)
    if rest:
        move(7, "zl", partial.at[2, second], side_recv.at[1, second]).wait_recv()
        total[second] += side_recv[1, second].astype(F32)
    beside(3)
    move(8, "zl", partial.at[2, first], side_recv.at[1, first]).wait_recv()
    total[first] += side_recv[1, first].astype(F32)
    if rest:
        move(9, "x", partial.at[1, second], side_recv.at[0, second]).wait_recv()
        total[second] += side_recv[0, second].astype(F32)
    return sends


def scatter_scratch(rows, width):
    return [
        pltpu.VMEM((4, rows, width), BF16),
        pltpu.VMEM((4, rows, width), BF16),
        pltpu.VMEM((3, rows, width), BF16),
        pltpu.VMEM((2, rows, width), BF16),
        pltpu.VMEM((2, rows, width), BF16),
        pltpu.VMEM((rows, width), F32),
        pltpu.SemaphoreType.DMA((10,)),
        pltpu.SemaphoreType.DMA((10,)),
    ]


def norm_back(values, grad, gain):
    scale = lax.rsqrt(jnp.mean(values * values, -1, keepdims=True) + 1e-05)
    scaled = grad * gain
    mean = jnp.mean(values * scaled, -1, keepdims=True)
    return scale * scaled - values * (scale * scale * scale * mean), grad * values * scale


def by_rows(rows, body, carry=0):
    def step(index, carry):
        return body(pl.ds(pl.multiple_of(index * 32, 32), 32), carry)

    return lax.fori_loop(0, rows // 32, step, carry)


def attn_tail(total, extras, outs):
    tokens, gain = extras
    resid, normed = outs

    def body(at, carry):
        values = tokens[at].astype(F32) + total[at]
        scale = lax.rsqrt(jnp.mean(values * values, -1, keepdims=True) + 1e-05)
        resid[at] = values
        normed[at] = (values * scale * gain[0:1]).astype(BF16)
        return carry

    by_rows(total.shape[0], body)


def grad_tail(total, extras, outs):
    resid, grad_rows, gain = extras[:3]
    resid_grad, attn_grad, gain_grad = outs[:3]

    def body(at, along):
        change, terms = norm_back(resid[at], total[at], gain[0:1])
        value = grad_rows[at].astype(F32) + change
        resid_grad[at] = value
        attn_grad[at] = value.astype(BF16)
        return along + jnp.sum(terms, 0, keepdims=True)

    along = by_rows(total.shape[0], body, jnp.zeros((1, total.shape[1]), F32))
    gain_grad[...] = jnp.broadcast_to(along, gain_grad.shape)


def scatter_body(dims, count, extra, out_count, tail, with_grad, kinds, *refs):
    first_ref, refs, errands = take_errands(kinds, refs, 2 * count + extra, out_count)
    refs = (first_ref, *refs)
    inputs = 2 * count + extra
    out_refs, held = refs[inputs : inputs + out_count], refs[inputs + out_count :]
    operands, extras = held[: 2 * count], held[2 * count : inputs]
    outs, held = held[inputs : inputs + out_count], held[inputs + out_count :]
    buffers, local = held[:8], held[8]
    loads = [
        pltpu.make_async_copy(ref, place, local.at[i])
        for i, (ref, place) in enumerate(zip(refs[:inputs], (*operands, *extras)))
    ]
    for load in loads:
        load.start()
    greet(bool(kinds))
    for load in loads[: 2 * count]:
        load.wait()

    def beside(point):
        for errand in errands:
            if point == 0:
                errand.start()
            elif point == 2 and hasattr(errand, "early"):
                errand.early()
            elif point == 3:
                errand.late() if hasattr(errand, "early") else errand.middle()
        if point == 2 and with_grad:
            turned, left = held[9], operands[count - 1]
            rows = left.shape[1]
            for slot in range(8):
                turned[:, slot * rows : (slot + 1) * rows] = left[slot].T
            loads[-1].wait()
            turned_product(turned, extras[-1], outs[-1], outs[-1].shape[1])

    cut = SCATTER_CUT if AcrossTotal in kinds or Swap in kinds else None
    sends = scatter_core(dims, operands[:count], operands[count:], buffers, beside, cut)
    for load in loads[2 * count : len(loads) - with_grad]:
        load.wait()
    tail(buffers[5], extras, outs)
    stores = Stores(local.at[pl.ds(inputs, out_count)])
    for place, ref in zip(outs, out_refs):
        stores.add(place, ref)
    for copy in sends:
        copy.wait_send()
    stores.finish()
    for errand in errands:
        errand.finish()


def multiply_scatter(
    lefts, weights, extras, outs, tail, dims, collective_id, name, errands=(), right=None,
):
    rows = lefts[0].shape[0] // 8
    width = weights[0].shape[1] if dims == NN else weights[0].shape[0]
    count = len(lefts)
    lefts = [left.reshape(8, rows, left.shape[1]) for left in lefts]
    kinds, sources = [e[0] for e in errands], [e[1] for e in errands]
    turned = []
    if right is not None:
        extras = (*extras, right)
        units = lefts[-1].shape[2]
        outs = (*outs, jax.ShapeDtypeStruct((units, right.shape[1]), BF16))
        turned = [pltpu.VMEM((units, right.shape[0]), BF16)]
    inputs = (*lefts, *weights, *extras)
    hbm = pl.BlockSpec(memory_space=pl.ANY)
    return pl.pallas_call(
        functools.partial(
            scatter_body, dims, count, len(extras), len(outs), tail, right is not None, kinds
        ),
        in_specs=[hbm] * (len(inputs) + len(kinds)),
        out_specs=[hbm] * (len(outs) + len(kinds)),
        out_shape=[*outs, *[errand_target(*errand) for errand in errands]],
        scratch_shapes=[
            *[pltpu.VMEM(v.shape, v.dtype) for v in (*inputs, *outs)],
            *scatter_scratch(rows, width),
            pltpu.SemaphoreType.DMA((len(inputs) + len(outs),)),
            *turned,
            *errand_scratch(kinds, sources),
        ],
        compiler_params=pltpu.CompilerParams(
            collective_id=collective_id, has_side_effects=True, vmem_limit_bytes=60 * 2**20
        ),
        name=name,
    )(*inputs, *sources)


def begin_body(kinds, *refs):
    tokens_ref, refs, errands = take_errands(kinds, refs, 8, 5)
    gain_ref, conv_ref, *refs = refs
    weight_refs, refs = refs[:5], refs[5:]
    moved_ref, gathered_ref, product_ref, weights_ref, new_conv_ref, *refs = refs
    tokens, held, weights, result, send, recv, errand_send, errand_recv, local = refs
    rows = tokens_ref.shape[0]
    half = rows // 2
    starts = [0]
    for ref in weight_refs:
        starts.append(starts[-1] + ref.shape[1])
    parts = [pl.ds(start, ref.shape[1]) for start, ref in zip(starts, weight_refs)]
    greet(True)
    own_kinds = [Exchange, Exchange] + [Swap] * 5
    targets = [tokens, new_conv_ref] + [weights.at[:, part] for part in parts]
    block, taps, *swaps = make_errands(
        own_kinds, [tokens_ref, conv_ref, *weight_refs], targets, errand_send, errand_recv, local
    )
    block.start()
    taps.start()
    block.finish()
    own = slot_of(0, 0, 0)
    values = tokens[...].astype(F32)
    scale = lax.rsqrt(jnp.mean(values * values, -1, keepdims=True) + 1e-05)
    held[own] = (values * scale * gain_ref[...]).astype(BF16)
    keep = pltpu.make_async_copy(tokens, moved_ref, local.at[7])
    keep.start()

    ring = Ring(held, send, recv, 0)
    ring.launch(0, 1, 2, 3, 4)
    for swap in swaps:
        swap.start()
    for errand in errands:
        errand.start()
    ring.arrived(0)
    ring.launch(5)
    ring.arrived(1)
    ring.launch(6)
    swaps[0].middle()
    ring.arrived(2)
    ring.launch(7)
    ring.arrived(3)
    ring.launch(8)
    swaps[1].middle()
    ring.arrived(5)
    ring.launch(9)
    ring.arrived(6)
    ring.launch(10)
    ring.arrived(4, 7, 8, 9, 10)
    store = pltpu.make_async_copy(held, gathered_ref, local.at[8])
    store.start()
    stores = []
    for index, (swap, part) in enumerate(zip(swaps, parts)):
        if index + 2 < len(swaps):
            swaps[index + 2].middle()
        swap.finish()
        if index == len(swaps) - 1:
            for errand in errands:
                errand.middle()

        def multiply(slot, _, part=part):
            result[slot, :, part] = dot(held[slot], weights[:, part], NN)
            return 0

        lax.fori_loop(0, 8, multiply, 0)
        for view, out, sem in (
            (result.at[:, :, part], product_ref.at[:, :, part], 9 + 2 * index),
            (weights.at[:, part], weights_ref.at[:, part], 10 + 2 * index),
        ):
            copy = pltpu.make_async_copy(view, out, local.at[sem])
            copy.start()
            stores.append(copy)
    taps.finish()
    ring.finish()
    keep.wait()
    store.wait()
    for copy in stores:
        copy.wait()
    for errand in errands:
        errand.finish()


def begin(tokens, gain, conv, weights, collective_id, errands=()):
    rows, depth = tokens.shape
    width = sum(w.shape[1] for w in weights)
    kinds, sources = [e[0] for e in errands], [e[1] for e in errands]
    hbm = pl.BlockSpec(memory_space=pl.ANY)
    moved, gathered, product, weights, conv, *more = pl.pallas_call(
        functools.partial(begin_body, kinds),
        in_specs=[hbm, pl.BlockSpec(memory_space=pltpu.VMEM)]
        + [hbm] * (1 + len(weights) + len(kinds)),
        out_specs=[hbm] * (5 + len(kinds)),
        out_shape=[
            jax.ShapeDtypeStruct(tokens.shape, BF16),
            jax.ShapeDtypeStruct((8, rows, depth), BF16),
            jax.ShapeDtypeStruct((8, rows, width), F32),
            jax.ShapeDtypeStruct((depth, width), BF16),
            jax.ShapeDtypeStruct(conv.shape, conv.dtype),
            *[errand_target(*errand) for errand in errands],
        ],
        scratch_shapes=[
            pltpu.VMEM((rows, depth), BF16),
            pltpu.VMEM((8, rows, depth), BF16),
            pltpu.VMEM((depth, width), BF16),
            pltpu.VMEM((8, rows, width), F32),
            pltpu.SemaphoreType.DMA((11,)),
            pltpu.SemaphoreType.DMA((11,)),
            pltpu.SemaphoreType.DMA((22,)),
            pltpu.SemaphoreType.DMA((22,)),
            pltpu.SemaphoreType.DMA((19,)),
            *errand_scratch(kinds, sources),
        ],
        compiler_params=pltpu.CompilerParams(
            collective_id=collective_id, has_side_effects=True, vmem_limit_bytes=60 * 2**20
        ),
        name="begin",
    )(tokens, gain, conv, *weights, *sources)
    flat = gathered.reshape(8 * rows, depth), product.reshape(8 * rows, width)
    return (moved, *flat, weights, conv, *more)


def turned_product(turned, right, out, columns):
    def column(at):
        out[:, at] = dot(turned[...], right[:, at], NN).astype(BF16)

    by_columns(columns, column)


def mlp_body(kinds, *refs):
    first_ref, refs, errands = take_errands(kinds, refs, 6, 3)
    sources, refs = (first_ref, *refs[:5]), refs[5:]
    output_ref, gate_ref, part_ref, *refs = refs
    hidden, weight, rights, gate_grad, turned, outs, came, resid, output = refs[:9]
    buffers, refs = refs[9:17], refs[17:]
    half_send, half_recv, local = refs
    hidden_ref, weight_ref, grads_ref, gate_grad_ref, rows_ref, resid_ref = sources

    def load(source, target, index):
        return pltpu.make_async_copy(source, target, local.at[index])

    early = [
        load(hidden_ref, hidden, 0), load(weight_ref, weight, 1), load(grads_ref, rights, 2),
        load(gate_grad_ref, gate_grad, 3), load(resid_ref, resid, 5),
    ]
    reload = load(rows_ref, rights, 4)
    for copy in early:
        copy.start()
    greet(True)
    for copy in early:
        copy.wait()
    stores = Stores(local.at[pl.ds(6, 4)])
    rows = hidden.shape[1]
    columns = rights.shape[1]

    def turn(left):
        for slot in range(8):
            turned[:, slot * rows : (slot + 1) * rows] = left[slot].T

    y = lax.axis_index("y")
    half = pltpu.make_async_remote_copy(
        src_ref=row_half(outs.at[0], 1 - y), dst_ref=came, send_sem=half_send.at[0],
        recv_sem=half_recv.at[0], device_id=neighbour("y"), device_id_type=MESH,
    )

    def beside(point):
        if point == 0:
            for errand in errands:
                errand.start()
        elif point == "far sent":
            turn(hidden)
            turned_product(turned, rights, outs.at[0], columns)
            reload.start()
            half.start()
        elif point == 2:
            turn(gate_grad)
            reload.wait()
            turned_product(turned, rights, outs.at[1], columns)
            stores.add(outs.at[1], gate_ref)
            for errand in errands:
                errand.middle()

    sends = scatter_core(NN, [hidden], [weight], buffers, beside)
    total = buffers[5]

    def body(at, carry):
        output[at] = (resid[at] + total[at]).astype(BF16)
        return carry

    by_rows(rows, body)
    stores.add(output, output_ref)
    for copy in sends:
        copy.wait_send()
    half.wait()
    part = row_half(outs.at[0], y)
    part[...] = (part[...].astype(F32) + came[...].astype(F32)).astype(BF16)
    stores.add(part, part_ref)
    stores.finish()
    for errand in errands:
        errand.finish()


def mlp_scatter(hidden, weight, grads, gate_grad, gathered, resid, collective_id, errands=()):
    tokens, units = hidden.shape
    rows, depth = tokens // 8, weight.shape[1]
    kinds, sources = [e[0] for e in errands], [e[1] for e in errands]
    hbm = pl.BlockSpec(memory_space=pl.ANY)
    by_unit = jax.ShapeDtypeStruct(weight.shape, BF16)
    blocks = [v.reshape(8, rows, units) for v in (hidden, gate_grad)]
    return pl.pallas_call(
        functools.partial(mlp_body, kinds),
        in_specs=[hbm] * (6 + len(kinds)),
        out_specs=[hbm] * (3 + len(kinds)),
        out_shape=[
            jax.ShapeDtypeStruct((rows, depth), BF16), by_unit,
            jax.ShapeDtypeStruct((units // 2, depth), BF16),
            *[errand_target(*errand) for errand in errands],
        ],
        scratch_shapes=[
            pltpu.VMEM((8, rows, units), BF16),
            pltpu.VMEM(weight.shape, BF16),
            pltpu.VMEM((tokens, depth), BF16),
            pltpu.VMEM((8, rows, units), BF16),
            pltpu.VMEM((units, tokens), BF16),
            pltpu.VMEM((2, *weight.shape), BF16),
            pltpu.VMEM((units // 2, depth), BF16),
            pltpu.VMEM((rows, depth), F32),
            pltpu.VMEM((rows, depth), BF16),
            *scatter_scratch(rows, depth),
            pltpu.SemaphoreType.DMA((1,)),
            pltpu.SemaphoreType.DMA((1,)),
            pltpu.SemaphoreType.DMA((10,)),
            *errand_scratch(kinds, sources),
        ],
        compiler_params=pltpu.CompilerParams(
            collective_id=collective_id, has_side_effects=True, vmem_limit_bytes=60 * 2**20
        ),
        name="scatter_mlp",
    )(blocks[0], weight, grads, blocks[1], gathered, resid, *sources)


CHUNKS = 8


def finish_body(kinds, *refs):
    first_ref, refs, errands = take_errands(kinds, refs, 8, 4)
    left_ref, (weight_ref, rows_ref, tokens_ref, resid_ref, gain_ref) = first_ref, refs[:5]
    small_refs, tokens_grad_ref, total_grad_ref = refs[5:7], *refs[7:9]
    taps_out_ref, gains_out_ref, *refs = refs[9:]
    left, weight, gathered, turned, mine, other, came, far, tokens = refs[:9]
    resid, moving, taps, taps_recv, gains, gains_recv, *refs = refs[9:]
    buffers, refs = refs[:8], refs[8:]
    chain_send, chain_recv, sum_send, sum_recv, local = refs
    loads = [
        pltpu.make_async_copy(source, target, local.at[i])
        for i, (source, target) in enumerate(
            (
                (left_ref, left), (weight_ref, weight), (rows_ref, gathered), (tokens_ref, tokens),
                (resid_ref, resid), (small_refs[0], taps), (small_refs[1], gains),
            )
        )
    ]
    for load in loads:
        load.start()
    greet(True)
    y = lax.axis_index("y")
    moved = is_moved()
    stays = jnp.logical_not(moved)
    size = mine.shape[0] // CHUNKS

    def chain(stage, index, source, target, axis):
        return pltpu.make_async_remote_copy(
            src_ref=source, dst_ref=target, send_sem=chain_send.at[stage, index],
            recv_sem=chain_recv.at[stage, index], device_id=neighbour(axis), device_id_type=MESH,
        )

    def total_rows(index, owner):
        start = owner * (size * CHUNKS) + index * size
        return total_grad_ref.at[pl.ds(pl.multiple_of(start, 16), size)]

    def chunk(ref, index):
        return ref.at[pl.ds(index * size, size)]

    def over(index):
        return chain(0, index, chunk(other, index), chunk(came, index), "y")

    def across(index):
        return chain(1, index, chunk(mine, index), chunk(far, index), "zh")

    def back(index):
        return chain(2, index, chunk(mine, index), total_rows(index, y), "y")

    def landing(index):
        return chain(2, index, total_rows(index, 1 - y), total_rows(index, 1 - y), "y")

    def cross(index):
        return chain(3, index, chunk(mine, index), total_rows(index, y), "core")

    def pass_on(index):
        return chain(4, index, total_rows(index, 1 - y), total_rows(index, 1 - y), "core")

    def near(index):
        return pltpu.make_async_copy(chunk(mine, index), total_rows(index, y), local.at[8 + index])

    def add(index, source):
        at, more = chunk(mine, index), chunk(source, index)
        at[...] = (at[...].astype(F32) + more[...].astype(F32)).astype(BF16)

    def sum_y(index):
        over(index).wait_recv()
        add(index, came)
        pl.when(moved)(lambda: across(index).start())

    def sum_z(index):
        @pl.when(stays)
        def _():
            across(index).wait_recv()
            add(index, far)
            back(index).start()
            cross(index).start()
            near(index).start()

    def forward(index):
        @pl.when(stays)
        def _():
            landing(index).wait_recv()
            pass_on(index).start()

    def weight_grad(owner, index, target):
        start = pl.multiple_of(owner * (size * CHUNKS) + index * size, size)
        turned[...] = gathered[:, pl.ds(start, size)].T
        turned_product(turned, left, chunk(target, index), left.shape[1])

    def sum_step(values, received, first, axes, index):
        def round_of(index):
            return pltpu.make_async_remote_copy(
                src_ref=values, dst_ref=received.at[index], send_sem=sum_send.at[first + index],
                recv_sem=sum_recv.at[first + index], device_id=neighbour(axes[index]),
                device_id_type=MESH,
            )

        if index > 0:
            round_of(index - 1).wait()
            values[...] += received[index - 1]
        if index < len(axes):
            round_of(index).start()

    def taps_step(index):
        sum_step(taps, taps_recv, 0, ("y", "zh"), index)

    def gains_step(index):
        sum_step(gains, gains_recv, 2, ("zh", "y", "core", "x", "zl"), index)

    def far_part(index):
        weight_grad(1 - y, index, other)
        over(index).start()

    def near_part(index):
        weight_grad(y, index, mine)
        sum_y(index)

    for load in loads:
        load.wait()
    for errand in errands:
        errand.start()
    taps_step(0)
    far_part(0)
    far_part(1)

    def beside(point):
        if point == 0:
            far_part(2)
            far_part(3)
            taps_step(1)
        elif point == "far sent":
            far_part(4)
            far_part(5)
            near_part(0)
        elif point == "side sent":
            far_part(6)
            far_part(7)
            taps_step(2)
            near_part(1)
            for errand in errands:
                errand.middle()
        elif point == 1:
            near_part(2)
        elif point == 2:
            near_part(3)
            sum_z(0)
        elif point == 3:
            near_part(4)

    sends = scatter_core(NT, [left], [weight], buffers, beside, 224)
    total = buffers[5]
    gain = gain_ref[...]

    def backward(at, along):
        change, terms = norm_back(tokens[at].astype(F32), total[at], gain)
        moving[at] = (resid[at] + change).astype(BF16)
        return along + jnp.sum(terms, 0, keepdims=True)

    along = by_rows(total.shape[0], backward, jnp.zeros((1, total.shape[1]), F32))
    wide = gains.shape[1]
    for index in range(along.shape[1] // wide):
        gains[index : index + 1, :] = along[:, index * wide : (index + 1) * wide]
    gains_step(0)
    near_part(5)
    sum_z(1)
    near_part(6)
    gains_step(1)
    stores = Stores(local.at[pl.ds(9 + CHUNKS, 3)])
    stores.add(taps, taps_out_ref)
    sum_z(2)
    near_part(7)
    stores.add(moving, tokens_grad_ref)
    gains_step(2)
    sum_z(3)
    forward(0)
    gains_step(3)
    forward(1)
    sum_z(4)
    gains_step(4)
    forward(2)
    sum_z(5)
    gains_step(5)
    stores.add(gains, gains_out_ref)
    forward(3)
    sum_z(6)
    forward(4)
    sum_z(7)
    forward(5)
    forward(6)
    forward(7)
    for copy in sends:
        copy.wait_send()
    for index in range(CHUNKS):
        over(index).wait_send()

        @pl.when(moved)
        def _(index=index):
            across(index).wait_send()
            cross(index).wait_recv()
            pass_on(index).wait_recv()

        @pl.when(stays)
        def _(index=index):
            back(index).wait_send()
            cross(index).wait_send()
            pass_on(index).wait_send()
            near(index).wait()

    for errand in errands:
        errand.finish()
    stores.finish()


def finish(
    left, weight, gathered, tokens, resid_grad, gain, taps, gains, collective_id,
    errands=(),
):
    rows, width = tokens.shape
    kinds, sources = [e[0] for e in errands], [e[1] for e in errands]
    hbm = pl.BlockSpec(memory_space=pl.ANY)
    depth, columns = weight.shape
    half = pltpu.VMEM((depth // 2, columns), BF16)
    return pl.pallas_call(
        functools.partial(finish_body, kinds),
        in_specs=[hbm] * 5 + [pl.BlockSpec(memory_space=pltpu.VMEM)] + [hbm] * (2 + len(kinds)),
        out_specs=[hbm] * (4 + len(kinds)),
        out_shape=[
            jax.ShapeDtypeStruct(tokens.shape, BF16),
            jax.ShapeDtypeStruct(weight.shape, BF16),
            jax.ShapeDtypeStruct(taps.shape, F32),
            jax.ShapeDtypeStruct(gains.shape, F32),
            *[errand_target(*errand) for errand in errands],
        ],
        scratch_shapes=[
            pltpu.VMEM(left.shape, BF16),
            pltpu.VMEM(weight.shape, BF16),
            pltpu.VMEM(gathered.shape, BF16),
            pltpu.VMEM((depth // 2 // CHUNKS, gathered.shape[0]), BF16),
            half,
            half,
            half,
            half,
            pltpu.VMEM((rows, width), BF16),
            pltpu.VMEM((rows, width), F32),
            pltpu.VMEM((rows, width), BF16),
            pltpu.VMEM(taps.shape, F32),
            pltpu.VMEM((2, *taps.shape), F32),
            pltpu.VMEM(gains.shape, F32),
            pltpu.VMEM((5, *gains.shape), F32),
            *scatter_scratch(rows, width),
            pltpu.SemaphoreType.DMA((5, CHUNKS)),
            pltpu.SemaphoreType.DMA((5, CHUNKS)),
            pltpu.SemaphoreType.DMA((7,)),
            pltpu.SemaphoreType.DMA((7,)),
            pltpu.SemaphoreType.DMA((12 + CHUNKS,)),
            *errand_scratch(kinds, sources),
        ],
        compiler_params=pltpu.CompilerParams(
            collective_id=collective_id, has_side_effects=True, vmem_limit_bytes=60 * 2**20
        ),
        name="finish",
    )(left, weight, gathered, tokens, resid_grad, gain, taps, gains, *sources)


def rms_scale(values, gain):
    return values * lax.rsqrt(jnp.mean(values * values, -1, keepdims=True) + 1e-05) * gain


def swiglu(gate, up_vals):
    return jax.nn.silu(gate) * up_vals


def left_product(left, right):
    return dot(left, right, TN)


def token_scales(group_ids, mixture_counts):
    group_cols = lax.broadcasted_iota(jnp.int32, (1, GROUPS), 1)
    counts = mixture_counts.astype(F32)
    group_scale = jnp.sqrt(jnp.mean(counts) / counts)
    return jnp.sum(jnp.where(group_ids[:, None] == group_cols, group_scale[None, :], 0.0), 1)


def mixer_weights(w_query, w_key, w_value, w_gate_mix, w_beta):
    padded = jnp.pad(w_beta, ((0, 0), (0, 128 - w_beta.shape[1])))
    return jnp.concatenate([w_query, w_key, w_value, w_gate_mix, padded], 1)


ALL = ("y", "core", "zh", "zl", "x")
SIZES = (2, 2, 2, 2, 2)


CORE_PAIRS = [(i, i ^ 8) for i in range(32)]
EXCHANGE_PAIRS = [(i, i & 19 | (i & 8) >> 1 | (i & 4) << 1) for i in range(32)]


FORWARD_PLAN = (
    (0, 0, "start"), (0, 1, "start"), (0, 2, "start"), (0, 3, "start"),
    (3, 1, "middle"), (4, 0, "early"), (5, 2, "early"), (6, 0, "middle"), (7, 2, "late"),
    (7, 0, "late"), (7, 3, "early"), (7, 3, "late_after"),
    (7, 0, "finish"), (7, 1, "finish"), (7, 2, "finish"), (7, 3, "finish"),
)
BACKWARD_PLAN = (
    (0, 0, "start"), (0, 2, "start"), (0, 0, "launch"), (0, 1, "start"), (4, 1, "middle"),
    (6, 0, "settle"), (6, 2, "launch"), (7, 3, "start"),
    (7, 3, "middle_late"), (7, 0, "forward"), (7, 2, "settle_late"), (7, 2, "forward"),
    (7, 0, "finish"), (7, 1, "finish"), (7, 2, "finish"), (7, 3, "finish"),
)


def shards_ring(
    tokens, group_ids, mixture_counts, grad_out, norm1_gain, w_query, w_key, w_value, w_gate_mix,
    w_beta, conv_query, conv_key, conv_value, out_gain, w_out, norm2_gain, w_gate, w_up, w_down,
):
    heads = w_beta.shape[1]
    head_cols = w_query.shape[1]
    gain = out_gain.astype(F32)[None]
    gain1 = norm1_gain.astype(F32)[None]
    conv = jnp.concatenate([conv_query, conv_key, conv_value], 1).astype(F32)
    conv = jnp.pad(conv, ((0, 4), (0, 0)))
    grad_mlp = grad_out.astype(F32) * token_scales(group_ids, mixture_counts)[:, None]
    padded_beta = jnp.pad(w_beta, ((0, 0), (0, 128 - heads)))
    tokens, gathered, projected, mix_weights, conv, grad_mlp = begin(
        tokens, gain1, conv, [w_query, w_key, w_value, w_gate_mix, padded_beta], 1,
        [(Exchange, grad_mlp.astype(BF16))],
    )
    mixed, *kept, gathered_grad, w_out, w_gate, w_up = mixer_forward(
        projected, conv, gain, heads,
        [(Gather, grad_mlp), (Swap, w_out), (Swap, w_gate.T), (Swap, w_up.T)], FORWARD_PLAN, 2,
    )
    block = jax.ShapeDtypeStruct(tokens.shape, F32)
    block_low = jax.ShapeDtypeStruct(tokens.shape, BF16)
    gain2 = jnp.broadcast_to(norm2_gain.astype(F32), (8, norm2_gain.shape[0]))
    resid, normed_mlp, w_down = multiply_scatter(
        [mixed], [w_out], [tokens, gain2], [block, block_low], attn_tail, NN, 3, "scatter_attn",
        [(Swap, w_down)],
    )
    gathered_mlp, hidden, gate_grad, up_grad = feed(
        normed_mlp, w_gate, w_up, w_down, gathered_grad, 4
    )
    gathered_grad = gathered_grad.reshape(-1, gathered_grad.shape[2])
    output, gate_wgrad, down_part = mlp_scatter(
        hidden, w_down, gathered_grad, gate_grad, gathered_mlp, resid, 5
    )
    resid_grad, attn_grad, norm2_grad, up_wgrad, gate_part, down_half = multiply_scatter(
        [gate_grad, up_grad], [w_gate, w_up], [resid, grad_mlp, gain2],
        [block, block_low, jax.ShapeDtypeStruct(gain2.shape, F32)], grad_tail, NN, 6,
        "scatter_normed_mlp_grad", [(HalfSum, gate_wgrad), (AcrossTotal, down_part)],
        gathered_mlp,
    )
    mixed_grad, out_grad, up_part, gate_half, down_total = gather_multiply(
        attn_grad, w_out, mixed, NT, 7, "gather_attn_grad",
        [(HalfSum, up_wgrad), (AcrossTotal, gate_part), (Spread, down_half)],
    )
    raw_grad, conv_grad, gain_grad, up_total, gate_total, out_total, output = (
        mixer_backward(
            projected, conv, gain, mixed_grad, *kept, heads,
            [
                (Chain, up_part), (Spread, gate_half), (FullChain, out_grad), (Exchange, output),
            ],
            BACKWARD_PLAN, 8,
        )
    )
    width = tokens.shape[1]
    wide = width // 2
    gains = jnp.concatenate(
        [
            jnp.zeros((2, wide), F32), norm2_grad[0].reshape(2, wide),
            jnp.pad(gain_grad[:1], ((0, 3), (0, wide - gain_grad.shape[1]))),
        ],
        0,
    )
    grad_tokens, mix_total, taps, gains = finish(
        raw_grad, mix_weights, gathered, tokens, resid_grad, gain1, conv_grad, gains, 9
    )
    grad_tokens = lax.ppermute(grad_tokens, ALL, EXCHANGE_PAIRS)
    other_taps = lax.ppermute(taps, ALL, CORE_PAIRS)
    conv_total = jnp.where(lax.axis_index("core") == lax.axis_index("zh"), taps, other_taps)[:4]
    mix_total = mix_total.astype(F32)
    return (
        output,
        grad_tokens,
        gains[:2].reshape(width),
        mix_total[:, 0:head_cols],
        mix_total[:, head_cols : 2 * head_cols],
        mix_total[:, 2 * head_cols : 3 * head_cols],
        mix_total[:, 3 * head_cols : 4 * head_cols],
        mix_total[:, 4 * head_cols : 4 * head_cols + heads],
        conv_total[:, 0:head_cols],
        conv_total[:, head_cols : 2 * head_cols],
        conv_total[:, 2 * head_cols :],
        gains[4, :HEAD_DIM],
        out_total.astype(F32),
        gains[2:4].reshape(width),
        gate_total.astype(F32).T,
        up_total.astype(F32).T,
        down_total.astype(F32),
    )


def right_product(left, right):
    return dot(left, right, NT)


def make_fold(kept_rows, weight, piece):
    weight_grad = left_product(kept_rows, piece)
    rows_grad = right_product(piece, weight)
    return (weight_grad, rows_grad)


def make_rows(source, weight, transposed):
    if transposed:
        return right_product(source, weight)
    return jnp.dot(source, weight, preferred_element_type=F32)


def shards(
    tokens,
    group_ids,
    mixture_counts,
    grad_out,
    norm1_gain,
    w_query,
    w_key,
    w_value,
    w_gate_mix,
    w_beta,
    conv_query,
    conv_key,
    conv_value,
    out_gain,
    w_out,
    norm2_gain,
    w_gate,
    w_up,
    w_down,
):
    inputs = tokens.astype(F32)
    normed, norm1_back = jax.vjp(rms_scale, inputs, norm1_gain.astype(F32))
    gathered = lax.all_gather(normed.astype(BF16), "tp", axis=0, tiled=True)
    heads = w_beta.shape[1]
    mix_weights = mixer_weights(w_query, w_key, w_value, w_gate_mix, w_beta)
    projected = jnp.dot(gathered, mix_weights, preferred_element_type=F32)
    head_cols = w_query.shape[1]
    conv = jnp.concatenate([conv_query, conv_key, conv_value], 1).astype(F32)
    gain = out_gain.astype(F32)[None]
    mixed, *kept = mixer_forward(projected, conv, gain, heads)
    attn = lax.psum_scatter(
        make_rows(mixed, w_out, False).astype(jnp.bfloat16), "tp", scatter_dimension=0, tiled=True
    ).astype(jnp.float32)
    resid = inputs + attn
    normed_mlp, norm2_back = jax.vjp(rms_scale, resid, norm2_gain.astype(F32))
    gathered_mlp = lax.all_gather(normed_mlp.astype(BF16), "tp", axis=0, tiled=True)
    pair_weights = jnp.concatenate([w_gate, w_up], 1)
    ff_cols = w_gate.shape[1]
    paired = jnp.dot(gathered_mlp, pair_weights, preferred_element_type=F32)
    hidden_full, swiglu_back = jax.vjp(swiglu, paired[:, :ff_cols], paired[:, ff_cols:])
    hidden = hidden_full.astype(BF16)
    mlp_out = lax.psum_scatter(
        make_rows(hidden, w_down, False).astype(jnp.bfloat16), "tp", scatter_dimension=0, tiled=True
    ).astype(jnp.float32)
    output = (resid + mlp_out).astype(BF16)
    token_scale = token_scales(group_ids, mixture_counts)
    grad_rows = grad_out.astype(F32) * token_scale[:, None]
    grad_mlp = grad_rows.astype(BF16)
    grad_w_down, hidden_grad = make_fold(
        hidden, w_down, lax.all_gather(grad_mlp, "tp", axis=0, tiled=True)
    )
    gate_grad, up_grad = swiglu_back(hidden_grad)
    pair_grad = jnp.concatenate([gate_grad, up_grad], 1).astype(BF16)
    pair_weight_grad = left_product(gathered_mlp, pair_grad)
    normed_mlp_grad = lax.psum_scatter(
        make_rows(pair_grad, pair_weights, True).astype(jnp.bfloat16),
        "tp",
        scatter_dimension=0,
        tiled=True,
    ).astype(jnp.float32)
    resid_norm_grad, norm2_grad = norm2_back(normed_mlp_grad)
    resid_grad = grad_rows + resid_norm_grad
    attn_grad = resid_grad.astype(BF16)
    grad_w_out, mixed_grad = make_fold(
        mixed, w_out, lax.all_gather(attn_grad, "tp", axis=0, tiled=True)
    )
    raw_grad, conv_grad, gain_grad = mixer_backward(
        projected, conv, gain, mixed_grad, *kept, heads
    )
    mix_weight_grad = left_product(gathered, raw_grad)
    normed_grad = lax.psum_scatter(
        make_rows(raw_grad, mix_weights, True).astype(jnp.bfloat16),
        "tp",
        scatter_dimension=0,
        tiled=True,
    ).astype(jnp.float32)
    input_norm_grad, norm1_grad = norm1_back(normed_grad)
    grad_tokens = (resid_grad + input_norm_grad).astype(BF16)
    summed = (
        lax.psum(mix_weight_grad.astype(jnp.bfloat16), "dp").astype(jnp.float32),
        lax.psum(grad_w_out.astype(jnp.bfloat16), "dp").astype(jnp.float32),
        lax.psum(pair_weight_grad.astype(jnp.bfloat16), "dp").astype(jnp.float32),
        lax.psum(grad_w_down.astype(jnp.bfloat16), "dp").astype(jnp.float32),
    )
    conv_total = lax.psum(conv_grad[:4], "dp")
    gains = lax.psum((norm1_grad, gain_grad[0], norm2_grad), ("dp", "tp"))
    mix_total = summed[0]
    pair_total = summed[2]
    return (
        output,
        grad_tokens,
        gains[0],
        mix_total[:, 0:head_cols],
        mix_total[:, head_cols : 2 * head_cols],
        mix_total[:, 2 * head_cols : 3 * head_cols],
        mix_total[:, 3 * head_cols : 4 * head_cols],
        mix_total[:, 4 * head_cols : 4 * head_cols + heads],
        conv_total[:, 0:head_cols],
        conv_total[:, head_cols : 2 * head_cols],
        conv_total[:, 2 * head_cols :],
        gains[1],
        summed[1],
        gains[2],
        pair_total[:, :ff_cols],
        pair_total[:, ff_cols:],
        summed[3],
    )


def solution(mesh):
    rows, cols, all_rows = "tp", "tp", ("dp", "tp")
    body = shards
    if dict(mesh.shape) == {"dp": 4, "tp": 8}:
        mesh = Mesh(mesh.devices.reshape(SIZES), ALL)
        rows = cols = ("zh", "zl", "x")
        all_rows = ALL
        body = shards_ring
    by_row, by_col, by_token = P(rows, None), P(None, cols), P(all_rows, None)
    return jax.shard_map(
        body,
        mesh=mesh,
        in_specs=(
            by_token, P(all_rows), P(), by_token, P(), by_col, by_col, by_col, by_col, by_col,
            by_col, by_col, by_col, P(), by_row, P(), by_col, by_col, by_row,
        ),
        out_specs=(
            by_token, by_token, P(), by_col, by_col, by_col, by_col, by_col, by_col, by_col,
            by_col, P(), by_row, P(), by_col, by_col, by_row,
        ),
        check_vma=False,
    )
```
